256 devices in a mesh: dp: 16 (over y, x), mp: 16 (over z, core).
Axes of the slice: x: 4, y: 4, z: 8, core: 2. Of those that a mesh axis runs over, the one named last changes fastest.
Arguments:
- features: bfloat16 [2, 1536, 8192], P(None, 'dp'), as said below
- weight: bfloat16 [8192, 8192], P(None, 'mp'), may hold values from -0.0625 to 0.0625
Outputs:
- grad_weight: float32 [8192, 8192], P('dp', 'mp')
- loss_value: float32 [], replicated
The draws below stay inside these ranges and needn't reach their ends.
Inputs may be any that keep to these rules, and one draw needn't show every extreme that they name: Nonnegative post-activation features.
All inputs are finite; a program needn't handle non-finite values.
Results may differ from the reference program's by a relative error of at most 0.0016.
Values may be sent and summed in bfloat16 or wider, within the bound.
A program may use at most 128 MiB of HBM per device.

```python
import jax
import jax.numpy as jnp
from jax import lax

D = 8192
BATCH = 1536


def draw_features(key, part):
    key = jax.random.fold_in(key, 11)
    keys = jax.random.split(key, 4)
    shared = jax.random.normal(keys[0], (1, BATCH, D), jnp.float32)
    noise = jax.random.normal(keys[1], (2, BATCH, D), jnp.float32)
    common = jax.random.normal(keys[2], (1, BATCH, 1), jnp.float32)
    loading = jax.random.uniform(keys[3], (1, 1, D), jnp.float32, -1.0, 1.0)
    mixed = 0.8 * shared + 0.6 * noise + common * loading
    return jnp.maximum(mixed, 0.0).astype(jnp.bfloat16)


def block_levels(rng, shape, shards, least, high):
    def one(position, parts):
        draws = jax.random.uniform(jax.random.fold_in(jax.random.fold_in(rng, 6), position), (parts,), jnp.float32, least / len(shards), high / len(shards))
        return jnp.repeat(jnp.exp(draws), shape[position] // parts).reshape((-1,) + (1,) * (len(shape) - position - 1))

    level = one(*shards[0])
    for cut in shards[1:]:
        level = level * one(*cut)
    return level


def scatter_about(stream_key, extent, scale, most, pieces=(), kind=jnp.bfloat16):
    entries = scale * jax.random.normal(stream_key, extent, jnp.float32)
    if pieces:
        entries = entries * block_levels(stream_key, extent, pieces, -0.22, 0.18)
    return jnp.clip(entries, -most, most).astype(kind)


def setup_inputs(seed: int = 0) -> dict:
    arg_keys = jax.random.split(jax.random.key(seed), 3)
    return {
        "features": draw_features(jax.random.fold_in(arg_keys[2], 71), 0),
        "weight": scatter_about(arg_keys[1], (D, D), D ** -0.5, 0.0625, ((1, 16),)),
    }


epsilon = 1e-05
off_weight = 0.0051

def normalize_view(projected):
    moment_mean = lax.optimization_barrier(jnp.mean(projected, axis=0))
    shifted = projected - moment_mean
    variance = lax.optimization_barrier(jnp.mean(shifted * shifted, axis=0))
    inv_std = lax.rsqrt(variance + epsilon)
    return (shifted * inv_std, inv_std)

def batch_back(normed_grad, centered, inv_std):
    first_mean = lax.optimization_barrier(jnp.mean(normed_grad, axis=0))
    second_mean = lax.optimization_barrier(jnp.mean(normed_grad * centered, axis=0))
    return (inv_std * (normed_grad - first_mean - centered * second_mean)).astype(jnp.bfloat16)

def reference(features, weight):
    proj_first = jnp.dot(features[0], weight, preferred_element_type=jnp.float32)
    proj_second = jnp.dot(features[1], weight, preferred_element_type=jnp.float32)
    cent_first, std_first = normalize_view(proj_first)
    cent_second, std_second = normalize_view(proj_second)
    norm_first = cent_first.astype(jnp.bfloat16)
    norm_second = cent_second.astype(jnp.bfloat16)
    correlation = lax.dot_general(norm_first, norm_second, (((0,), (0,)), ((), ())), preferred_element_type=jnp.float32) / BATCH
    index_line = jnp.arange(D, dtype=jnp.int32)
    on_diagonal = index_line[:, None] == index_line[None, :]
    terms = jnp.where(on_diagonal, (1.0 - correlation) ** 2, off_weight * correlation * correlation)
    loss_value = jnp.sum(terms) / D
    corr_grad = jnp.where(on_diagonal, 2.0 * (correlation - 1.0), 2.0 * off_weight * correlation).astype(jnp.bfloat16)
    grad_first = lax.dot_general(norm_second, corr_grad, (((1,), (1,)), ((), ())), preferred_element_type=jnp.float32) / BATCH
    grad_second = jnp.dot(norm_first, corr_grad, preferred_element_type=jnp.float32) / BATCH
    out_first = batch_back(grad_first, cent_first, std_first)
    out_second = batch_back(grad_second, cent_second, std_second)
    grad_weight = lax.dot_general(features[0], out_first, (((0,), (0,)), ((), ())), preferred_element_type=jnp.float32)
    grad_weight = grad_weight + lax.dot_general(features[1], out_second, (((0,), (0,)), ((), ())), preferred_element_type=jnp.float32)
    return (grad_weight, loss_value)
```

```python
import jax
import jax.numpy as jnp
from jax import lax
from jax.sharding import PartitionSpec as P

epsilon = 1e-05
off_weight = 0.0051


def body(features, weight):
    n_dp = lax.axis_size("dp")
    n_mp = lax.axis_size("mp")
    rows = features.shape[1]
    full_width = features.shape[2]
    cols = weight.shape[1]
    batch = rows * n_dp
    swap = [(a * n_mp + b, b * n_mp + a) for a in range(n_dp) for b in range(n_mp)]

    features_cols = lax.all_to_all(features, "dp", split_axis=2, concat_axis=1, tiled=True)
    projected = jnp.einsum("vrk,kc->vrc", features, weight, preferred_element_type=jnp.float32)
    local_mean = jnp.mean(projected, axis=1)
    local_dev = projected - local_mean[:, None, :]
    local_m2 = jnp.sum(local_dev * local_dev, axis=1)
    stats = lax.all_gather(jnp.stack([local_mean, local_m2]), "dp", axis=0)
    mean = jnp.mean(stats[:, 0], axis=0)
    gap = stats[:, 0] - mean[None]
    variance = (jnp.sum(stats[:, 1], axis=0) + rows * jnp.sum(gap * gap, axis=0)) / batch
    inv_std = lax.rsqrt(variance + epsilon)
    centered = (projected - mean[:, None, :]) * inv_std[:, None, :]
    normed = centered.astype(jnp.bfloat16)
    second_cols = lax.all_gather(normed[1], "dp", axis=0, tiled=True)
    first_block = lax.all_gather(
        lax.ppermute(normed[0], ("dp", "mp"), swap), "mp", axis=0, tiled=True
    )
    correlation = (
        lax.dot_general(
            first_block, second_cols, (((0,), (0,)), ((), ())), preferred_element_type=jnp.float32
        )
        / batch
    )
    row_ids = lax.axis_index("dp") * cols + lax.broadcasted_iota(jnp.int32, (cols, cols), 0)
    col_ids = lax.axis_index("mp") * cols + lax.broadcasted_iota(jnp.int32, (cols, cols), 1)
    on_diagonal = row_ids == col_ids
    terms = jnp.where(on_diagonal, (1.0 - correlation) ** 2, off_weight * correlation * correlation)
    loss_value = lax.psum(jnp.sum(terms), ("dp", "mp")) / full_width
    corr_grad = jnp.where(
        on_diagonal, 2.0 * (correlation - 1.0), 2.0 * off_weight * correlation
    ).astype(jnp.bfloat16)
    wide_grad = corr_grad.astype(jnp.float32)
    first_sum = jnp.sum(first_block.astype(jnp.float32), axis=0)
    second_sum = jnp.sum(second_cols.astype(jnp.float32), axis=0)
    across_second = lax.psum(
        jnp.stack(
            [jnp.sum(wide_grad * first_sum[:, None], axis=0) / batch, jnp.sum(wide_grad * correlation, axis=0)]
        ),
        "dp",
    )
    across_first = lax.psum(
        jnp.stack(
            [jnp.sum(wide_grad * second_sum[None, :], axis=1) / batch, jnp.sum(wide_grad * correlation, axis=1)]
        ),
        "mp",
    )
    part_second = jnp.dot(first_block, corr_grad, preferred_element_type=jnp.float32)
    part_first = lax.dot_general(
        second_cols, corr_grad, (((1,), (1,)), ((), ())), preferred_element_type=jnp.float32
    )
    grad_second = lax.psum_scatter(part_second, "dp", scatter_dimension=0, tiled=True) / batch
    grad_first = lax.psum_scatter(part_first, "mp", scatter_dimension=0, tiled=True) / batch
    grad_first, across_first = lax.ppermute((grad_first, across_first), ("dp", "mp"), swap)
    normed_grad = jnp.stack([grad_first, grad_second])
    across = jnp.stack([across_first, across_second])
    out_grad = (
        inv_std[:, None, :]
        * (
            normed_grad
            - across[:, 0][:, None, :] / batch
            - centered * (across[:, 1][:, None, :] / batch)
        )
    ).astype(jnp.bfloat16)
    out_cols = lax.all_gather(out_grad, "dp", axis=1, tiled=True)
    grad_weight = jnp.einsum("vrk,vrc->kc", features_cols, out_cols, preferred_element_type=jnp.float32)
    return (grad_weight, loss_value)


def solution(mesh):
    placed = (P(None, "dp", None), P(None, "mp"))
    return jax.shard_map(
        body, mesh=mesh, in_specs=placed, out_specs=(P("dp", "mp"), P()), check_vma=False
    )
```

```python
import functools

import jax
import jax.numpy as jnp
from jax import lax
from jax.experimental import pallas as pl
from jax.experimental.pallas import tpu as pltpu
from jax.sharding import PartitionSpec as P

epsilon = 1e-05
off_weight = 0.0051
SIDE = 4
CORES = 2
STAT = 8
MSGS = 160
MESH = pl.DeviceIdType.MESH


class Mail:
    def __init__(self, send_sem, recv_sem):
        self.send_sem, self.recv_sem, self.sent = send_sem, recv_sem, []

    def push(self, src, dst, device):
        index = len(self.sent)
        copy = pltpu.make_async_remote_copy(
            src_ref=src,
            dst_ref=dst,
            send_sem=self.send_sem.at[index],
            recv_sem=self.recv_sem.at[index],
            device_id=device,
            device_id_type=MESH,
        )
        copy.start()
        self.sent.append(copy)
        return copy

    def close(self):
        for copy in self.sent:
            copy.wait_send()


def kernel(
    n_dp,
    n_mp,
    features,
    weight,
    grad,
    loss,
    w_buf,
    f_buf,
    cent,
    stat_x,
    stat_y,
    inv_buf,
    turn_out,
    t0,
    t1,
    corr_buf,
    g_buf,
    p0,
    p1_buf,
    opp_l,
    opp_r,
    fin_l,
    fin_r,
    opp2_l,
    opp2_r,
    fin2_l,
    fin2_r,
    sib,
    up_a,
    up_b,
    down_a,
    down_b,
    turn_back,
    og,
    fk,
    loss_x,
    loss_y,
    loss_z,
    loss_c,
    send_sem,
    recv_sem,
    load_sem,
    turn_sem,
):
    rows = cent.shape[1]
    cols = cent.shape[2]
    depth = features.shape[2]
    batch = rows * n_dp
    ring = n_mp // CORES
    piece = rows + STAT
    top = piece // 2 // 8 * 8 + (8 if piece // 2 % 8 else 0)

    i = lax.axis_index("dp")
    j = lax.axis_index("mp")
    y, x = i // SIDE, i % SIDE
    z, c = j // CORES, j % CORES
    q1 = x * (1 - c) + y * c
    q2 = y * (1 - c) + x * c
    s1 = 1 * (1 - c) + SIDE * c
    s2 = SIDE * (1 - c) + 1 * c

    def ring1(q):
        return (q * s1 + q2 * s2, j)

    def ring2(q):
        return (q1 * s1 + q * s2, j)

    def zdev(q):
        return (i, q * CORES + c)

    def slot_of(a, core):
        ay, ax = a // SIDE, a % SIDE
        return (ax * SIDE + ay) * (1 - core) + a * core

    right1, left1, far1 = (q1 + 1) % SIDE, (q1 + SIDE - 1) % SIDE, (q1 + 2) % SIDE
    right2, left2, far2 = (q2 + 1) % SIDE, (q2 + SIDE - 1) % SIDE, (q2 + 2) % SIDE
    up, down = (z + 1) % ring, (z + ring - 1) % ring
    sibling = (i, z * CORES + 1 - c)
    mail = Mail(send_sem, recv_sem)

    barrier = pltpu.get_barrier_semaphore()
    for d in range(1, n_dp):
        pl.semaphore_signal(barrier, inc=1, device_id=((i + d) % n_dp, j), device_id_type=MESH)
    for d in range(1, ring):
        pl.semaphore_signal(barrier, inc=1, device_id=zdev((z + d) % ring), device_id_type=MESH)
    pl.semaphore_signal(barrier, inc=1, device_id=sibling, device_id_type=MESH)

    @pl.when(i != j)
    def _():
        pl.semaphore_signal(barrier, inc=1, device_id=(j, i), device_id_type=MESH)

    parts = 8
    step = depth // parts

    def loads(k):
        cut = pl.ds(pl.multiple_of(k * step, step), step)
        return (
            pltpu.make_async_copy(weight.at[cut, :], w_buf.at[cut, :], load_sem.at[k]),
            pltpu.make_async_copy(
                features.at[:, :, cut], f_buf.at[:, :, cut], load_sem.at[parts + k]
            ),
        )

    for k in range(parts):
        for load in loads(k):
            load.start()
    own_k = pltpu.make_async_copy(
        features.at[c, :, pl.ds(pl.multiple_of(i * cols, cols), cols)],
        fk.at[c, i],
        load_sem.at[2 * parts],
    )
    own_k.start()

    greeted = n_dp - 1 + ring - 1 + 1

    @pl.when(i != j)
    def _():
        pl.semaphore_wait(barrier, greeted + 1)

    @pl.when(i == j)
    def _():
        pl.semaphore_wait(barrier, greeted)

    cent[...] = jnp.zeros_like(cent)

    def project(k, carry):
        for load in loads(k):
            load.wait()
        cut = pl.ds(pl.multiple_of(k * step, step), step)
        left = f_buf[:, :, cut].reshape(2 * rows, step)
        got = jnp.dot(left, w_buf[cut, :], preferred_element_type=jnp.float32)
        cent[...] += got.reshape(2, rows, cols)
        return carry

    lax.fori_loop(0, parts, project, 0)

    projected = cent[...]
    mean = jnp.sum(projected, axis=1) / rows
    shifted = projected - mean[:, None, :]
    spread = jnp.sum(shifted * shifted, axis=1)
    pad = jnp.zeros((STAT - 4, cols), jnp.float32)
    for buf, at, stride, count in (
        (stat_x, x, 1, rows),
        (stat_y, y, SIDE, rows * SIDE),
    ):
        buf[at] = jnp.concatenate([mean, spread, pad], axis=0)
        copies = []
        for d in range(1, SIDE):
            other = (at + d) % SIDE
            copies.append(mail.push(buf.at[at], buf.at[at], (i + (other - at) * stride, j)))
        for copy in copies:
            copy.wait_recv()
        got = buf[...]
        mean = (got[0, 0:2] + got[1, 0:2] + got[2, 0:2] + got[3, 0:2]) / SIDE
        spread = got[0, 2:4] + got[1, 2:4] + got[2, 2:4] + got[3, 2:4]
        for s in range(SIDE):
            gap = got[s, 0:2] - mean
            spread = spread + count * (gap * gap)
    inv_std = lax.rsqrt(spread / batch + epsilon)
    inv_buf[0:2] = inv_std
    centered = (projected - mean[:, None, :]) * inv_std[:, None, :]
    cent[...] = centered
    normed = centered.astype(jnp.bfloat16)
    own = q1 * SIDE + q2
    turn_out[...] = normed[0]
    t1[own] = normed[1]

    turn_slot = slot_of(j, c)
    partner_slot = slot_of(i, i % CORES)
    go = pltpu.make_async_remote_copy(
        src_ref=turn_out,
        dst_ref=t0.at[partner_slot],
        send_sem=turn_sem.at[0],
        recv_sem=turn_sem.at[1],
        device_id=(j, i),
        device_id_type=MESH,
    )
    stay = pltpu.make_async_copy(turn_out, t0.at[turn_slot], turn_sem.at[2])

    @pl.when(i != j)
    def _():
        go.start()

    @pl.when(i == j)
    def _():
        stay.start()

    half = rows // 2

    def spread2(slot):
        return (
            mail.push(t1.at[slot], t1.at[slot], ring2(right2)),
            mail.push(t1.at[slot], t1.at[slot], ring2(left2)),
        )

    a1 = mail.push(t1.at[own], t1.at[own], ring1(right1))
    b1 = mail.push(t1.at[own], t1.at[own], ring1(left1))
    second = [spread2(own)]

    @pl.when(i != j)
    def _():
        go.wait_recv()

    @pl.when(i == j)
    def _():
        stay.wait()

    z_up = [mail.push(t0.at[turn_slot], t0.at[turn_slot], zdev(up))]
    z_down = [mail.push(t0.at[turn_slot], t0.at[turn_slot], zdev(down))]
    side_copies = []

    def to_side(q):
        a = q * CORES + c
        side_copies.append(
            mail.push(t0.at[slot_of(a, c)], t0.at[slot_of(a, 1 - c)], sibling)
        )

    to_side(z)

    a1.wait_recv()
    from_left = left1 * SIDE + q2
    c1 = mail.push(
        t1.at[from_left, pl.ds(0, half)], t1.at[from_left, pl.ds(0, half)], ring1(right1)
    )
    second.append(spread2(from_left))
    b1.wait_recv()
    from_right = right1 * SIDE + q2
    d1 = mail.push(
        t1.at[from_right, pl.ds(half, half)], t1.at[from_right, pl.ds(half, half)], ring1(left1)
    )
    second.append(spread2(from_right))

    far = ring // 2
    for t in range(1, far):
        low, high = (z + ring - t) % ring, (z + t) % ring
        low_slot, high_slot = slot_of(low * CORES + c, c), slot_of(high * CORES + c, c)
        z_up[-1].wait_recv()
        if t < far - 1:
            z_up.append(mail.push(t0.at[low_slot], t0.at[low_slot], zdev(up)))
        else:
            part = t0.at[low_slot, pl.ds(0, half)]
            z_up.append(mail.push(part, part, zdev(up)))
        z_down[-1].wait_recv()
        if t < far - 1:
            z_down.append(mail.push(t0.at[high_slot], t0.at[high_slot], zdev(down)))
        else:
            part = t0.at[high_slot, pl.ds(half, half)]
            z_down.append(mail.push(part, part, zdev(down)))
        to_side(low)
        to_side(high)
        if t == 1:
            c1.wait_recv()
            d1.wait_recv()
            second.append(spread2(far1 * SIDE + q2))

    forwards = []
    for n, (q, pair) in enumerate(zip((q1, left1, right1, far1), second)):
        to_right, to_left = pair
        to_right.wait_recv()
        if n in (0, 3):
            part = t1.at[q * SIDE + left2]
            forwards.append(mail.push(part, part, ring2(right2)))
        to_left.wait_recv()
        if n in (1, 2):
            part = t1.at[q * SIDE + right2]
            forwards.append(mail.push(part, part, ring2(left2)))

    own_k.wait()
    feature_copies = []
    for d in range(1, n_dp):
        other = (i + d) % n_dp
        feature_copies.append(
            mail.push(
                features.at[c, :, pl.ds(pl.multiple_of(other * cols, cols), cols)],
                fk.at[c, i],
                (other, j),
            )
        )

    z_up[-1].wait_recv()
    z_down[-1].wait_recv()
    to_side((z + far) % ring)
    for copy in forwards:
        copy.wait_recv()
    for copy in side_copies:
        copy.wait_recv()

    tile = 128
    tiles = cols // tile
    col_ids = j * cols + lax.broadcasted_iota(jnp.int32, (tile, cols), 1)

    def correlate(t, carry):
        total, cross_cols = carry
        cut = pl.ds(pl.multiple_of(t * tile, tile), tile)
        left = t0[:, :, cut].reshape(batch, tile)
        corr = lax.dot_general(
            left, t1[...].reshape(batch, cols), (((0,), (0,)), ((), ())),
            preferred_element_type=jnp.float32,
        ) * (1.0 / batch)
        row_ids = i * cols + t * tile + lax.broadcasted_iota(jnp.int32, (tile, cols), 0)
        on_diagonal = row_ids == col_ids
        gap = corr - 1.0
        terms = jnp.where(on_diagonal, gap * gap, off_weight * corr * corr)
        g = jnp.where(on_diagonal, 2.0 * gap, 2.0 * off_weight * corr).astype(jnp.bfloat16)
        g_buf[pl.ds(pl.multiple_of(t * tile, tile), tile), :] = g
        both = g.astype(jnp.float32) * corr
        corr_buf[pl.ds(pl.multiple_of(t * tile, tile), tile), :] = jnp.broadcast_to(
            jnp.sum(both, axis=1, keepdims=True), (tile, tile)
        )
        return (
            total + jnp.sum(terms, axis=0, keepdims=True),
            cross_cols + jnp.sum(both, axis=0, keepdims=True),
        )

    nothing = jnp.zeros((1, cols), jnp.float32)
    total, cross_cols = lax.fori_loop(0, tiles, correlate, (nothing, nothing))
    cross_rows = corr_buf[...].T[0:1, :]
    g_all = g_buf[...]

    def three(v):
        high = v.astype(jnp.bfloat16)
        rest = v - high.astype(jnp.float32)
        mid = rest.astype(jnp.bfloat16)
        low = (rest - mid.astype(jnp.float32)).astype(jnp.bfloat16)
        return jnp.concatenate([high, mid, low, jnp.zeros((13, cols), jnp.bfloat16)], axis=0)

    def add_rows(n, carry):
        first, other = carry
        return (
            first + jnp.sum(t0[n].astype(jnp.float32), axis=0, keepdims=True),
            other + jnp.sum(t1[n].astype(jnp.float32), axis=0, keepdims=True),
        )

    sum0, sum1 = lax.fori_loop(0, n_dp, add_rows, (nothing, nothing))
    down_g = jnp.dot(three(sum0), g_all, preferred_element_type=jnp.float32)
    across_g = lax.dot_general(
        three(sum1), g_all, (((1,), (1,)), ((), ())), preferred_element_type=jnp.float32
    )
    scale = 1.0 / batch
    blank = jnp.zeros((STAT - 2, cols), jnp.float32)
    stats1 = jnp.concatenate(
        [jnp.sum(down_g[0:3], axis=0, keepdims=True) * (scale * scale), cross_cols * scale, blank], axis=0
    )
    stats0 = jnp.concatenate(
        [jnp.sum(across_g[0:3], axis=0, keepdims=True) * (scale * scale), cross_rows * scale, blank], axis=0
    )

    def part1(q):
        cut = pl.ds(q * SIDE, SIDE)
        got = jnp.dot(
            t0[cut].reshape(SIDE * rows, cols), g_buf[...], preferred_element_type=jnp.float32
        )
        p1_buf[cut, 0:rows, :] = (got * scale).reshape(SIDE, rows, cols)
        p1_buf[cut, rows:piece, :] = jnp.broadcast_to(stats1[None], (SIDE, STAT, cols))

    def part0(q, carry):
        cut = pl.ds(q * SIDE, SIDE)
        got = lax.dot_general(
            t1[cut].reshape(SIDE * rows, cols), g_buf[...], (((1,), (1,)), ((), ())),
            preferred_element_type=jnp.float32,
        )
        p0[cut, 0:rows, :] = (got * scale).reshape(SIDE, rows, cols)
        p0[cut, rows:piece, :] = jnp.broadcast_to(stats0[None], (SIDE, STAT, cols))
        return carry

    part1(far1)
    far_r = [mail.push(p1_buf.at[far1 * SIDE + n], opp_l.at[n], ring1(right1)) for n in (0, 1)]
    far_l = [
        mail.push(p1_buf.at[far1 * SIDE + 2 + n], opp_r.at[n], ring1(left1)) for n in (0, 1)
    ]
    lax.fori_loop(0, SIDE, part0, 0)
    order = [(z + far) % ring]
    for t in range(far - 1, 0, -1):
        order += [(z + t) % ring, (z + ring - t) % ring]
    order.append(z)
    side = [
        mail.push(
            p0.at[slot_of(q * CORES + 1 - c, c)], sib.at[q], sibling
        )
        for q in order
    ]
    part1(right1)
    near_r = [None, None] + [
        mail.push(p1_buf.at[right1 * SIDE + n], fin_l.at[n], ring1(right1)) for n in (2, 3)
    ]
    part1(left1)
    near_l = [
        mail.push(p1_buf.at[left1 * SIDE + n], fin_r.at[n], ring1(left1)) for n in (0, 1)
    ] + [None, None]
    part1(q1)

    def loss_send(buf, at, others, value):
        buf[at] = value
        return [mail.push(buf.at[at], buf.at[at], device) for device in others]

    def loss_sum(buf, copies):
        for copy in copies:
            copy.wait_recv()
        value = buf[0]
        for n in range(1, buf.shape[0]):
            value = value + buf[n]
        return value

    mine = jnp.broadcast_to(jnp.sum(total, axis=1, keepdims=True), (8, 128))
    loss_copies = loss_send(
        loss_x, x, [(y * SIDE + (x + d) % SIDE, j) for d in range(1, SIDE)], mine
    )

    halves = (pl.ds(0, top), pl.ds(top, piece - top))

    def settle(n):
        side[n].wait_recv()
        q = order[n]
        at = slot_of(q * CORES + c, c)
        p0[at] = p0[at] + sib[q]

    settle(0)
    settle(1)
    settle(2)

    def row(q, h):
        return p0.at[slot_of(q * CORES + c, c), halves[h]]

    dest_up = lambda t: (z + t) % ring
    dest_down = lambda t: (z + ring - t) % ring
    chain_ua = [mail.push(row(dest_up(far), 0), up_a.at[0], zdev(up))]
    chain_db = [mail.push(row(dest_down(far), 1), down_b.at[0], zdev(down))]
    chain_ub = [mail.push(row(dest_up(far - 1), 1), up_b.at[0], zdev(up))]
    chain_da = [mail.push(row(dest_down(far - 1), 0), down_a.at[0], zdev(down))]
    for n in range(3, ring):
        settle(n)

    for n in (0, 1):
        far_r[n].wait_recv()
        at = right1 * SIDE + n
        p1_buf[at] = p1_buf[at] + opp_l[n]
        near_r[n] = mail.push(p1_buf.at[at], fin_l.at[n], ring1(right1))
        far_l[n].wait_recv()
        at = left1 * SIDE + 2 + n
        p1_buf[at] = p1_buf[at] + opp_r[n]
        near_l[2 + n] = mail.push(p1_buf.at[at], fin_r.at[2 + n], ring1(left1))

    def pass_on(chain, buf, h, dest, device):
        n = len(chain) - 1
        chain[n].wait_recv()
        at = slot_of(dest * CORES + c, c)
        p0[at, halves[h]] = p0[at, halves[h]] + buf[n]
        chain.append(mail.push(p0.at[at, halves[h]], buf.at[n + 1], device))

    total = loss_sum(loss_x, loss_copies)
    loss_copies = loss_send(
        loss_y, y, [(((y + d) % SIDE) * SIDE + x, j) for d in range(1, SIDE)], total
    )

    for t in range(far - 1, 0, -1):
        pass_on(chain_ua, up_a, 0, dest_up(t), zdev(up))
        pass_on(chain_db, down_b, 1, dest_down(t), zdev(down))
        if t > 1:
            pass_on(chain_ub, up_b, 1, dest_up(t - 1), zdev(up))
            pass_on(chain_da, down_a, 0, dest_down(t - 1), zdev(down))

    total = loss_sum(loss_y, loss_copies)
    loss_copies = loss_send(loss_z, z, [zdev((z + d) % ring) for d in range(1, ring)], total)

    for n in range(SIDE):
        near_r[n].wait_recv()
        near_l[n].wait_recv()
        at = q1 * SIDE + n
        p1_buf[at] = p1_buf[at] + fin_l[n] + fin_r[n]
    base = q1 * SIDE
    far2_r = mail.push(p1_buf.at[base + far2, halves[0]], opp2_l, ring2(right2))
    far2_l = mail.push(p1_buf.at[base + far2, halves[1]], opp2_r, ring2(left2))
    n2r = mail.push(
        p1_buf.at[base + right2, halves[1]], fin2_l.at[halves[1]], ring2(right2)
    )
    n2l = mail.push(p1_buf.at[base + left2, halves[0]], fin2_r.at[halves[0]], ring2(left2))
    far2_r.wait_recv()
    p1_buf[base + right2, halves[0]] = p1_buf[base + right2, halves[0]] + opp2_l[...]
    n2r2 = mail.push(
        p1_buf.at[base + right2, halves[0]], fin2_l.at[halves[0]], ring2(right2)
    )
    far2_l.wait_recv()
    p1_buf[base + left2, halves[1]] = p1_buf[base + left2, halves[1]] + opp2_r[...]
    n2l2 = mail.push(p1_buf.at[base + left2, halves[1]], fin2_r.at[halves[1]], ring2(left2))

    for chain in (chain_ua, chain_db, chain_ub, chain_da):
        chain[-1].wait_recv()
    mine_at = slot_of(j, c)
    p0[mine_at, halves[0]] = p0[mine_at, halves[0]] + up_a[far - 1] + down_a[far - 2]
    p0[mine_at, halves[1]] = p0[mine_at, halves[1]] + up_b[far - 2] + down_b[far - 1]
    back = pltpu.make_async_remote_copy(
        src_ref=p0.at[mine_at],
        dst_ref=turn_back,
        send_sem=turn_sem.at[3],
        recv_sem=turn_sem.at[4],
        device_id=(j, i),
        device_id_type=MESH,
    )
    back_stay = pltpu.make_async_copy(p0.at[mine_at], turn_back, turn_sem.at[5])

    @pl.when(i != j)
    def _():
        back.start()

    @pl.when(i == j)
    def _():
        back_stay.start()

    n2r.wait_recv()
    n2l.wait_recv()
    n2r2.wait_recv()
    n2l2.wait_recv()

    def finish(view, total):
        inv = inv_buf[view : view + 1]
        got = inv * (
            total[0:rows] - total[rows : rows + 1] - cent[view] * total[rows + 1 : rows + 2]
        )
        og[view, i] = got.astype(jnp.bfloat16)

    finish(1, p1_buf[base + q2] + fin2_l[...] + fin2_r[...])

    def index_of(a, b):
        return a * s1 + b * s2

    def gather_first(view):
        part = og.at[view, i]
        first = (mail.push(part, part, ring1(right1)), mail.push(part, part, ring1(left1)))
        return first

    def gather_second(view, a):
        part = og.at[view, index_of(a, q2)]
        return (mail.push(part, part, ring2(right2)), mail.push(part, part, ring2(left2)))

    def gather_mid(view, first):
        first[0].wait_recv()
        if view == 0:
            part = og.at[view, index_of(left1, q2)]
            last = mail.push(part, part, ring1(right1))
        sends = [gather_second(view, left1)]
        first[1].wait_recv()
        if view == 1:
            part = og.at[view, index_of(right1, q2)]
            last = mail.push(part, part, ring1(left1))
        sends.append(gather_second(view, right1))
        return last, sends

    def gather_pass(view, n, a, pair):
        pair[0].wait_recv()
        pair[1].wait_recv()
        if n % 2 == view:
            part = og.at[view, index_of(a, left2)]
            return mail.push(part, part, ring2(right2))
        part = og.at[view, index_of(a, right2)]
        return mail.push(part, part, ring2(left2))

    first1 = gather_first(1)
    own1 = gather_second(1, q1)
    last1, mid1 = gather_mid(1, first1)

    @pl.when(i != j)
    def _():
        back.wait_recv()

    @pl.when(i == j)
    def _():
        back_stay.wait()

    finish(0, turn_back[...])
    first0 = gather_first(0)
    own0 = gather_second(0, q1)

    total = loss_sum(loss_z, loss_copies)
    loss_copies = loss_send(loss_c, c, [sibling], total)

    last = []
    last.append(gather_pass(1, 0, q1, own1))
    last1.wait_recv()
    end1 = gather_second(1, far1)
    last0, mid0 = gather_mid(0, first0)
    last.append(gather_pass(1, 1, left1, mid1[0]))
    last.append(gather_pass(1, 2, right1, mid1[1]))
    last.append(gather_pass(0, 0, q1, own0))
    last0.wait_recv()
    end0 = gather_second(0, far1)

    for copy in feature_copies:
        copy.wait_recv()
    to_twin = mail.push(fk.at[c], fk.at[c], sibling)

    last.append(gather_pass(1, 3, far1, end1))
    last.append(gather_pass(0, 1, left1, mid0[0]))
    last.append(gather_pass(0, 2, right1, mid0[1]))
    last.append(gather_pass(0, 3, far1, end0))
    loss[...] = loss_sum(loss_c, loss_copies) / (n_mp * cols)
    for copy in last:
        copy.wait_recv()
    to_twin.wait_recv()

    def weigh(t, carry):
        cut = pl.ds(pl.multiple_of(t * tile, tile), tile)
        left = fk[:, :, :, cut].reshape(2 * batch, tile)
        grad[pl.ds(pl.multiple_of(t * tile, tile), tile), :] = lax.dot_general(
            left, og[...].reshape(2 * batch, cols), (((0,), (0,)), ((), ())),
            preferred_element_type=jnp.float32,
        )
        return carry

    lax.fori_loop(0, tiles, weigh, 0)

    @pl.when(i != j)
    def _():
        go.wait_send()
        back.wait_send()

    mail.close()


def body(n_dp, n_mp, features, weight):
    rows, depth = features.shape[1], features.shape[2]
    cols = weight.shape[1]
    ring = n_mp // CORES
    far = ring // 2
    piece = rows + STAT
    top = piece // 2 // 8 * 8 + (8 if piece // 2 % 8 else 0)
    f32, bf16 = jnp.float32, jnp.bfloat16
    V = pltpu.VMEM
    scratch = [
        V((depth, cols), bf16),
        V((2, rows, depth), bf16),
        V((2, rows, cols), f32),
        V((SIDE, STAT, cols), f32),
        V((SIDE, STAT, cols), f32),
        V((STAT, cols), f32),
        V((rows, cols), bf16),
        V((n_dp, rows, cols), bf16),
        V((n_dp, rows, cols), bf16),
        V((cols, 128), f32),
        V((cols, cols), bf16),
        V((n_dp, piece, cols), f32),
        V((n_dp, piece, cols), f32),
        V((2, piece, cols), f32),
        V((2, piece, cols), f32),
        V((SIDE, piece, cols), f32),
        V((SIDE, piece, cols), f32),
        V((top, cols), f32),
        V((piece - top, cols), f32),
        V((piece, cols), f32),
        V((piece, cols), f32),
        V((ring, piece, cols), f32),
        V((far, top, cols), f32),
        V((far - 1, piece - top, cols), f32),
        V((far - 1, top, cols), f32),
        V((far, piece - top, cols), f32),
        V((piece, cols), f32),
        V((2, n_dp, rows, cols), bf16),
        V((2, n_dp, rows, cols), bf16),
        V((SIDE, 8, 128), f32),
        V((SIDE, 8, 128), f32),
        V((ring, 8, 128), f32),
        V((CORES, 8, 128), f32),
        pltpu.SemaphoreType.DMA((MSGS,)),
        pltpu.SemaphoreType.DMA((MSGS,)),
        pltpu.SemaphoreType.DMA((17,)),
        pltpu.SemaphoreType.DMA((6,)),
    ]
    grad, loss = pl.pallas_call(
        functools.partial(kernel, n_dp, n_mp),
        out_shape=(
            jax.ShapeDtypeStruct((cols, cols), f32),
            jax.ShapeDtypeStruct((8, 128), f32),
        ),
        in_specs=[pl.BlockSpec(memory_space=pl.ANY)] * 2,
        out_specs=(pl.BlockSpec(memory_space=V), pl.BlockSpec(memory_space=V)),
        scratch_shapes=scratch,
        compiler_params=pltpu.CompilerParams(
            collective_id=0, has_side_effects=True, vmem_limit_bytes=60 * 2**20
        ),
    )(features, weight)
    return (grad, loss[0, 0])


def solution(mesh):
    placed = (P(None, "dp", None), P(None, "mp"))
    return jax.shard_map(
        functools.partial(body, mesh.shape["dp"], mesh.shape["mp"]),
        mesh=mesh,
        in_specs=placed,
        out_specs=(P("dp", "mp"), P()),
        check_vma=False,
    )
```

```python
import functools

import jax
import jax.numpy as jnp
from jax import lax
from jax.experimental import pallas as pl
from jax.experimental.pallas import tpu as pltpu
from jax.sharding import PartitionSpec as P

epsilon = 1e-05
off_weight = 0.0051
SIDE = 4
CORES = 2
LANES = 128
MSGS = 160
MESH = pl.DeviceIdType.MESH


class Mail:
    def __init__(self, send_sem, recv_sem):
        self.send_sem, self.recv_sem, self.sent = send_sem, recv_sem, []

    def push(self, src, dst, device):
        index = len(self.sent)
        copy = pltpu.make_async_remote_copy(
            src_ref=src,
            dst_ref=dst,
            send_sem=self.send_sem.at[index],
            recv_sem=self.recv_sem.at[index],
            device_id=device,
            device_id_type=MESH,
        )
        copy.start()
        self.sent.append(copy)
        return copy

    def close(self):
        for copy in self.sent:
            copy.wait_send()


def kernel(
    n_dp,
    n_mp,
    features,
    weight,
    grad,
    loss,
    w_buf,
    f_buf,
    acc,
    turned,
    arrived,
    cent,
    t0,
    t1,
    g_buf,
    gt_buf,
    p0,
    p1,
    opp_l,
    opp_r,
    fin_l,
    fin_r,
    opp2_l,
    opp2_r,
    fin2_l,
    fin2_r,
    sib,
    up_a,
    up_b,
    down_a,
    down_b,
    og,
    fk,
    loss_x,
    loss_y,
    loss_z,
    loss_c,
    send_sem,
    recv_sem,
    load_sem,
):
    rows = f_buf.shape[1]
    depth, cols = w_buf.shape
    batch = rows * n_dp
    sub = cols // n_dp
    ring = n_mp // CORES
    far = ring // 2
    scale = 1.0 / batch

    i = lax.axis_index("dp")
    j = lax.axis_index("mp")
    y, x = i // SIDE, i % SIDE
    z, c = j // CORES, j % CORES
    q1 = x * (1 - c) + y * c
    q2 = y * (1 - c) + x * c
    s1 = 1 * (1 - c) + SIDE * c
    s2 = SIDE * (1 - c) + 1 * c

    def index_of(a, b):
        return a * s1 + b * s2

    def ring1(q):
        return (index_of(q, q2), j)

    def ring2(q):
        return (index_of(q1, q), j)

    def zdev(q):
        return (i, q * CORES + c)

    right1, left1, far1 = (q1 + 1) % SIDE, (q1 + SIDE - 1) % SIDE, (q1 + 2) % SIDE
    right2, left2, far2 = (q2 + 1) % SIDE, (q2 + SIDE - 1) % SIDE, (q2 + 2) % SIDE
    up, down = (z + 1) % ring, (z + ring - 1) % ring
    sibling = (i, z * CORES + 1 - c)
    mail = Mail(send_sem, recv_sem)
    low, high = pl.ds(0, sub // 2), pl.ds(sub // 2, sub // 2)

    barrier = pltpu.get_barrier_semaphore()
    for d in range(1, n_dp):
        pl.semaphore_signal(barrier, inc=1, device_id=((i + d) % n_dp, j), device_id_type=MESH)
    for d in range(1, ring):
        pl.semaphore_signal(barrier, inc=1, device_id=zdev((z + d) % ring), device_id_type=MESH)
    pl.semaphore_signal(barrier, inc=1, device_id=sibling, device_id_type=MESH)

    parts = 8
    step = depth // parts

    def loads(k):
        cut = pl.ds(pl.multiple_of(k * step, step), step)
        return (
            pltpu.make_async_copy(weight.at[cut, :], w_buf.at[cut, :], load_sem.at[k]),
            pltpu.make_async_copy(
                features.at[:, :, cut], f_buf.at[:, :, cut], load_sem.at[parts + k]
            ),
        )

    for k in range(parts):
        for load in loads(k):
            load.start()

    quarters = cols // LANES

    def quarter(q):
        return pl.ds(pl.multiple_of((q % quarters) * LANES, LANES), LANES)

    def feature_cut(a):
        return pl.ds(pl.multiple_of(a * cols + (z % quarters) * LANES, LANES), LANES)

    own_k = pltpu.make_async_copy(
        features.at[c, :, feature_cut(i)], fk.at[c, i, :, quarter(z)], load_sem.at[2 * parts]
    )
    own_k.start()
    acc[...] = jnp.zeros_like(acc)

    pl.semaphore_wait(barrier, n_dp - 1 + ring - 1 + 1)
    feature_copies = []
    for d in range(1, n_dp):
        other = (i + d) % n_dp
        feature_copies.append(
            mail.push(
                features.at[c, :, feature_cut(other)], fk.at[c, i, :, quarter(z)], (other, j)
            )
        )

    def project(k, carry):
        for load in loads(k):
            load.wait()
        cut = pl.ds(pl.multiple_of(k * step, step), step)
        left = f_buf[:, :, cut].reshape(2 * rows, step)
        got = jnp.dot(left, w_buf[cut, :], preferred_element_type=jnp.float32)
        acc[:, 0:rows, :] += got.reshape(2, rows, cols)
        return carry

    lax.fori_loop(0, parts, project, 0)

    for v in range(2):
        turned[v] = acc[v].T
    strip_copies = []
    for d in range(1, n_dp):
        other = (i + d) % n_dp
        cut = pl.ds(pl.multiple_of(other * sub, sub), sub)
        strip_copies.append(mail.push(turned.at[:, cut, :], arrived.at[i], (other, j)))
    arrived[i] = turned[:, pl.ds(pl.multiple_of(i * sub, sub), sub), :]

    own_k.wait()
    for copy in feature_copies:
        copy.wait_recv()
    mine = fk.at[c, :, :, quarter(z)]
    feature_up = mail.push(mine, mine, zdev(up))
    feature_down = mail.push(mine, mine, zdev(down))

    for copy in strip_copies:
        copy.wait_recv()

    inv_std = [None, None]
    for v in (0, 1):
        strip = jnp.concatenate([arrived[a, v][:, 0:rows] for a in range(n_dp)], axis=1)
        mean = jnp.sum(strip, axis=1, keepdims=True) * scale
        shifted = strip - mean
        variance = jnp.sum(shifted * shifted, axis=1, keepdims=True) * scale
        inv_std[v] = lax.rsqrt(variance + epsilon)
        centered = shifted * inv_std[v]
        cent[v] = centered
        if v == 0:
            t0[j] = centered.astype(jnp.bfloat16)
        else:
            t1[i] = centered.astype(jnp.bfloat16)

    def gather(block, first_flip):
        own = block(index_of(q1, q2))
        ends = []

        def onward(a):
            part = block(index_of(a, q2))
            return (mail.push(part, part, ring2(right2)), mail.push(part, part, ring2(left2)))

        def across(n, a, pair):
            pair[0].wait_recv()
            pair[1].wait_recv()
            if (n + first_flip) % 2 == 0:
                part = block(index_of(a, left2))
                ends.append(mail.push(part, part, ring2(right2)))
            else:
                part = block(index_of(a, right2))
                ends.append(mail.push(part, part, ring2(left2)))

        to_right = mail.push(own, own, ring1(right1))
        to_left = mail.push(own, own, ring1(left1))
        pair_own = onward(q1)
        yield
        to_right.wait_recv()
        part = block(index_of(left1, q2)).at[low]
        far_low = mail.push(part, part, ring1(right1))
        pair_left = onward(left1)
        yield
        to_left.wait_recv()
        part = block(index_of(right1, q2)).at[high]
        far_high = mail.push(part, part, ring1(left1))
        pair_right = onward(right1)
        yield
        across(0, q1, pair_own)
        yield
        far_low.wait_recv()
        far_high.wait_recv()
        pair_far = onward(far1)
        yield
        across(1, left1, pair_left)
        yield
        across(2, right1, pair_right)
        yield
        across(3, far1, pair_far)
        yield
        for copy in ends:
            copy.wait_recv()

    def gather_z():
        side = []

        def to_side(q):
            part = t0.at[q * CORES + c]
            side.append(mail.push(part, part, sibling))

        part = t0.at[j]
        ups, downs = [mail.push(part, part, zdev(up))], [mail.push(part, part, zdev(down))]
        to_side(z)
        for t in range(1, far):
            yield
            below, above = (z + ring - t) % ring, (z + t) % ring
            part = t0.at[below * CORES + c]
            ups[-1].wait_recv()
            part = part if t < far - 1 else part.at[low]
            ups.append(mail.push(part, part, zdev(up)))
            part = t0.at[above * CORES + c]
            downs[-1].wait_recv()
            part = part if t < far - 1 else part.at[high]
            downs.append(mail.push(part, part, zdev(down)))
            to_side(below)
            to_side(above)
        yield
        ups[-1].wait_recv()
        downs[-1].wait_recv()
        to_side((z + far) % ring)
        yield
        for copy in side:
            copy.wait_recv()

    def feature_chain():
        yield
        feature_up.wait_recv()
        part = fk.at[c, pl.ds(0, n_dp // 2), :, quarter(z + ring - 1)]
        one = mail.push(part, part, zdev(up))
        feature_down.wait_recv()
        part = fk.at[c, pl.ds(n_dp // 2, n_dp // 2), :, quarter(z + 1)]
        two = mail.push(part, part, zdev(down))
        yield
        one.wait_recv()
        two.wait_recv()
        last = mail.push(fk.at[c], fk.at[c], sibling)
        yield
        last.wait_recv()

    def run(chain, steps=99):
        for _ in range(steps):
            if next(chain, 0) == 0:
                return

    rows_of_second = gather(lambda a: t1.at[a], 0)
    rows_of_first = gather_z()
    wanted = feature_chain()
    run(rows_of_second, 1)
    run(rows_of_first, 1)
    run(wanted, 1)
    run(rows_of_second, 2)
    run(rows_of_first, 1)
    run(rows_of_second, 1)
    run(rows_of_first, 1)
    run(wanted, 1)
    run(rows_of_second, 2)
    run(rows_of_first, 1)
    run(rows_of_second, 2)
    run(rows_of_first, 1)
    run(wanted, 1)
    run(rows_of_first)
    run(rows_of_second)

    tile = 256

    def correlate(t, total):
        per = tile // sub
        left = t0[pl.ds(t * per, per)].reshape(tile, batch)
        corr = lax.dot_general(
            left, t1[...].reshape(cols, batch), (((1,), (1,)), ((), ())),
            preferred_element_type=jnp.float32,
        ) * scale
        r = t * tile + lax.broadcasted_iota(jnp.int32, (tile, cols), 0)
        where_diagonal = jnp.where(r // sub == j, i * sub + r % sub, -1)
        on_diagonal = where_diagonal == lax.broadcasted_iota(jnp.int32, (tile, cols), 1)
        gap = corr - 1.0
        terms = jnp.where(on_diagonal, gap * gap, off_weight * corr * corr)
        g = jnp.where(on_diagonal, 2.0 * gap, 2.0 * off_weight * corr)
        g_buf[pl.ds(pl.multiple_of(t * tile, tile), tile), :] = g.astype(jnp.bfloat16)
        gt_buf[:, pl.ds(pl.multiple_of(t * tile, tile), tile)] = g.T.astype(jnp.bfloat16)
        return total + jnp.sum(terms, axis=0, keepdims=True)

    total = lax.fori_loop(0, cols // tile, correlate, jnp.zeros((1, cols), jnp.float32))

    wide = batch // 3

    def partial(into, left, right):
        def one(t, carry):
            cut = pl.ds(pl.multiple_of(t * wide, wide), wide)
            got = jnp.dot(
                left[...], right[:, :, cut].reshape(cols, wide), preferred_element_type=jnp.float32
            )
            into[:, :, cut] = (got * scale).reshape(n_dp, sub, wide)
            return carry

        lax.fori_loop(0, batch // wide, one, 0)

    def scatter():
        fars_r = [mail.push(p1.at[index_of(far1, n)], opp_l.at[n], ring1(right1)) for n in (0, 1)]
        fars_l = [
            mail.push(p1.at[index_of(far1, 2 + n)], opp_r.at[n], ring1(left1)) for n in (0, 1)
        ]
        near_r = [None, None] + [
            mail.push(p1.at[index_of(right1, n)], fin_l.at[n], ring1(right1)) for n in (2, 3)
        ]
        near_l = [
            mail.push(p1.at[index_of(left1, n)], fin_r.at[n], ring1(left1)) for n in (0, 1)
        ] + [None, None]
        for n in (0, 1):
            yield
            fars_r[n].wait_recv()
            at = index_of(right1, n)
            p1[at] = p1[at] + opp_l[n]
            near_r[n] = mail.push(p1.at[at], fin_l.at[n], ring1(right1))
            fars_l[n].wait_recv()
            at = index_of(left1, 2 + n)
            p1[at] = p1[at] + opp_r[n]
            near_l[2 + n] = mail.push(p1.at[at], fin_r.at[2 + n], ring1(left1))
        yield
        for n in range(SIDE):
            near_r[n].wait_recv()
            near_l[n].wait_recv()
            at = index_of(q1, n)
            p1[at] = p1[at] + fin_l[n] + fin_r[n]
        at_far, at_right, at_left = (index_of(q1, q) for q in (far2, right2, left2))
        far_r = mail.push(p1.at[at_far, low], opp2_l, ring2(right2))
        far_l = mail.push(p1.at[at_far, high], opp2_r, ring2(left2))
        ends = [
            mail.push(p1.at[at_right, high], fin2_l.at[high], ring2(right2)),
            mail.push(p1.at[at_left, low], fin2_r.at[low], ring2(left2)),
        ]
        yield
        far_r.wait_recv()
        p1[at_right, low] = p1[at_right, low] + opp2_l[...]
        ends.append(mail.push(p1.at[at_right, low], fin2_l.at[low], ring2(right2)))
        far_l.wait_recv()
        p1[at_left, high] = p1[at_left, high] + opp2_r[...]
        ends.append(mail.push(p1.at[at_left, high], fin2_r.at[high], ring2(left2)))
        yield
        for copy in ends:
            copy.wait_recv()
        finish(1, p1[i] + fin2_l[...] + fin2_r[...])

    def scatter_z():
        order = [(z + far) % ring]
        for t in range(far - 1, 0, -1):
            order += [(z + t) % ring, (z + ring - t) % ring]
        order.append(z)
        side = [mail.push(p0.at[q * CORES + 1 - c], sib.at[q], sibling) for q in order]

        def settle(n):
            side[n].wait_recv()
            at = order[n] * CORES + c
            p0[at] = p0[at] + sib[order[n]]

        def above(t):
            return (z + t) % ring

        def below(t):
            return (z + ring - t) % ring

        def part(q, cut):
            return p0.at[q * CORES + c, cut]

        def pass_on(chain, buf, cut, dest, device):
            n = len(chain) - 1
            chain[n].wait_recv()
            at = dest * CORES + c
            p0[at, cut] = p0[at, cut] + buf[n]
            chain.append(mail.push(p0.at[at, cut], buf.at[n + 1], device))

        yield
        settle(0)
        ua = [mail.push(part(above(far), low), up_a.at[0], zdev(up))]
        db = [mail.push(part(below(far), high), down_b.at[0], zdev(down))]
        settle(1)
        ub = [mail.push(part(above(far - 1), high), up_b.at[0], zdev(up))]
        settle(2)
        da = [mail.push(part(below(far - 1), low), down_a.at[0], zdev(down))]
        for n in range(3, ring):
            settle(n)
        for t in range(far - 1, 0, -1):
            yield
            pass_on(ua, up_a, low, above(t), zdev(up))
            pass_on(db, down_b, high, below(t), zdev(down))
            if t > 1:
                yield
                pass_on(ub, up_b, high, above(t - 1), zdev(up))
                pass_on(da, down_a, low, below(t - 1), zdev(down))
        yield
        for chain in (ub, da, ua, db):
            chain[-1].wait_recv()
        p0[j, low] = p0[j, low] + up_a[far - 1] + down_a[far - 2]
        p0[j, high] = p0[j, high] + up_b[far - 2] + down_b[far - 1]
        finish(0, p0[j])

    def finish(v, got):
        first = jnp.sum(got, axis=1, keepdims=True) * scale
        cross = jnp.sum(got * cent[v], axis=1, keepdims=True) * scale
        og[v, i] = (inv_std[v] * (got - first - cent[v] * cross)).astype(jnp.bfloat16)

    def loss_chain(value):
        stages = (
            (loss_x, x, [(y * SIDE + (x + d) % SIDE, j) for d in range(1, SIDE)]),
            (loss_y, y, [(((y + d) % SIDE) * SIDE + x, j) for d in range(1, SIDE)]),
            (loss_z, z, [zdev((z + d) % ring) for d in range(1, ring)]),
            (loss_c, c, [sibling]),
        )
        for buf, at, others in stages:
            buf[at] = value
            copies = [mail.push(buf.at[at], buf.at[at], device) for device in others]
            yield
            for copy in copies:
                copy.wait_recv()
            value = buf[0]
            for n in range(1, buf.shape[0]):
                value = value + buf[n]
        loss[...] = value / (n_mp * cols)

    partial(p1, gt_buf, t0)
    second = scatter()
    run(second, 1)
    partial(p0, g_buf, t1)
    first = scatter_z()
    run(first, 1)
    score = loss_chain(jnp.broadcast_to(jnp.sum(total, axis=1, keepdims=True), (8, 128)))
    run(score, 1)
    run(first, 1)
    run(second, 2)
    run(first, 2)
    run(score, 1)
    run(first, 2)
    run(second, 1)
    run(first, 1)
    run(score, 1)
    run(second, 1)
    run(second)
    out_second = gather(lambda a: og.at[1, a], 1)
    run(out_second, 3)
    run(first)
    out_first = gather(lambda a: og.at[0, a], 0)
    run(out_first, 1)
    run(out_second, 2)
    run(out_first, 2)
    run(score, 1)
    run(out_second, 2)
    run(out_first, 2)
    run(out_second, 1)
    run(score)
    run(out_first, 3)
    run(out_second)
    run(out_first)
    run(wanted)

    half = cols // 2

    def weigh(t, carry):
        cut = pl.ds(pl.multiple_of(t * half, half), half)
        got = jnp.dot(
            og[0].reshape(cols, batch),
            fk[0, :, :, cut].reshape(batch, half),
            preferred_element_type=jnp.float32,
        ) + jnp.dot(
            og[1].reshape(cols, batch),
            fk[1, :, :, cut].reshape(batch, half),
            preferred_element_type=jnp.float32,
        )
        grad[cut, :] = got.T
        return carry

    lax.fori_loop(0, 2, weigh, 0)

    mail.close()


def body(n_dp, n_mp, features, weight):
    rows, depth = features.shape[1], features.shape[2]
    cols = weight.shape[1]
    batch = rows * n_dp
    sub = cols // n_dp
    ring = n_mp // CORES
    far = ring // 2
    f32, bf16 = jnp.float32, jnp.bfloat16
    V = pltpu.VMEM
    scratch = [
        V((depth, cols), bf16),
        V((2, rows, depth), bf16),
        V((2, LANES, cols), f32),
        V((2, cols, LANES), f32),
        V((n_dp, 2, sub, LANES), f32),
        V((2, sub, batch), f32),
        V((n_mp, sub, batch), bf16),
        V((n_dp, sub, batch), bf16),
        V((cols, cols), bf16),
        V((cols, cols), bf16),
        V((n_mp, sub, batch), f32),
        V((n_dp, sub, batch), f32),
        V((2, sub, batch), f32),
        V((2, sub, batch), f32),
        V((SIDE, sub, batch), f32),
        V((SIDE, sub, batch), f32),
        V((sub // 2, batch), f32),
        V((sub // 2, batch), f32),
        V((sub, batch), f32),
        V((sub, batch), f32),
        V((ring, sub, batch), f32),
        V((far, sub // 2, batch), f32),
        V((far - 1, sub // 2, batch), f32),
        V((far - 1, sub // 2, batch), f32),
        V((far, sub // 2, batch), f32),
        V((2, n_dp, sub, batch), bf16),
        V((2, n_dp, rows, cols), bf16),
        V((SIDE, 8, 128), f32),
        V((SIDE, 8, 128), f32),
        V((ring, 8, 128), f32),
        V((CORES, 8, 128), f32),
        pltpu.SemaphoreType.DMA((MSGS,)),
        pltpu.SemaphoreType.DMA((MSGS,)),
        pltpu.SemaphoreType.DMA((17,)),
    ]
    grad, loss = pl.pallas_call(
        functools.partial(kernel, n_dp, n_mp),
        out_shape=(
            jax.ShapeDtypeStruct((cols, cols), f32),
            jax.ShapeDtypeStruct((8, 128), f32),
        ),
        in_specs=[pl.BlockSpec(memory_space=pl.ANY)] * 2,
        out_specs=(pl.BlockSpec(memory_space=V), pl.BlockSpec(memory_space=V)),
        scratch_shapes=scratch,
        compiler_params=pltpu.CompilerParams(
            collective_id=0, has_side_effects=True, vmem_limit_bytes=60 * 2**20
        ),
    )(features, weight)
    return (grad, loss[0, 0])


def solution(mesh):
    placed = (P(None, "dp", None), P(None, "mp"))
    return jax.shard_map(
        functools.partial(body, mesh.shape["dp"], mesh.shape["mp"]),
        mesh=mesh,
        in_specs=placed,
        out_specs=(P("dp", "mp"), P()),
        check_vma=False,
    )
```

```python
import functools

import jax
import jax.numpy as jnp
from jax import lax
from jax.experimental import pallas as pl
from jax.experimental.pallas import tpu as pltpu
from jax.sharding import PartitionSpec as P

epsilon = 1e-05
off_weight = 0.0051
SIDE = 4
CORES = 2
LANES = 128
MSGS = 170
MESH = pl.DeviceIdType.MESH


class Mail:
    def __init__(self, send_sem, recv_sem):
        self.send_sem, self.recv_sem, self.sent = send_sem, recv_sem, []

    def push(self, src, dst, device):
        index = len(self.sent)
        copy = pltpu.make_async_remote_copy(
            src_ref=src,
            dst_ref=dst,
            send_sem=self.send_sem.at[index],
            recv_sem=self.recv_sem.at[index],
            device_id=device,
            device_id_type=MESH,
        )
        copy.start()
        self.sent.append(copy)
        return copy

    def close(self):
        for copy in self.sent:
            copy.wait_send()


def kernel(
    n_dp,
    n_mp,
    features,
    weight,
    grad,
    loss,
    w_buf,
    f_buf,
    acc,
    turned,
    arrived,
    cent,
    t0,
    t1,
    g_buf,
    gt_buf,
    p0,
    p1,
    opp_l,
    opp_r,
    fin_l,
    fin_r,
    opp2_l,
    opp2_r,
    fin2_l,
    fin2_r,
    sib,
    up_a,
    up_b,
    down_a,
    down_b,
    og,
    fk,
    part_buf,
    loss_x,
    loss_y,
    loss_z,
    loss_c,
    send_sem,
    recv_sem,
    load_sem,
):
    rows = f_buf.shape[1]
    depth, cols = w_buf.shape
    batch = rows * n_dp
    sub = cols // n_dp
    ring = n_mp // CORES
    far = ring // 2
    scale = 1.0 / batch

    i = lax.axis_index("dp")
    j = lax.axis_index("mp")
    y, x = i // SIDE, i % SIDE
    z, c = j // CORES, j % CORES
    q1 = x * (1 - c) + y * c
    q2 = y * (1 - c) + x * c
    s1 = 1 * (1 - c) + SIDE * c
    s2 = SIDE * (1 - c) + 1 * c

    def index_of(a, b):
        return a * s1 + b * s2

    def slot_of(a, b):
        return a * SIDE + b

    def ring1(q):
        return (index_of(q, q2), j)

    def ring2(q):
        return (index_of(q1, q), j)

    def zdev(q):
        return (i, q * CORES + c)

    right1, left1, far1 = (q1 + 1) % SIDE, (q1 + SIDE - 1) % SIDE, (q1 + 2) % SIDE
    right2, left2, far2 = (q2 + 1) % SIDE, (q2 + SIDE - 1) % SIDE, (q2 + 2) % SIDE
    up, down = (z + 1) % ring, (z + ring - 1) % ring
    sibling = (i, z * CORES + 1 - c)
    mail = Mail(send_sem, recv_sem)
    low, high = pl.ds(0, sub // 2), pl.ds(sub // 2, sub // 2)

    barrier = pltpu.get_barrier_semaphore()
    for d in range(1, n_dp):
        pl.semaphore_signal(barrier, inc=1, device_id=((i + d) % n_dp, j), device_id_type=MESH)
    for d in range(1, ring):
        pl.semaphore_signal(barrier, inc=1, device_id=zdev((z + d) % ring), device_id_type=MESH)
    pl.semaphore_signal(barrier, inc=1, device_id=sibling, device_id_type=MESH)

    parts = 8
    step = depth // parts

    def loads(k):
        cut = pl.ds(pl.multiple_of(k * step, step), step)
        return (
            pltpu.make_async_copy(weight.at[cut, :], w_buf.at[cut, :], load_sem.at[k]),
            pltpu.make_async_copy(
                features.at[:, :, cut], f_buf.at[:, :, cut], load_sem.at[parts + k]
            ),
        )

    for k in range(parts):
        for load in loads(k):
            load.start()

    acc[...] = jnp.zeros_like(acc)

    def project(k, carry):
        for load in loads(k):
            load.wait()
        cut = pl.ds(pl.multiple_of(k * step, step), step)
        left = f_buf[:, :, cut].reshape(2 * rows, step)
        got = jnp.dot(left, w_buf[cut, :], preferred_element_type=jnp.float32)
        acc[:, 0:rows, :] += got.reshape(2, rows, cols)
        return carry

    lax.fori_loop(0, parts, project, 0)
    for v in range(2):
        turned[v] = acc[v].T

    pl.semaphore_wait(barrier, n_dp - 1 + ring - 1 + 1)

    strip_copies = []
    for d in range(1, n_dp):
        other = (i + d) % n_dp
        cut = pl.ds(pl.multiple_of(other * sub, sub), sub)
        strip_copies.append(mail.push(turned.at[:, cut, :], arrived.at[i], (other, j)))
    arrived[i] = turned[:, pl.ds(pl.multiple_of(i * sub, sub), sub), :]

    for copy in strip_copies:
        copy.wait_recv()

    inv_std = [None, None]
    for v in (0, 1):
        strip = jnp.concatenate([arrived[a, v][:, 0:rows] for a in range(n_dp)], axis=1)
        mean = jnp.sum(strip, axis=1, keepdims=True) * scale
        shifted = strip - mean
        variance = jnp.sum(shifted * shifted, axis=1, keepdims=True) * scale
        inv_std[v] = lax.rsqrt(variance + epsilon)
        centered = shifted * inv_std[v]
        cent[v] = centered
        if v == 0:
            t0[j] = centered.astype(jnp.bfloat16)
        else:
            t1[slot_of(q1, q2)] = centered.astype(jnp.bfloat16)

    def gather(block, at, first_flip):
        own = block(at(q1, q2))
        ends = []

        def onward(a):
            part = block(at(a, q2))
            return (mail.push(part, part, ring2(right2)), mail.push(part, part, ring2(left2)))

        def across(n, a, pair):
            pair[0].wait_recv()
            pair[1].wait_recv()
            if (n + first_flip) % 2 == 0:
                part = block(at(a, left2))
                ends.append(mail.push(part, part, ring2(right2)))
            else:
                part = block(at(a, right2))
                ends.append(mail.push(part, part, ring2(left2)))

        to_right = mail.push(own, own, ring1(right1))
        to_left = mail.push(own, own, ring1(left1))
        pair_own = onward(q1)
        yield
        to_right.wait_recv()
        part = block(at(left1, q2)).at[low]
        far_low = mail.push(part, part, ring1(right1))
        pair_left = onward(left1)
        yield
        to_left.wait_recv()
        part = block(at(right1, q2)).at[high]
        far_high = mail.push(part, part, ring1(left1))
        pair_right = onward(right1)
        yield
        across(0, q1, pair_own)
        yield
        far_low.wait_recv()
        far_high.wait_recv()
        pair_far = onward(far1)
        yield
        across(1, left1, pair_left)
        yield
        across(2, right1, pair_right)
        yield
        across(3, far1, pair_far)
        yield
        for copy in ends:
            copy.wait_recv()

    def gather_z():
        side = []

        def block(q):
            return t0.at[q * CORES + c]

        def to_side(q):
            side.append(mail.push(block(q), block(q), sibling))

        def hop(q, cut, device):
            part = block(q).at[cut]
            return mail.push(part, part, device)

        up_low, down_high = hop(z, low, zdev(up)), hop(z, high, zdev(down))
        up_high, down_low = hop(z, high, zdev(up)), hop(z, low, zdev(down))
        to_side(z)
        for t in range(1, far):
            below, above = (z + ring - t) % ring, (z + t) % ring
            yield
            up_low.wait_recv()
            up_low = hop(below, low, zdev(up))
            down_high.wait_recv()
            down_high = hop(above, high, zdev(down))
            yield
            up_high.wait_recv()
            if t < far - 1:
                up_high = hop(below, high, zdev(up))
            down_low.wait_recv()
            if t < far - 1:
                down_low = hop(above, low, zdev(down))
            to_side(below)
            to_side(above)
        yield
        up_low.wait_recv()
        down_high.wait_recv()
        to_side((z + far) % ring)
        yield
        for copy in side:
            copy.wait_recv()

    quarters = cols // LANES

    def quarter(q):
        return pl.ds(pl.multiple_of((q % quarters) * LANES, LANES), LANES)

    def feature_cut(a):
        return pl.ds(pl.multiple_of(a * cols + (z % quarters) * LANES, LANES), LANES)

    def feature_chain():
        own = pltpu.make_async_copy(
            features.at[c, :, feature_cut(i)], fk.at[c, i, :, quarter(z)], load_sem.at[2 * parts]
        )
        own.start()
        copies = []
        for d in range(1, n_dp):
            other = (i + d) % n_dp
            copies.append(
                mail.push(
                    features.at[c, :, feature_cut(other)], fk.at[c, i, :, quarter(z)], (other, j)
                )
            )
        yield
        own.wait()
        for copy in copies:
            copy.wait_recv()
        part = fk.at[c, :, :, quarter(z)]
        one = mail.push(part, part, zdev(up))
        two = mail.push(part, part, zdev(down))
        yield
        one.wait_recv()
        part = fk.at[c, pl.ds(0, n_dp // 2), :, quarter(z + ring - 1)]
        one = mail.push(part, part, zdev(up))
        two.wait_recv()
        part = fk.at[c, pl.ds(n_dp // 2, n_dp // 2), :, quarter(z + 1)]
        two = mail.push(part, part, zdev(down))
        yield
        one.wait_recv()
        two.wait_recv()
        last = mail.push(fk.at[c], fk.at[c], sibling)
        yield
        last.wait_recv()

    def run(chain, steps=99):
        for _ in range(steps):
            if next(chain, 0) == 0:
                return

    rows_of_second = gather(lambda a: t1.at[a], slot_of, 0)
    rows_of_first = gather_z()
    wanted = feature_chain()
    run(rows_of_second, 1)
    run(rows_of_first, 1)
    run(rows_of_second, 2)
    run(rows_of_first, 1)
    run(rows_of_second, 1)
    run(rows_of_first, 1)
    run(rows_of_second, 1)
    run(rows_of_first, 1)
    run(rows_of_second, 1)
    run(rows_of_first, 1)
    run(rows_of_second, 1)
    run(rows_of_first, 1)
    run(rows_of_second, 1)
    run(wanted, 1)
    run(rows_of_first, 2)
    run(rows_of_second)
    run(rows_of_first)

    tile = 256

    def correlate(t, total):
        per = tile // sub
        left = t0[pl.ds(t * per, per)].reshape(tile, batch)
        corr = lax.dot_general(
            left, t1[...].reshape(cols, batch), (((1,), (1,)), ((), ())),
            preferred_element_type=jnp.float32,
        ) * scale
        r = t * tile + lax.broadcasted_iota(jnp.int32, (tile, cols), 0)
        where_diagonal = jnp.where(r // sub == j, slot_of(q1, q2) * sub + r % sub, -1)
        on_diagonal = where_diagonal == lax.broadcasted_iota(jnp.int32, (tile, cols), 1)
        gap = corr - 1.0
        terms = jnp.where(on_diagonal, gap * gap, off_weight * corr * corr)
        g = jnp.where(on_diagonal, 2.0 * gap, 2.0 * off_weight * corr)
        g_buf[pl.ds(pl.multiple_of(t * tile, tile), tile), :] = g.astype(jnp.bfloat16)
        gt_buf[:, pl.ds(pl.multiple_of(t * tile, tile), tile)] = g.T.astype(jnp.bfloat16)
        return total + jnp.sum(terms, axis=0, keepdims=True)

    total = lax.fori_loop(0, cols // tile, correlate, jnp.zeros((1, cols), jnp.float32))

    wide = batch // 3

    def partial(into, left, right):
        def one(t, carry):
            cut = pl.ds(pl.multiple_of(t * wide, wide), wide)
            got = jnp.dot(
                left[...], right[:, :, cut].reshape(cols, wide), preferred_element_type=jnp.float32
            )
            into[:, :, cut] = (got * scale).reshape(n_dp, sub, wide)
            return carry

        lax.fori_loop(0, batch // wide, one, 0)

    def scatter():
        f, r, l, o = far2, right2, left2, q2
        far_f = mail.push(p1.at[slot_of(far1, f)], opp_l.at[0], ring1(right1))
        far_l = mail.push(p1.at[slot_of(far1, l)], opp_r.at[0], ring1(left1))
        far_r = mail.push(p1.at[slot_of(far1, r)], opp_l.at[1], ring1(right1))
        far_o = mail.push(p1.at[slot_of(far1, o)], opp_r.at[1], ring1(left1))
        l_right = mail.push(p1.at[slot_of(right1, l)], fin_l.at[2], ring1(right1))
        f_left = mail.push(p1.at[slot_of(left1, f)], fin_r.at[0], ring1(left1))

        def onward(copy, at, buf, n, into, m, device):
            copy.wait_recv()
            p1[at] = p1[at] + buf[n]
            return mail.push(p1.at[at], into.at[m], device)

        def settle(n, m, one, two):
            one.wait_recv()
            two.wait_recv()
            at = slot_of(q1, n)
            p1[at] = p1[at] + fin_l[m] + fin_r[m]
            return at

        yield
        f_right = onward(far_f, slot_of(right1, f), opp_l, 0, fin_l, 0, ring1(right1))
        l_left = onward(far_l, slot_of(left1, l), opp_r, 0, fin_r, 2, ring1(left1))
        r_left = mail.push(p1.at[slot_of(left1, r)], fin_r.at[1], ring1(left1))
        yield
        r_right = onward(far_r, slot_of(right1, r), opp_l, 1, fin_l, 1, ring1(right1))
        o_right = mail.push(p1.at[slot_of(right1, o)], fin_l.at[3], ring1(right1))
        o_left = onward(far_o, slot_of(left1, o), opp_r, 1, fin_r, 3, ring1(left1))
        yield
        at = settle(f, 0, f_right, f_left)
        opp_low = mail.push(p1.at[at, low], opp2_l, ring2(right2))
        opp_high = mail.push(p1.at[at, high], opp2_r, ring2(left2))
        yield
        at_left = settle(l, 2, l_right, l_left)
        ends = [mail.push(p1.at[at_left, low], fin2_r.at[low], ring2(left2))]
        yield
        at_right = settle(r, 1, r_right, r_left)
        ends.append(mail.push(p1.at[at_right, high], fin2_l.at[high], ring2(right2)))
        yield
        opp_low.wait_recv()
        p1[at_right, low] = p1[at_right, low] + opp2_l[...]
        ends.append(mail.push(p1.at[at_right, low], fin2_l.at[low], ring2(right2)))
        opp_high.wait_recv()
        p1[at_left, high] = p1[at_left, high] + opp2_r[...]
        ends.append(mail.push(p1.at[at_left, high], fin2_r.at[high], ring2(left2)))
        yield
        at = settle(o, 3, o_right, o_left)
        yield
        for copy in ends:
            copy.wait_recv()
        finish(1, p1[at] + fin2_l[...] + fin2_r[...])

    def scatter_z():
        order = [(z + far) % ring]
        for t in range(far - 1, 0, -1):
            order += [(z + t) % ring, (z + ring - t) % ring]
        order.append(z)
        side = [mail.push(p0.at[q * CORES + 1 - c], sib.at[q], sibling) for q in order]

        def settle(n):
            side[n].wait_recv()
            at = order[n] * CORES + c
            p0[at] = p0[at] + sib[order[n]]

        def above(t):
            return (z + t) % ring

        def below(t):
            return (z + ring - t) % ring

        def part(q, cut):
            return p0.at[q * CORES + c, cut]

        def pass_on(chain, buf, cut, dest, device):
            n = len(chain) - 1
            chain[n].wait_recv()
            at = dest * CORES + c
            p0[at, cut] = p0[at, cut] + buf[n]
            chain.append(mail.push(p0.at[at, cut], buf.at[n + 1], device))

        yield
        settle(0)
        ua = [mail.push(part(above(far), low), up_a.at[0], zdev(up))]
        db = [mail.push(part(below(far), high), down_b.at[0], zdev(down))]
        settle(1)
        ub = [mail.push(part(above(far - 1), high), up_b.at[0], zdev(up))]
        settle(2)
        da = [mail.push(part(below(far - 1), low), down_a.at[0], zdev(down))]
        for n in range(3, ring):
            settle(n)
        for t in range(far - 1, 0, -1):
            yield
            pass_on(ua, up_a, low, above(t), zdev(up))
            pass_on(db, down_b, high, below(t), zdev(down))
            if t > 1:
                yield
                pass_on(ub, up_b, high, above(t - 1), zdev(up))
                pass_on(da, down_a, low, below(t - 1), zdev(down))
        yield
        for chain in (ub, da, ua, db):
            chain[-1].wait_recv()
        p0[j, low] = p0[j, low] + up_a[far - 1] + down_a[far - 2]
        p0[j, high] = p0[j, high] + up_b[far - 2] + down_b[far - 1]
        finish(0, p0[j])

    def finish(v, got):
        first = jnp.sum(got, axis=1, keepdims=True) * scale
        cross = jnp.sum(got * cent[v], axis=1, keepdims=True) * scale
        og[v, i] = (inv_std[v] * (got - first - cent[v] * cross)).astype(jnp.bfloat16)

    def loss_chain(value):
        stages = (
            (loss_x, x, [(y * SIDE + (x + d) % SIDE, j) for d in range(1, SIDE)]),
            (loss_y, y, [(((y + d) % SIDE) * SIDE + x, j) for d in range(1, SIDE)]),
            (loss_z, z, [zdev((z + d) % ring) for d in range(1, ring)]),
            (loss_c, c, [sibling]),
        )
        for buf, at, others in stages:
            buf[at] = value
            copies = [mail.push(buf.at[at], buf.at[at], device) for device in others]
            yield
            for copy in copies:
                copy.wait_recv()
            value = buf[0]
            for n in range(1, buf.shape[0]):
                value = value + buf[n]
        loss[...] = value[0:1, 0:1] / (n_mp * cols)

    partial(p1, gt_buf, t0)
    second = scatter()
    run(second, 1)
    partial(p0, g_buf, t1)
    first = scatter_z()
    run(first, 1)
    score = loss_chain(jnp.broadcast_to(jnp.sum(total, axis=1, keepdims=True), (8, 128)))
    run(score, 1)
    run(second, 1)
    run(first, 1)
    run(second, 1)
    run(first, 1)
    run(score, 1)
    run(first, 1)
    run(second, 1)
    run(second, 1)
    run(first, 1)
    run(score, 1)
    run(second, 1)
    run(first, 1)
    run(second, 1)
    run(second, 1)
    run(first, 1)
    run(wanted, 1)
    run(second)
    out_second = gather(lambda a: og.at[1, a], index_of, 1)
    run(out_second, 3)
    run(score, 1)
    run(first)
    out_first = gather(lambda a: og.at[0, a], index_of, 0)
    run(out_first, 1)
    run(out_second, 2)
    run(out_first, 2)
    run(wanted, 1)
    run(score)
    run(out_second, 1)
    run(out_first, 1)
    run(out_second, 1)
    run(out_first, 1)
    run(out_second, 1)
    run(out_first, 1)
    run(wanted, 1)
    run(out_first, 1)
    run(out_first, 1)
    run(out_second)
    run(wanted)

    half = cols // 2

    def weigh(v, t):
        cut = pl.ds(pl.multiple_of(t * half, half), half)
        return cut, jnp.dot(
            og[v].reshape(cols, batch),
            fk[v, :, :, cut].reshape(batch, half),
            preferred_element_type=jnp.float32,
        )

    def weigh_second(t, carry):
        cut, got = weigh(1, t)
        part_buf[:, cut] = got
        return carry

    def weigh_first(t, carry):
        cut, got = weigh(0, t)
        grad[cut, :] = (got + part_buf[:, cut]).T
        return carry

    lax.fori_loop(0, 2, weigh_second, 0)
    run(out_first)
    lax.fori_loop(0, 2, weigh_first, 0)

    mail.close()


def body(n_dp, n_mp, features, weight):
    rows, depth = features.shape[1], features.shape[2]
    cols = weight.shape[1]
    batch = rows * n_dp
    sub = cols // n_dp
    ring = n_mp // CORES
    far = ring // 2
    f32, bf16 = jnp.float32, jnp.bfloat16
    V = pltpu.VMEM
    scratch = [
        V((depth, cols), bf16),
        V((2, rows, depth), bf16),
        V((2, LANES, cols), f32),
        V((2, cols, LANES), f32),
        V((n_dp, 2, sub, LANES), f32),
        V((2, sub, batch), f32),
        V((n_mp, sub, batch), bf16),
        V((n_dp, sub, batch), bf16),
        V((cols, cols), bf16),
        V((cols, cols), bf16),
        V((n_mp, sub, batch), f32),
        V((n_dp, sub, batch), f32),
        V((2, sub, batch), f32),
        V((2, sub, batch), f32),
        V((SIDE, sub, batch), f32),
        V((SIDE, sub, batch), f32),
        V((sub // 2, batch), f32),
        V((sub // 2, batch), f32),
        V((sub, batch), f32),
        V((sub, batch), f32),
        V((ring, sub, batch), f32),
        V((far, sub // 2, batch), f32),
        V((far - 1, sub // 2, batch), f32),
        V((far - 1, sub // 2, batch), f32),
        V((far, sub // 2, batch), f32),
        V((2, n_dp, sub, batch), bf16),
        V((2, n_dp, rows, cols), bf16),
        V((cols, cols), f32),
        V((SIDE, 8, 128), f32),
        V((SIDE, 8, 128), f32),
        V((ring, 8, 128), f32),
        V((CORES, 8, 128), f32),
        pltpu.SemaphoreType.DMA((MSGS,)),
        pltpu.SemaphoreType.DMA((MSGS,)),
        pltpu.SemaphoreType.DMA((17,)),
    ]
    grad, loss = pl.pallas_call(
        functools.partial(kernel, n_dp, n_mp),
        out_shape=(
            jax.ShapeDtypeStruct((cols, cols), f32),
            jax.ShapeDtypeStruct((1, 1), f32),
        ),
        in_specs=[pl.BlockSpec(memory_space=pl.ANY)] * 2,
        out_specs=(pl.BlockSpec(memory_space=V), pl.BlockSpec(memory_space=V)),
        scratch_shapes=scratch,
        compiler_params=pltpu.CompilerParams(
            collective_id=0, has_side_effects=True, vmem_limit_bytes=60 * 2**20
        ),
    )(features, weight)
    return (grad, loss.reshape(()))


def solution(mesh):
    placed = (P(None, "dp", None), P(None, "mp"))
    return jax.shard_map(
        functools.partial(body, mesh.shape["dp"], mesh.shape["mp"]),
        mesh=mesh,
        in_specs=placed,
        out_specs=(P("dp", "mp"), P()),
        check_vma=False,
    )
```

```python
import functools

import jax
import jax.numpy as jnp
from jax import lax
from jax.experimental import pallas as pl
from jax.experimental.pallas import tpu as pltpu
from jax.sharding import PartitionSpec as P

epsilon = 1e-05
off_weight = 0.0051
SIDE = 4
CORES = 2
LANES = 128
MSGS = 190
MESH = pl.DeviceIdType.MESH
OFFSETS = sorted(
    ((a, b) for a in range(SIDE) for b in range(SIDE) if a or b),
    key=lambda o: -min(o[0], SIDE - o[0]) - min(o[1], SIDE - o[1]),
)


class Mail:
    def __init__(self, send_sem, recv_sem):
        self.send_sem, self.recv_sem, self.sent = send_sem, recv_sem, []

    def push(self, src, dst, device):
        index = len(self.sent)
        copy = pltpu.make_async_remote_copy(
            src_ref=src,
            dst_ref=dst,
            send_sem=self.send_sem.at[index],
            recv_sem=self.recv_sem.at[index],
            device_id=device,
            device_id_type=MESH,
        )
        copy.start()
        self.sent.append(copy)
        return copy

    def close(self):
        for copy in self.sent:
            copy.wait_send()


def kernel(
    n_dp,
    n_mp,
    features,
    weight,
    grad,
    loss,
    w_buf,
    f_buf,
    acc,
    turned,
    arrived,
    cent,
    t0,
    t1,
    g_buf,
    gt_buf,
    p0,
    p1,
    opp_l,
    opp_r,
    fin_l,
    fin_r,
    opp2_l,
    opp2_r,
    fin2_l,
    fin2_r,
    sib,
    up_a,
    up_b,
    down_a,
    down_b,
    og,
    fk,
    part_buf,
    loss_x,
    loss_y,
    loss_z,
    loss_c,
    send_sem,
    recv_sem,
    load_sem,
):
    rows = f_buf.shape[1]
    depth, cols = w_buf.shape
    batch = rows * n_dp
    sub = cols // n_dp
    ring = n_mp // CORES
    far = ring // 2
    scale = 1.0 / batch

    i = lax.axis_index("dp")
    j = lax.axis_index("mp")
    y, x = i // SIDE, i % SIDE
    z, c = j // CORES, j % CORES
    q1 = x * (1 - c) + y * c
    q2 = y * (1 - c) + x * c
    s1 = 1 * (1 - c) + SIDE * c
    s2 = SIDE * (1 - c) + 1 * c

    def index_of(a, b):
        return a * s1 + b * s2

    def slot_of(a, b):
        return a * SIDE + b

    def ring1(q):
        return (index_of(q, q2), j)

    def ring2(q):
        return (index_of(q1, q), j)

    def zdev(q):
        return (i, q * CORES + c)

    right1, left1, far1 = (q1 + 1) % SIDE, (q1 + SIDE - 1) % SIDE, (q1 + 2) % SIDE
    right2, left2, far2 = (q2 + 1) % SIDE, (q2 + SIDE - 1) % SIDE, (q2 + 2) % SIDE
    up, down = (z + 1) % ring, (z + ring - 1) % ring
    sibling = (i, z * CORES + 1 - c)
    mail = Mail(send_sem, recv_sem)
    low, high = pl.ds(0, sub // 2), pl.ds(sub // 2, sub // 2)

    parts = 8
    step = depth // parts

    def loads(k):
        cut = pl.ds(pl.multiple_of(k * step, step), step)
        return (
            pltpu.make_async_copy(weight.at[cut, :], w_buf.at[cut, :], load_sem.at[k]),
            pltpu.make_async_copy(
                features.at[:, :, cut], f_buf.at[:, :, cut], load_sem.at[parts + k]
            ),
        )

    for k in range(parts):
        for load in loads(k):
            load.start()

    barrier = pltpu.get_barrier_semaphore()
    for d in range(1, n_dp):
        pl.semaphore_signal(barrier, inc=1, device_id=((i + d) % n_dp, j), device_id_type=MESH)
    for d in range(1, ring):
        pl.semaphore_signal(barrier, inc=1, device_id=zdev((z + d) % ring), device_id_type=MESH)
    pl.semaphore_signal(barrier, inc=1, device_id=sibling, device_id_type=MESH)

    acc[...] = jnp.zeros_like(acc)

    def project(k, carry):
        for load in loads(k):
            load.wait()
        cut = pl.ds(pl.multiple_of(k * step, step), step)
        left = f_buf[:, :, cut].reshape(2 * rows, step)
        got = jnp.dot(left, w_buf[cut, :], preferred_element_type=jnp.float32)
        acc[:, 0:rows, :] += got.reshape(2, rows, cols)
        return carry

    lax.fori_loop(0, parts, project, 0)
    for v in range(2):
        turned[v] = acc[v].T

    pl.semaphore_wait(barrier, n_dp - 1 + ring - 1 + 1)

    strip_copies = ([], [])
    for v in (0, 1):
        for dx, dy in OFFSETS:
            other = (y + dy) % SIDE * SIDE + (x + dx) % SIDE
            cut = pl.ds(pl.multiple_of(other * sub, sub), sub)
            strip_copies[v].append(
                mail.push(turned.at[v, cut, :], arrived.at[i, v], (other, j))
            )
    arrived[i] = turned[:, pl.ds(pl.multiple_of(i * sub, sub), sub), :]
    inv_std = [None, None]

    def normalize(v):
        for copy in strip_copies[v]:
            copy.wait_recv()
        strip = jnp.concatenate([arrived[a, v][:, 0:rows] for a in range(n_dp)], axis=1)
        mean = jnp.sum(strip, axis=1, keepdims=True) * scale
        shifted = strip - mean
        variance = jnp.sum(shifted * shifted, axis=1, keepdims=True) * scale
        inv_std[v] = lax.rsqrt(variance + epsilon)
        centered = shifted * inv_std[v]
        cent[v] = centered
        return centered.astype(jnp.bfloat16)

    def gather(block, at, first_flip):
        own = block(at(q1, q2))
        ends = []

        def onward(a):
            part = block(at(a, q2))
            return (mail.push(part, part, ring2(right2)), mail.push(part, part, ring2(left2)))

        def across(n, a, pair):
            pair[0].wait_recv()
            pair[1].wait_recv()
            if (n + first_flip) % 2 == 0:
                part = block(at(a, left2))
                ends.append(mail.push(part, part, ring2(right2)))
            else:
                part = block(at(a, right2))
                ends.append(mail.push(part, part, ring2(left2)))

        to_right = mail.push(own, own, ring1(right1))
        to_left = mail.push(own, own, ring1(left1))
        to_far = mail.push(own, own, ring1(far1))
        pair_own = onward(q1)
        yield
        to_right.wait_recv()
        pair_left = onward(left1)
        yield
        to_left.wait_recv()
        pair_right = onward(right1)
        yield
        across(0, q1, pair_own)
        yield
        to_far.wait_recv()
        pair_far = onward(far1)
        yield
        across(1, left1, pair_left)
        yield
        across(2, right1, pair_right)
        yield
        across(3, far1, pair_far)
        yield
        for copy in ends:
            copy.wait_recv()

    def gather_z():
        side = []

        def block(q):
            return t0.at[q * CORES + c]

        def to_side(q):
            side.append(mail.push(block(q), block(q), sibling))

        def hop(q, cut, device):
            part = block(q).at[cut]
            return mail.push(part, part, device)

        up_low, down_high = hop(z, low, zdev(up)), hop(z, high, zdev(down))
        up_high, down_low = hop(z, high, zdev(up)), hop(z, low, zdev(down))
        to_side(z)
        for t in range(1, far):
            below, above = (z + ring - t) % ring, (z + t) % ring
            yield
            up_low.wait_recv()
            up_low = hop(below, low, zdev(up))
            down_high.wait_recv()
            down_high = hop(above, high, zdev(down))
            yield
            up_high.wait_recv()
            if t < far - 1:
                up_high = hop(below, high, zdev(up))
            down_low.wait_recv()
            if t < far - 1:
                down_low = hop(above, low, zdev(down))
            to_side(below)
            to_side(above)
        yield
        up_low.wait_recv()
        down_high.wait_recv()
        to_side((z + far) % ring)
        yield
        for copy in side:
            copy.wait_recv()

    quarters = cols // LANES

    def quarter(q):
        return pl.ds(pl.multiple_of((q % quarters) * LANES, LANES), LANES)

    def feature_cut(a):
        return pl.ds(pl.multiple_of(a * cols + (z % quarters) * LANES, LANES), LANES)

    def feature_chain():
        own = pltpu.make_async_copy(
            features.at[c, :, feature_cut(i)], fk.at[c, i, :, quarter(z)], load_sem.at[2 * parts]
        )
        own.start()
        copies = []
        for dx, dy in OFFSETS:
            other = (y + dy) % SIDE * SIDE + (x + dx) % SIDE
            copies.append(
                mail.push(
                    features.at[c, :, feature_cut(other)], fk.at[c, i, :, quarter(z)], (other, j)
                )
            )
        yield
        own.wait()
        for copy in copies:
            copy.wait_recv()
        halves = (pl.ds(0, n_dp // 2), pl.ds(n_dp // 2, n_dp // 2))

        def send(n, q, device):
            part = fk.at[c, halves[n], :, quarter(q)]
            return mail.push(part, part, device)

        def to_side(q):
            part = fk.at[c, :, :, quarter(q)]
            return mail.push(part, part, sibling)

        ups = [send(0, z, zdev(up)), send(1, z, zdev(up))]
        downs = [send(1, z, zdev(down)), send(0, z, zdev(down))]
        side = [to_side(z)]
        yield
        ups[0].wait_recv()
        ups.append(send(0, z + ring - 1, zdev(up)))
        downs[0].wait_recv()
        downs.append(send(1, z + 1, zdev(down)))
        yield
        ups[1].wait_recv()
        side.append(to_side(z + ring - 1))
        downs[1].wait_recv()
        side.append(to_side(z + 1))
        yield
        ups[2].wait_recv()
        downs[2].wait_recv()
        side.append(to_side(z + 2))
        yield
        for copy in side:
            copy.wait_recv()

    def run(chain, steps=99):
        for _ in range(steps):
            if next(chain, 0) == 0:
                return

    rows_of_second = gather(lambda a: t1.at[a], slot_of, 0)
    rows_of_first = gather_z()
    wanted = feature_chain()
    t0[j] = normalize(0)
    run(rows_of_first, 1)
    t1[slot_of(q1, q2)] = normalize(1)
    run(rows_of_second, 1)
    run(rows_of_first, 2)
    run(rows_of_second, 2)
    run(rows_of_first, 1)
    run(rows_of_second, 2)
    run(rows_of_first, 1)
    run(rows_of_second, 1)
    run(rows_of_first, 1)
    run(rows_of_second, 1)
    run(rows_of_first, 1)
    run(rows_of_second, 1)
    run(wanted, 1)
    run(rows_of_first, 1)
    run(rows_of_second)
    run(rows_of_first)

    tile = 256

    def correlate(t, total):
        per = tile // sub
        left = t0[pl.ds(t * per, per)].reshape(tile, batch)
        corr = lax.dot_general(
            left, t1[...].reshape(cols, batch), (((1,), (1,)), ((), ())),
            preferred_element_type=jnp.float32,
        ) * scale
        r = t * tile + lax.broadcasted_iota(jnp.int32, (tile, cols), 0)
        where_diagonal = jnp.where(r // sub == j, slot_of(q1, q2) * sub + r % sub, -1)
        on_diagonal = where_diagonal == lax.broadcasted_iota(jnp.int32, (tile, cols), 1)
        gap = corr - 1.0
        terms = jnp.where(on_diagonal, gap * gap, off_weight * corr * corr)
        g = jnp.where(on_diagonal, 2.0 * gap, 2.0 * off_weight * corr)
        g_buf[pl.ds(pl.multiple_of(t * tile, tile), tile), :] = g.astype(jnp.bfloat16)
        gt_buf[:, pl.ds(pl.multiple_of(t * tile, tile), tile)] = g.T.astype(jnp.bfloat16)
        return total + jnp.sum(terms, axis=0, keepdims=True)

    total = lax.fori_loop(0, cols // tile, correlate, jnp.zeros((1, cols), jnp.float32))

    wide = batch // 3

    def partial(into, left, right):
        def one(t, carry):
            cut = pl.ds(pl.multiple_of(t * wide, wide), wide)
            got = jnp.dot(
                left[...], right[:, :, cut].reshape(cols, wide), preferred_element_type=jnp.float32
            )
            into[:, :, cut] = (got * scale).reshape(n_dp, sub, wide)
            return carry

        lax.fori_loop(0, batch // wide, one, 0)

    def partial_line(q):
        cut = pl.ds(pl.multiple_of(q * (cols // SIDE), cols // SIDE), cols // SIDE)
        got = jnp.dot(
            gt_buf[cut, :], t0[...].reshape(cols, batch), preferred_element_type=jnp.float32
        )
        p1[pl.ds(q * SIDE, SIDE)] = (got * scale).reshape(SIDE, sub, batch)

    def scatter():
        f, r, l, o = far2, right2, left2, q2
        partial_line(far1)
        far_f = mail.push(p1.at[slot_of(far1, f)], opp_l.at[0], ring1(right1))
        far_l = mail.push(p1.at[slot_of(far1, l)], opp_r.at[0], ring1(left1))
        far_r = mail.push(p1.at[slot_of(far1, r)], opp_l.at[1], ring1(right1))
        far_o = mail.push(p1.at[slot_of(far1, o)], opp_r.at[1], ring1(left1))
        partial_line(right1)
        l_right = mail.push(p1.at[slot_of(right1, l)], fin_l.at[2], ring1(right1))
        partial_line(left1)
        f_left = mail.push(p1.at[slot_of(left1, f)], fin_r.at[0], ring1(left1))

        def onward(copy, at, buf, n, into, m, device):
            copy.wait_recv()
            p1[at] = p1[at] + buf[n]
            return mail.push(p1.at[at], into.at[m], device)

        def settle(n, m, one, two):
            one.wait_recv()
            two.wait_recv()
            at = slot_of(q1, n)
            p1[at] = p1[at] + fin_l[m] + fin_r[m]
            return at

        partial_line(q1)
        yield
        f_right = onward(far_f, slot_of(right1, f), opp_l, 0, fin_l, 0, ring1(right1))
        l_left = onward(far_l, slot_of(left1, l), opp_r, 0, fin_r, 2, ring1(left1))
        r_left = mail.push(p1.at[slot_of(left1, r)], fin_r.at[1], ring1(left1))
        yield
        r_right = onward(far_r, slot_of(right1, r), opp_l, 1, fin_l, 1, ring1(right1))
        o_right = mail.push(p1.at[slot_of(right1, o)], fin_l.at[3], ring1(right1))
        o_left = onward(far_o, slot_of(left1, o), opp_r, 1, fin_r, 3, ring1(left1))
        yield
        at = settle(f, 0, f_right, f_left)
        opp_low = mail.push(p1.at[at, low], opp2_l, ring2(right2))
        opp_high = mail.push(p1.at[at, high], opp2_r, ring2(left2))
        yield
        at_left = settle(l, 2, l_right, l_left)
        ends = [mail.push(p1.at[at_left, low], fin2_r.at[low], ring2(left2))]
        yield
        at_right = settle(r, 1, r_right, r_left)
        ends.append(mail.push(p1.at[at_right, high], fin2_l.at[high], ring2(right2)))
        yield
        opp_low.wait_recv()
        p1[at_right, low] = p1[at_right, low] + opp2_l[...]
        ends.append(mail.push(p1.at[at_right, low], fin2_l.at[low], ring2(right2)))
        opp_high.wait_recv()
        p1[at_left, high] = p1[at_left, high] + opp2_r[...]
        ends.append(mail.push(p1.at[at_left, high], fin2_r.at[high], ring2(left2)))
        yield
        at = settle(o, 3, o_right, o_left)
        yield
        for copy in ends:
            copy.wait_recv()
        finish(1, p1[at] + fin2_l[...] + fin2_r[...])

    def scatter_z():
        order = [(z + far) % ring]
        for t in range(far - 1, 0, -1):
            order += [(z + t) % ring, (z + ring - t) % ring]
        order.append(z)
        side = [mail.push(p0.at[q * CORES + 1 - c], sib.at[q], sibling) for q in order]

        def settle(n):
            side[n].wait_recv()
            at = order[n] * CORES + c
            p0[at] = p0[at] + sib[order[n]]

        def above(t):
            return (z + t) % ring

        def below(t):
            return (z + ring - t) % ring

        def part(q, cut):
            return p0.at[q * CORES + c, cut]

        def pass_on(chain, buf, cut, dest, device):
            n = len(chain) - 1
            chain[n].wait_recv()
            at = dest * CORES + c
            p0[at, cut] = p0[at, cut] + buf[n]
            chain.append(mail.push(p0.at[at, cut], buf.at[n + 1], device))

        yield
        settle(0)
        ua = [mail.push(part(above(far), low), up_a.at[0], zdev(up))]
        db = [mail.push(part(below(far), high), down_b.at[0], zdev(down))]
        settle(1)
        ub = [mail.push(part(above(far - 1), high), up_b.at[0], zdev(up))]
        settle(2)
        da = [mail.push(part(below(far - 1), low), down_a.at[0], zdev(down))]
        yield
        for n in range(3, ring):
            settle(n)
        for t in range(far - 1, 0, -1):
            yield
            pass_on(ua, up_a, low, above(t), zdev(up))
            pass_on(db, down_b, high, below(t), zdev(down))
            if t > 1:
                yield
                pass_on(ub, up_b, high, above(t - 1), zdev(up))
                pass_on(da, down_a, low, below(t - 1), zdev(down))
        yield
        for chain in (ub, da, ua, db):
            chain[-1].wait_recv()
        p0[j, low] = p0[j, low] + up_a[far - 1] + down_a[far - 2]
        p0[j, high] = p0[j, high] + up_b[far - 2] + down_b[far - 1]
        finish(0, p0[j])

    def finish(v, got):
        first = jnp.sum(got, axis=1, keepdims=True) * scale
        cross = jnp.sum(got * cent[v], axis=1, keepdims=True) * scale
        og[v, i] = (inv_std[v] * (got - first - cent[v] * cross)).astype(jnp.bfloat16)

    def loss_chain(value):
        stages = (
            (loss_x, x, [(y * SIDE + (x + d) % SIDE, j) for d in range(1, SIDE)]),
            (loss_y, y, [(((y + d) % SIDE) * SIDE + x, j) for d in range(1, SIDE)]),
            (loss_z, z, [zdev((z + d) % ring) for d in range(1, ring)]),
            (loss_c, c, [sibling]),
        )
        for buf, at, others in stages:
            buf[at] = value
            copies = [mail.push(buf.at[at], buf.at[at], device) for device in others]
            yield
            for copy in copies:
                copy.wait_recv()
            value = buf[0]
            for n in range(1, buf.shape[0]):
                value = value + buf[n]
        loss[...] = value[0:1, 0:1] / (n_mp * cols)

    second = scatter()
    run(second, 1)
    partial(p0, g_buf, t1)
    first = scatter_z()
    run(first, 1)
    score = loss_chain(jnp.broadcast_to(jnp.sum(total, axis=1, keepdims=True), (8, 128)))
    run(first, 1)
    run(score, 1)
    run(second, 1)
    run(first, 2)
    run(second, 1)
    run(score, 1)
    run(first, 2)
    run(second, 2)
    run(score, 1)
    run(first, 1)
    run(second, 1)
    run(first, 1)
    run(wanted, 1)
    run(second, 2)
    run(score, 1)
    run(first)
    out_first = gather(lambda a: og.at[0, a], index_of, 0)
    run(out_first, 1)
    run(second)
    out_second = gather(lambda a: og.at[1, a], index_of, 1)
    run(out_second, 1)
    run(out_first, 2)
    run(wanted, 1)
    run(score)
    run(out_second, 2)
    run(out_first, 2)
    run(out_second, 2)
    run(wanted, 1)
    run(out_first, 2)
    run(out_second, 2)
    run(out_first, 1)
    run(wanted, 1)
    run(out_second, 1)
    run(out_first)
    run(wanted)

    half = cols // 2

    def weigh(v, t):
        cut = pl.ds(pl.multiple_of(t * half, half), half)
        return cut, jnp.dot(
            og[v].reshape(cols, batch),
            fk[v, :, :, cut].reshape(batch, half),
            preferred_element_type=jnp.float32,
        )

    def weigh_first(t, carry):
        cut, got = weigh(0, t)
        part_buf[:, cut] = got
        return carry

    def weigh_second(t, carry):
        cut, got = weigh(1, t)
        grad[cut, :] = (got + part_buf[:, cut]).T
        return carry

    lax.fori_loop(0, 2, weigh_first, 0)
    run(out_second)
    lax.fori_loop(0, 2, weigh_second, 0)

    mail.close()


def body(n_dp, n_mp, features, weight):
    rows, depth = features.shape[1], features.shape[2]
    cols = weight.shape[1]
    batch = rows * n_dp
    sub = cols // n_dp
    ring = n_mp // CORES
    far = ring // 2
    f32, bf16 = jnp.float32, jnp.bfloat16
    V = pltpu.VMEM
    scratch = [
        V((depth, cols), bf16),
        V((2, rows, depth), bf16),
        V((2, LANES, cols), f32),
        V((2, cols, LANES), f32),
        V((n_dp, 2, sub, LANES), f32),
        V((2, sub, batch), f32),
        V((n_mp, sub, batch), bf16),
        V((n_dp, sub, batch), bf16),
        V((cols, cols), bf16),
        V((cols, cols), bf16),
        V((n_mp, sub, batch), f32),
        V((n_dp, sub, batch), f32),
        V((2, sub, batch), f32),
        V((2, sub, batch), f32),
        V((SIDE, sub, batch), f32),
        V((SIDE, sub, batch), f32),
        V((sub // 2, batch), f32),
        V((sub // 2, batch), f32),
        V((sub, batch), f32),
        V((sub, batch), f32),
        V((ring, sub, batch), f32),
        V((far, sub // 2, batch), f32),
        V((far - 1, sub // 2, batch), f32),
        V((far - 1, sub // 2, batch), f32),
        V((far, sub // 2, batch), f32),
        V((2, n_dp, sub, batch), bf16),
        V((2, n_dp, rows, cols), bf16),
        V((cols, cols), f32),
        V((SIDE, 8, 128), f32),
        V((SIDE, 8, 128), f32),
        V((ring, 8, 128), f32),
        V((CORES, 8, 128), f32),
        pltpu.SemaphoreType.DMA((MSGS,)),
        pltpu.SemaphoreType.DMA((MSGS,)),
        pltpu.SemaphoreType.DMA((17,)),
    ]
    grad, loss = pl.pallas_call(
        functools.partial(kernel, n_dp, n_mp),
        out_shape=(
            jax.ShapeDtypeStruct((cols, cols), f32),
            jax.ShapeDtypeStruct((1, 1), f32),
        ),
        in_specs=[pl.BlockSpec(memory_space=pl.ANY)] * 2,
        out_specs=(pl.BlockSpec(memory_space=V), pl.BlockSpec(memory_space=V)),
        scratch_shapes=scratch,
        compiler_params=pltpu.CompilerParams(
            collective_id=0, has_side_effects=True, vmem_limit_bytes=60 * 2**20
        ),
    )(features, weight)
    return (grad, loss.reshape(()))


def solution(mesh):
    placed = (P(None, "dp", None), P(None, "mp"))
    return jax.shard_map(
        functools.partial(body, mesh.shape["dp"], mesh.shape["mp"]),
        mesh=mesh,
        in_specs=placed,
        out_specs=(P("dp", "mp"), P()),
        check_vma=False,
    )
```

```python
import functools

import jax
import jax.numpy as jnp
from jax import lax
from jax.experimental import pallas as pl
from jax.experimental.pallas import tpu as pltpu
from jax.sharding import PartitionSpec as P

epsilon = 1e-05
off_weight = 0.0051
SIDE = 4
CORES = 2
LANES = 128
MSGS = 190
MESH = pl.DeviceIdType.MESH
OFFSETS = sorted(
    ((a, b) for a in range(SIDE) for b in range(SIDE) if a or b),
    key=lambda o: -min(o[0], SIDE - o[0]) - min(o[1], SIDE - o[1]),
)


class Mail:
    def __init__(self, send_sem, recv_sem):
        self.send_sem, self.recv_sem, self.sent = send_sem, recv_sem, []

    def push(self, src, dst, device):
        index = len(self.sent)
        copy = pltpu.make_async_remote_copy(
            src_ref=src,
            dst_ref=dst,
            send_sem=self.send_sem.at[index],
            recv_sem=self.recv_sem.at[index],
            device_id=device,
            device_id_type=MESH,
        )
        copy.start()
        self.sent.append(copy)
        return copy

    def close(self):
        for copy in self.sent:
            copy.wait_send()


def kernel(
    n_dp,
    n_mp,
    features,
    weight,
    grad,
    loss,
    w_buf,
    f_buf,
    acc,
    turned,
    arrived,
    cent,
    t0,
    t1,
    g_buf,
    gt_buf,
    p0,
    p1,
    opp_l,
    opp_r,
    fin_l,
    fin_r,
    opp2_l,
    opp2_r,
    fin2_l,
    fin2_r,
    sib,
    up_a,
    up_b,
    down_a,
    down_b,
    og,
    fk,
    part_buf,
    loss_x,
    loss_y,
    loss_z,
    loss_c,
    send_sem,
    recv_sem,
    load_sem,
):
    rows = f_buf.shape[1]
    depth, cols = w_buf.shape
    batch = rows * n_dp
    sub = cols // n_dp
    ring = n_mp // CORES
    far = ring // 2
    scale = 1.0 / batch

    i = lax.axis_index("dp")
    j = lax.axis_index("mp")
    y, x = i // SIDE, i % SIDE
    z, c = j // CORES, j % CORES
    q1 = x * (1 - c) + y * c
    q2 = y * (1 - c) + x * c
    s1 = 1 * (1 - c) + SIDE * c
    s2 = SIDE * (1 - c) + 1 * c

    def index_of(a, b):
        return a * s1 + b * s2

    def slot_of(a, b):
        return a * SIDE + b

    def ring1(q):
        return (index_of(q, q2), j)

    def ring2(q):
        return (index_of(q1, q), j)

    def zdev(q):
        return (i, q * CORES + c)

    right1, left1, far1 = (q1 + 1) % SIDE, (q1 + SIDE - 1) % SIDE, (q1 + 2) % SIDE
    right2, left2, far2 = (q2 + 1) % SIDE, (q2 + SIDE - 1) % SIDE, (q2 + 2) % SIDE
    up, down = (z + 1) % ring, (z + ring - 1) % ring
    sibling = (i, z * CORES + 1 - c)
    mail = Mail(send_sem, recv_sem)
    low, high = pl.ds(0, sub // 2), pl.ds(sub // 2, sub // 2)

    parts = 8
    step = depth // parts

    def loads(k):
        cut = pl.ds(pl.multiple_of(k * step, step), step)
        return (
            pltpu.make_async_copy(weight.at[cut, :], w_buf.at[cut, :], load_sem.at[k]),
            pltpu.make_async_copy(
                features.at[:, :, cut], f_buf.at[:, :, cut], load_sem.at[parts + k]
            ),
        )

    for k in range(parts):
        for load in loads(k):
            load.start()

    barrier = pltpu.get_barrier_semaphore()
    for d in range(1, n_dp):
        pl.semaphore_signal(barrier, inc=1, device_id=((i + d) % n_dp, j), device_id_type=MESH)
    for d in range(1, ring):
        pl.semaphore_signal(barrier, inc=1, device_id=zdev((z + d) % ring), device_id_type=MESH)
    pl.semaphore_signal(barrier, inc=1, device_id=sibling, device_id_type=MESH)

    acc[...] = jnp.zeros_like(acc)

    def project(k, carry):
        for load in loads(k):
            load.wait()
        cut = pl.ds(pl.multiple_of(k * step, step), step)
        left = f_buf[:, :, cut].reshape(2 * rows, step)
        got = jnp.dot(left, w_buf[cut, :], preferred_element_type=jnp.float32)
        acc[...] += got.reshape(2, rows, cols)
        return carry

    lax.fori_loop(0, parts, project, 0)
    spare = LANES - rows
    keep = sub * rows // LANES
    tail = sub - keep
    place = lax.broadcasted_iota(jnp.int32, (spare, cols), 1) % sub // tail
    for v in range(2):
        fill = jnp.zeros((spare, cols), jnp.float32)
        for n in range(rows // spare):
            moved = pltpu.roll(acc[v, n * spare : (n + 1) * spare, :], cols - keep + n * tail, 1)
            fill = jnp.where(place == n, moved, fill)
        turned[v] = jnp.concatenate([acc[v], fill], axis=0).T.reshape(n_dp, sub, LANES)

    pl.semaphore_wait(barrier, n_dp - 1 + ring - 1 + 1)

    def run(chain, steps=99):
        for _ in range(steps):
            if next(chain, 0) == 0:
                return

    quarters = cols // LANES

    def quarter(q):
        return pl.ds(pl.multiple_of((q % quarters) * LANES, LANES), LANES)

    def feature_cut(a):
        return pl.ds(pl.multiple_of(a * cols + (z % quarters) * LANES, LANES), LANES)

    def feature_chain():
        own = pltpu.make_async_copy(
            features.at[c, :, feature_cut(i)], fk.at[c, i, :, quarter(z)], load_sem.at[2 * parts]
        )
        own.start()
        copies = []
        for n, (dx, dy) in enumerate(OFFSETS):
            other = (y + dy) % SIDE * SIDE + (x + dx) % SIDE
            copies.append(
                mail.push(
                    features.at[c, :, feature_cut(other)], fk.at[c, i, :, quarter(z)], (other, j)
                )
            )
        yield
        own.wait()
        for copy in copies:
            copy.wait_recv()
        halves = (pl.ds(0, n_dp // 2), pl.ds(n_dp // 2, n_dp // 2))

        def send(n, q, device):
            part = fk.at[c, halves[n], :, quarter(q)]
            return mail.push(part, part, device)

        def to_side(q):
            part = fk.at[c, :, :, quarter(q)]
            return mail.push(part, part, sibling)

        ups = [send(0, z, zdev(up)), send(1, z, zdev(up))]
        downs = [send(1, z, zdev(down)), send(0, z, zdev(down))]
        side = [to_side(z)]
        yield
        ups[0].wait_recv()
        ups.append(send(0, z + ring - 1, zdev(up)))
        downs[0].wait_recv()
        downs.append(send(1, z + 1, zdev(down)))
        yield
        ups[1].wait_recv()
        side.append(to_side(z + ring - 1))
        downs[1].wait_recv()
        side.append(to_side(z + 1))
        yield
        ups[2].wait_recv()
        downs[2].wait_recv()
        side.append(to_side(z + 2))
        yield
        for copy in side:
            copy.wait_recv()

    wanted = feature_chain()

    strip_copies = ([], [])
    for v in (0, 1):
        for dx, dy in OFFSETS:
            other = (y + dy) % SIDE * SIDE + (x + dx) % SIDE
            strip_copies[v].append(
                mail.push(turned.at[v, other, pl.ds(0, keep)], arrived.at[v, i], (other, j))
            )
        arrived[v, i] = turned[v, i, 0:keep, :]
    inv_std = [None, None]

    def normalize(v):
        for copy in strip_copies[v]:
            copy.wait_recv()
        whole = jnp.concatenate([arrived[v, a][:, 0:rows] for a in range(n_dp)], axis=1)
        parts = [
            arrived[v, a][n * tail : (n + 1) * tail, rows:LANES]
            for a in range(n_dp)
            for n in range(rows // spare)
        ]
        strip = jnp.concatenate([whole, jnp.concatenate(parts, axis=1)], axis=0)
        mean = jnp.sum(strip, axis=1, keepdims=True) * scale
        shifted = strip - mean
        variance = jnp.sum(shifted * shifted, axis=1, keepdims=True) * scale
        inv_std[v] = lax.rsqrt(variance + epsilon)
        centered = shifted * inv_std[v]
        cent[v] = centered
        return centered.astype(jnp.bfloat16)

    def gather(block, at, first_flip, direct=False):
        own = block(at(q1, q2))
        ends = []

        def onward(a):
            part = block(at(a, q2))
            if direct:
                ends.append(mail.push(part, part, ring2(far2)))
            return (mail.push(part, part, ring2(right2)), mail.push(part, part, ring2(left2)))

        def across(n, a, pair):
            pair[0].wait_recv()
            pair[1].wait_recv()
            if direct:
                return
            if (n + first_flip) % 2 == 0:
                part = block(at(a, left2))
                ends.append(mail.push(part, part, ring2(right2)))
            else:
                part = block(at(a, right2))
                ends.append(mail.push(part, part, ring2(left2)))

        to_right = mail.push(own, own, ring1(right1))
        to_left = mail.push(own, own, ring1(left1))
        to_far = mail.push(own, own, ring1(far1))
        pair_own = onward(q1)
        yield
        to_right.wait_recv()
        pair_left = onward(left1)
        yield
        to_left.wait_recv()
        pair_right = onward(right1)
        yield
        across(0, q1, pair_own)
        yield
        to_far.wait_recv()
        pair_far = onward(far1)
        yield
        across(1, left1, pair_left)
        yield
        across(2, right1, pair_right)
        yield
        across(3, far1, pair_far)
        yield
        for copy in ends[:3]:
            copy.wait_recv()
        yield
        ends[3].wait_recv()

    def gather_z():
        side = []

        def block(q):
            return t0.at[q * CORES + c]

        def to_side(q):
            side.append(mail.push(block(q), block(q), sibling))

        def hop(q, cut, device):
            part = block(q).at[cut]
            return mail.push(part, part, device)

        up_low, down_high = hop(z, low, zdev(up)), hop(z, high, zdev(down))
        up_high, down_low = hop(z, high, zdev(up)), hop(z, low, zdev(down))
        to_side(z)
        for t in range(1, far):
            below, above = (z + ring - t) % ring, (z + t) % ring
            yield
            up_low.wait_recv()
            up_low = hop(below, low, zdev(up))
            down_high.wait_recv()
            down_high = hop(above, high, zdev(down))
            yield
            up_high.wait_recv()
            if t < far - 1:
                up_high = hop(below, high, zdev(up))
            down_low.wait_recv()
            if t < far - 1:
                down_low = hop(above, low, zdev(down))
            to_side(below)
            to_side(above)
        yield
        up_low.wait_recv()
        down_high.wait_recv()
        to_side((z + far) % ring)
        yield
        for copy in side:
            copy.wait_recv()

    rows_of_second = gather(lambda a: t1.at[a], slot_of, 0, direct=True)
    rows_of_first = gather_z()
    t0[j] = normalize(0)
    run(rows_of_first, 1)
    t1[slot_of(q1, q2)] = normalize(1)
    run(rows_of_second, 1)
    run(rows_of_first, 2)
    run(rows_of_second, 2)
    run(rows_of_first, 1)
    run(rows_of_second, 2)
    run(rows_of_first, 1)
    run(rows_of_second, 1)
    run(rows_of_first, 1)
    run(rows_of_second, 1)
    run(rows_of_first, 1)
    run(rows_of_second, 1)
    run(rows_of_first, 1)
    run(rows_of_second)
    run(rows_of_first)
    run(wanted, 1)

    tile = 256

    def correlate(t, total):
        per = tile // sub
        left = t0[pl.ds(t * per, per)].reshape(tile, batch)
        corr = lax.dot_general(
            left, t1[...].reshape(cols, batch), (((1,), (1,)), ((), ())),
            preferred_element_type=jnp.float32,
        ) * scale
        r = t * tile + lax.broadcasted_iota(jnp.int32, (tile, cols), 0)
        where_diagonal = jnp.where(r // sub == j, slot_of(q1, q2) * sub + r % sub, -1)
        on_diagonal = where_diagonal == lax.broadcasted_iota(jnp.int32, (tile, cols), 1)
        gap = corr - 1.0
        terms = jnp.where(on_diagonal, gap * gap, off_weight * corr * corr)
        g = jnp.where(on_diagonal, 2.0 * gap, 2.0 * off_weight * corr)
        g_buf[pl.ds(pl.multiple_of(t * tile, tile), tile), :] = g.astype(jnp.bfloat16)
        gt_buf[:, pl.ds(pl.multiple_of(t * tile, tile), tile)] = g.T.astype(jnp.bfloat16)
        return total + jnp.sum(terms, axis=0, keepdims=True)

    total = lax.fori_loop(0, cols // tile, correlate, jnp.zeros((1, cols), jnp.float32))

    wide = batch // 3

    def partial(into, left, right):
        def one(t, carry):
            cut = pl.ds(pl.multiple_of(t * wide, wide), wide)
            got = jnp.dot(
                left[...], right[:, :, cut].reshape(cols, wide), preferred_element_type=jnp.float32
            )
            into[:, :, cut] = (got * scale).reshape(n_dp, sub, wide)
            return carry

        lax.fori_loop(0, batch // wide, one, 0)

    def partial_line(q):
        cut = pl.ds(pl.multiple_of(q * (cols // SIDE), cols // SIDE), cols // SIDE)
        got = jnp.dot(
            gt_buf[cut, :], t0[...].reshape(cols, batch), preferred_element_type=jnp.float32
        )
        p1[pl.ds(q * SIDE, SIDE)] = (got * scale).reshape(SIDE, sub, batch)

    def scatter():
        f, r, l, o = far2, right2, left2, q2
        partial_line(far1)
        far_f = mail.push(p1.at[slot_of(far1, f)], opp_l.at[0], ring1(right1))
        far_l = mail.push(p1.at[slot_of(far1, l)], opp_r.at[0], ring1(left1))
        far_r = mail.push(p1.at[slot_of(far1, r)], opp_l.at[1], ring1(right1))
        far_o = mail.push(p1.at[slot_of(far1, o)], opp_r.at[1], ring1(left1))
        yield
        partial_line(right1)
        l_right = mail.push(p1.at[slot_of(right1, l)], fin_l.at[2], ring1(right1))
        partial_line(left1)
        f_left = mail.push(p1.at[slot_of(left1, f)], fin_r.at[0], ring1(left1))

        def onward(copy, at, buf, n, into, m, device):
            copy.wait_recv()
            p1[at] = p1[at] + buf[n]
            return mail.push(p1.at[at], into.at[m], device)

        def settle(n, m, one, two):
            one.wait_recv()
            two.wait_recv()
            at = slot_of(q1, n)
            p1[at] = p1[at] + fin_l[m] + fin_r[m]
            return at

        partial_line(q1)
        yield
        f_right = onward(far_f, slot_of(right1, f), opp_l, 0, fin_l, 0, ring1(right1))
        l_left = onward(far_l, slot_of(left1, l), opp_r, 0, fin_r, 2, ring1(left1))
        r_left = mail.push(p1.at[slot_of(left1, r)], fin_r.at[1], ring1(left1))
        yield
        r_right = onward(far_r, slot_of(right1, r), opp_l, 1, fin_l, 1, ring1(right1))
        o_right = mail.push(p1.at[slot_of(right1, o)], fin_l.at[3], ring1(right1))
        o_left = onward(far_o, slot_of(left1, o), opp_r, 1, fin_r, 3, ring1(left1))
        yield
        at = settle(f, 0, f_right, f_left)
        opp_low = mail.push(p1.at[at, low], opp2_l, ring2(right2))
        opp_high = mail.push(p1.at[at, high], opp2_r, ring2(left2))
        yield
        at_left = settle(l, 2, l_right, l_left)
        ends = [mail.push(p1.at[at_left, low], fin2_r.at[low], ring2(left2))]
        yield
        at_right = settle(r, 1, r_right, r_left)
        ends.append(mail.push(p1.at[at_right, high], fin2_l.at[high], ring2(right2)))
        yield
        opp_low.wait_recv()
        p1[at_right, low] = p1[at_right, low] + opp2_l[...]
        ends.append(mail.push(p1.at[at_right, low], fin2_l.at[low], ring2(right2)))
        opp_high.wait_recv()
        p1[at_left, high] = p1[at_left, high] + opp2_r[...]
        ends.append(mail.push(p1.at[at_left, high], fin2_r.at[high], ring2(left2)))
        yield
        at = settle(o, 3, o_right, o_left)
        yield
        for copy in ends:
            copy.wait_recv()
        finish(1, p1[at] + fin2_l[...] + fin2_r[...])

    def scatter_z():
        order = [(z + far) % ring]
        for t in range(far - 1, 0, -1):
            order += [(z + t) % ring, (z + ring - t) % ring]
        order.append(z)
        side = [mail.push(p0.at[q * CORES + 1 - c], sib.at[q], sibling) for q in order]

        def settle(n):
            side[n].wait_recv()
            at = order[n] * CORES + c
            p0[at] = p0[at] + sib[order[n]]

        def above(t):
            return (z + t) % ring

        def below(t):
            return (z + ring - t) % ring

        def part(q, cut):
            return p0.at[q * CORES + c, cut]

        def pass_on(chain, buf, cut, dest, device):
            n = len(chain) - 1
            chain[n].wait_recv()
            at = dest * CORES + c
            p0[at, cut] = p0[at, cut] + buf[n]
            chain.append(mail.push(p0.at[at, cut], buf.at[n + 1], device))

        yield
        settle(0)
        ua = [mail.push(part(above(far), low), up_a.at[0], zdev(up))]
        db = [mail.push(part(below(far), high), down_b.at[0], zdev(down))]
        settle(1)
        ub = [mail.push(part(above(far - 1), high), up_b.at[0], zdev(up))]
        settle(2)
        da = [mail.push(part(below(far - 1), low), down_a.at[0], zdev(down))]
        yield
        for n in range(3, ring):
            settle(n)
        for t in range(far - 1, 0, -1):
            yield
            pass_on(ua, up_a, low, above(t), zdev(up))
            pass_on(db, down_b, high, below(t), zdev(down))
            if t > 1:
                yield
                pass_on(ub, up_b, high, above(t - 1), zdev(up))
                pass_on(da, down_a, low, below(t - 1), zdev(down))
        yield
        for chain in (ub, da, ua, db):
            chain[-1].wait_recv()
        p0[j, low] = p0[j, low] + up_a[far - 1] + down_a[far - 2]
        p0[j, high] = p0[j, high] + up_b[far - 2] + down_b[far - 1]
        finish(0, p0[j])

    def finish(v, got):
        first = jnp.sum(got, axis=1, keepdims=True) * scale
        cross = jnp.sum(got * cent[v], axis=1, keepdims=True) * scale
        og[v, i] = (inv_std[v] * (got - first - cent[v] * cross)).astype(jnp.bfloat16)

    half = cols // 2

    def weigh_first(t, carry):
        cut = pl.ds(pl.multiple_of(t * half, half), half)
        got = jnp.dot(
            og[0].reshape(cols, batch),
            fk[0, :, :, cut].reshape(batch, half),
            preferred_element_type=jnp.float32,
        )
        part_buf[:, :, cut] = got.reshape(n_dp, sub, half)
        return carry

    def weigh(v, lines):
        places = [index_of(q, n) for q in lines for n in range(SIDE)]

        def one(t, carry):
            cut = pl.ds(pl.multiple_of(t * half, half), half)
            got = jnp.dot(
                jnp.concatenate([og[v, a] for a in places], axis=0),
                fk[v, :, :, cut].reshape(batch, half),
                preferred_element_type=jnp.float32,
            )
            for n, a in enumerate(places):
                part_buf[a, :, cut] += got[n * sub : (n + 1) * sub]
            return carry

        lax.fori_loop(0, 2, one, 0)

    def loss_chain(value):
        stages = (
            (loss_x, x, [(y * SIDE + (x + d) % SIDE, j) for d in range(1, SIDE)]),
            (loss_y, y, [(((y + d) % SIDE) * SIDE + x, j) for d in range(1, SIDE)]),
            (loss_z, z, [zdev((z + d) % ring) for d in range(1, ring)]),
            (loss_c, c, [sibling]),
        )
        for buf, at, others in stages:
            buf[at] = value
            copies = [mail.push(buf.at[at], buf.at[at], device) for device in others]
            yield
            for copy in copies:
                copy.wait_recv()
            value = buf[0]
            for n in range(1, buf.shape[0]):
                value = value + buf[n]
        loss[...] = value[0:1, 0:1] / (n_mp * cols)

    second = scatter()
    run(second, 1)
    partial(p0, g_buf, t1)
    first = scatter_z()
    run(first, 1)
    score = loss_chain(jnp.broadcast_to(jnp.sum(total, axis=1, keepdims=True), (8, 128)))
    run(second, 1)
    run(first, 1)
    run(score, 1)
    run(second, 1)
    run(first, 2)
    run(second, 1)
    run(first, 2)
    run(second, 1)
    run(first, 1)
    run(second, 1)
    run(first, 1)
    run(second, 1)
    run(score, 1)
    run(second, 1)
    run(first)
    out_first = gather(lambda a: og.at[0, a], index_of, 0)
    run(out_first, 1)
    run(second)
    out_second = gather(lambda a: og.at[1, a], index_of, 1)
    run(out_second, 1)
    run(score, 1)
    run(wanted, 1)
    run(out_first, 2)
    run(out_second, 1)
    run(out_first, 2)
    run(out_second, 1)
    run(wanted, 1)
    run(out_first, 1)
    run(out_second, 2)
    run(out_first, 1)
    run(wanted, 1)
    run(out_second, 2)
    run(out_first, 1)
    run(wanted, 1)
    run(out_second, 1)
    run(wanted)
    run(score)
    run(out_first)
    lax.fori_loop(0, 2, weigh_first, 0)
    run(out_second, 1)
    weigh(1, (q1, left1, right1))

    run(out_second)
    weigh(1, (far1,))

    def hand_over(t, carry):
        cut = pl.ds(pl.multiple_of(t * half, half), half)
        grad[cut, :] = part_buf[:, :, cut].reshape(cols, half).T
        return carry

    lax.fori_loop(0, 2, hand_over, 0)

    mail.close()


def body(n_dp, n_mp, features, weight):
    rows, depth = features.shape[1], features.shape[2]
    cols = weight.shape[1]
    batch = rows * n_dp
    sub = cols // n_dp
    ring = n_mp // CORES
    far = ring // 2
    f32, bf16 = jnp.float32, jnp.bfloat16
    V = pltpu.VMEM
    scratch = [
        V((depth, cols), bf16),
        V((2, rows, depth), bf16),
        V((2, rows, cols), f32),
        V((2, n_dp, sub, LANES), f32),
        V((2, n_dp, sub * rows // LANES, LANES), f32),
        V((2, sub, batch), f32),
        V((n_mp, sub, batch), bf16),
        V((n_dp, sub, batch), bf16),
        V((cols, cols), bf16),
        V((cols, cols), bf16),
        V((n_mp, sub, batch), f32),
        V((n_dp, sub, batch), f32),
        V((2, sub, batch), f32),
        V((2, sub, batch), f32),
        V((SIDE, sub, batch), f32),
        V((SIDE, sub, batch), f32),
        V((sub // 2, batch), f32),
        V((sub // 2, batch), f32),
        V((sub, batch), f32),
        V((sub, batch), f32),
        V((ring, sub, batch), f32),
        V((far, sub // 2, batch), f32),
        V((far - 1, sub // 2, batch), f32),
        V((far - 1, sub // 2, batch), f32),
        V((far, sub // 2, batch), f32),
        V((2, n_dp, sub, batch), bf16),
        V((2, n_dp, rows, cols), bf16),
        V((n_dp, sub, cols), f32),
        V((SIDE, 8, 128), f32),
        V((SIDE, 8, 128), f32),
        V((ring, 8, 128), f32),
        V((CORES, 8, 128), f32),
        pltpu.SemaphoreType.DMA((MSGS,)),
        pltpu.SemaphoreType.DMA((MSGS,)),
        pltpu.SemaphoreType.DMA((17,)),
    ]
    grad, loss = pl.pallas_call(
        functools.partial(kernel, n_dp, n_mp),
        out_shape=(
            jax.ShapeDtypeStruct((cols, cols), f32),
            jax.ShapeDtypeStruct((1, 1), f32),
        ),
        in_specs=[pl.BlockSpec(memory_space=pl.ANY)] * 2,
        out_specs=(pl.BlockSpec(memory_space=V), pl.BlockSpec(memory_space=V)),
        scratch_shapes=scratch,
        compiler_params=pltpu.CompilerParams(
            collective_id=0, has_side_effects=True, vmem_limit_bytes=60 * 2**20
        ),
    )(features, weight)
    return (grad, loss.reshape(()))


def solution(mesh):
    placed = (P(None, "dp", None), P(None, "mp"))
    return jax.shard_map(
        functools.partial(body, mesh.shape["dp"], mesh.shape["mp"]),
        mesh=mesh,
        in_specs=placed,
        out_specs=(P("dp", "mp"), P()),
        check_vma=False,
    )
```

```python
import functools

import jax
import jax.numpy as jnp
from jax import lax
from jax.experimental import pallas as pl
from jax.experimental.pallas import tpu as pltpu
from jax.sharding import PartitionSpec as P

epsilon = 1e-05
off_weight = 0.0051
SIDE = 4
CORES = 2
LANES = 128
MSGS = 190
WHOLE, HALF = 12, 20
MESH = pl.DeviceIdType.MESH
OFFSETS = sorted(
    ((a, b) for a in range(SIDE) for b in range(SIDE) if a or b),
    key=lambda o: -min(o[0], SIDE - o[0]) - min(o[1], SIDE - o[1]),
)


class Mail:
    def __init__(self, send_sem, recv_sem):
        self.send_sem, self.recv_sem, self.sent = send_sem, recv_sem, []

    def push(self, src, dst, device):
        index = len(self.sent)
        copy = pltpu.make_async_remote_copy(
            src_ref=src,
            dst_ref=dst,
            send_sem=self.send_sem.at[index],
            recv_sem=self.recv_sem.at[index],
            device_id=device,
            device_id_type=MESH,
        )
        copy.start()
        self.sent.append(copy)
        return copy

    def close(self):
        for copy in self.sent:
            copy.wait_send()


def kernel(
    n_dp,
    n_mp,
    features,
    weight,
    grad,
    loss,
    w_buf,
    f_buf,
    acc,
    turned,
    arrived,
    cent,
    t0,
    t1,
    g_buf,
    gt_buf,
    p0,
    p1,
    whole_out,
    whole_in,
    half_out,
    half_in,
    sib,
    og,
    fk,
    part_buf,
    loss_x,
    loss_y,
    loss_z,
    loss_c,
    send_sem,
    recv_sem,
    load_sem,
):
    rows = f_buf.shape[1]
    depth, cols = w_buf.shape
    batch = rows * n_dp
    sub = cols // n_dp
    ring = n_mp // CORES
    far = ring // 2
    scale = 1.0 / batch

    i = lax.axis_index("dp")
    j = lax.axis_index("mp")
    y, x = i // SIDE, i % SIDE
    z, c = j // CORES, j % CORES
    q1 = x * (1 - c) + y * c
    q2 = y * (1 - c) + x * c
    s1 = 1 * (1 - c) + SIDE * c
    s2 = SIDE * (1 - c) + 1 * c

    def index_of(a, b):
        return a * s1 + b * s2

    def slot_of(a, b):
        return a * SIDE + b

    def ring1(q):
        return (index_of(q, q2), j)

    def ring2(q):
        return (index_of(q1, q), j)

    def zdev(q):
        return (i, q * CORES + c)

    right1, left1, far1 = (q1 + 1) % SIDE, (q1 + SIDE - 1) % SIDE, (q1 + 2) % SIDE
    right2, left2, far2 = (q2 + 1) % SIDE, (q2 + SIDE - 1) % SIDE, (q2 + 2) % SIDE
    up, down = (z + 1) % ring, (z + ring - 1) % ring
    sibling = (i, z * CORES + 1 - c)
    mail = Mail(send_sem, recv_sem)
    low, high = pl.ds(0, sub // 2), pl.ds(sub // 2, sub // 2)

    parts = 8
    step = depth // parts

    def loads(k):
        cut = pl.ds(pl.multiple_of(k * step, step), step)
        return (
            pltpu.make_async_copy(weight.at[cut, :], w_buf.at[cut, :], load_sem.at[k]),
            pltpu.make_async_copy(
                features.at[:, :, cut], f_buf.at[:, :, cut], load_sem.at[parts + k]
            ),
        )

    for k in range(parts):
        for load in loads(k):
            load.start()

    barrier = pltpu.get_barrier_semaphore()
    for d in range(1, n_dp):
        pl.semaphore_signal(barrier, inc=1, device_id=((i + d) % n_dp, j), device_id_type=MESH)
    for d in range(1, ring):
        pl.semaphore_signal(barrier, inc=1, device_id=zdev((z + d) % ring), device_id_type=MESH)
    pl.semaphore_signal(barrier, inc=1, device_id=sibling, device_id_type=MESH)

    acc[...] = jnp.zeros_like(acc)

    def project(k, carry):
        for load in loads(k):
            load.wait()
        cut = pl.ds(pl.multiple_of(k * step, step), step)
        left = f_buf[:, :, cut].reshape(2 * rows, step)
        got = jnp.dot(left, w_buf[cut, :], preferred_element_type=jnp.float32)
        acc[...] += got.reshape(2, rows, cols)
        return carry

    lax.fori_loop(0, parts, project, 0)
    spare = LANES - rows
    keep = sub * rows // LANES
    tail = sub - keep
    place = lax.broadcasted_iota(jnp.int32, (spare, cols), 1) % sub // tail
    for v in range(2):
        fill = jnp.zeros((spare, cols), jnp.float32)
        for n in range(rows // spare):
            moved = pltpu.roll(acc[v, n * spare : (n + 1) * spare, :], cols - keep + n * tail, 1)
            fill = jnp.where(place == n, moved, fill)
        turned[v] = jnp.concatenate([acc[v], fill], axis=0).T.reshape(n_dp, sub, LANES)

    pl.semaphore_wait(barrier, n_dp - 1 + ring - 1 + 1)

    def run(chain, steps=99):
        for _ in range(steps):
            if next(chain, 0) == 0:
                return

    quarters = cols // LANES

    def quarter(q):
        return pl.ds(pl.multiple_of((q % quarters) * LANES, LANES), LANES)

    def feature_cut(a):
        return pl.ds(pl.multiple_of(a * cols + (z % quarters) * LANES, LANES), LANES)

    def feature_chain():
        own = pltpu.make_async_copy(
            features.at[c, :, feature_cut(i)], fk.at[c, i, :, quarter(z)], load_sem.at[2 * parts]
        )
        own.start()
        copies = []
        for n, (dx, dy) in enumerate(OFFSETS):
            other = (y + dy) % SIDE * SIDE + (x + dx) % SIDE
            copies.append(
                mail.push(
                    features.at[c, :, feature_cut(other)], fk.at[c, i, :, quarter(z)], (other, j)
                )
            )
        yield
        own.wait()
        for copy in copies:
            copy.wait_recv()
        halves = (pl.ds(0, n_dp // 2), pl.ds(n_dp // 2, n_dp // 2))

        def send(n, q, device):
            part = fk.at[c, halves[n], :, quarter(q)]
            return mail.push(part, part, device)

        def to_side(q):
            part = fk.at[c, :, :, quarter(q)]
            return mail.push(part, part, sibling)

        ups = [send(0, z, zdev(up)), send(1, z, zdev(up))]
        downs = [send(1, z, zdev(down)), send(0, z, zdev(down))]
        side = [to_side(z)]
        yield
        ups[0].wait_recv()
        ups.append(send(0, z + ring - 1, zdev(up)))
        downs[0].wait_recv()
        downs.append(send(1, z + 1, zdev(down)))
        yield
        ups[1].wait_recv()
        side.append(to_side(z + ring - 1))
        downs[1].wait_recv()
        side.append(to_side(z + 1))
        yield
        ups[2].wait_recv()
        downs[2].wait_recv()
        side.append(to_side(z + 2))
        yield
        for copy in side:
            copy.wait_recv()

    wanted = feature_chain()

    strip_copies = ([], [])
    for v in (0, 1):
        for dx, dy in OFFSETS:
            other = (y + dy) % SIDE * SIDE + (x + dx) % SIDE
            strip_copies[v].append(
                mail.push(turned.at[v, other, pl.ds(0, keep)], arrived.at[v, i], (other, j))
            )
        arrived[v, i] = turned[v, i, 0:keep, :]
    inv_std = [None, None]

    def normalize(v):
        for copy in strip_copies[v]:
            copy.wait_recv()
        whole = jnp.concatenate([arrived[v, a][:, 0:rows] for a in range(n_dp)], axis=1)
        parts = [
            arrived[v, a][n * tail : (n + 1) * tail, rows:LANES]
            for a in range(n_dp)
            for n in range(rows // spare)
        ]
        strip = jnp.concatenate([whole, jnp.concatenate(parts, axis=1)], axis=0)
        mean = jnp.sum(strip, axis=1, keepdims=True) * scale
        shifted = strip - mean
        variance = jnp.sum(shifted * shifted, axis=1, keepdims=True) * scale
        inv_std[v] = lax.rsqrt(variance + epsilon)
        centered = shifted * inv_std[v]
        cent[v] = centered
        return centered.astype(jnp.bfloat16)

    def gather(block, at, first_flip, direct=False):
        own = block(at(q1, q2))
        ends = []

        def onward(a):
            part = block(at(a, q2))
            if direct:
                ends.append(mail.push(part, part, ring2(far2)))
            return (mail.push(part, part, ring2(right2)), mail.push(part, part, ring2(left2)))

        def across(n, a, pair):
            pair[0].wait_recv()
            pair[1].wait_recv()
            if direct:
                return
            if (n + first_flip) % 2 == 0:
                part = block(at(a, left2))
                ends.append(mail.push(part, part, ring2(right2)))
            else:
                part = block(at(a, right2))
                ends.append(mail.push(part, part, ring2(left2)))

        to_right = mail.push(own, own, ring1(right1))
        to_left = mail.push(own, own, ring1(left1))
        to_far = mail.push(own, own, ring1(far1))
        pair_own = onward(q1)
        yield
        to_right.wait_recv()
        pair_left = onward(left1)
        yield
        to_left.wait_recv()
        pair_right = onward(right1)
        yield
        across(0, q1, pair_own)
        yield
        to_far.wait_recv()
        pair_far = onward(far1)
        yield
        across(1, left1, pair_left)
        yield
        across(2, right1, pair_right)
        yield
        across(3, far1, pair_far)
        yield
        for copy in ends[:3]:
            copy.wait_recv()
        yield
        ends[3].wait_recv()

    def gather_z():
        side = []

        def block(q):
            return t0.at[q * CORES + c]

        def to_side(q):
            side.append(mail.push(block(q), block(q), sibling))

        def hop(q, cut, device):
            part = block(q).at[cut]
            return mail.push(part, part, device)

        up_low, down_high = hop(z, low, zdev(up)), hop(z, high, zdev(down))
        up_high, down_low = hop(z, high, zdev(up)), hop(z, low, zdev(down))
        to_side(z)
        for t in range(1, far):
            below, above = (z + ring - t) % ring, (z + t) % ring
            yield
            up_low.wait_recv()
            up_low = hop(below, low, zdev(up))
            down_high.wait_recv()
            down_high = hop(above, high, zdev(down))
            yield
            up_high.wait_recv()
            if t < far - 1:
                up_high = hop(below, high, zdev(up))
            down_low.wait_recv()
            if t < far - 1:
                down_low = hop(above, low, zdev(down))
            to_side(below)
            to_side(above)
        yield
        up_low.wait_recv()
        down_high.wait_recv()
        to_side((z + far) % ring)
        yield
        for copy in side:
            copy.wait_recv()

    rows_of_second = gather(lambda a: t1.at[a], slot_of, 0, direct=True)
    rows_of_first = gather_z()
    t0[j] = normalize(0)
    run(rows_of_first, 1)
    t1[slot_of(q1, q2)] = normalize(1)
    run(rows_of_second, 1)
    run(rows_of_first, 2)
    run(rows_of_second, 2)
    run(rows_of_first, 1)
    run(rows_of_second, 2)
    run(rows_of_first, 1)
    run(rows_of_second, 1)
    run(rows_of_first, 1)
    run(rows_of_second, 1)
    run(rows_of_first, 1)
    run(rows_of_second, 1)
    run(rows_of_first, 1)
    run(rows_of_second)
    run(rows_of_first)
    run(wanted, 1)

    tile = 256

    def correlate(t, total):
        per = tile // sub
        left = t0[pl.ds(t * per, per)].reshape(tile, batch)
        corr = lax.dot_general(
            left, t1[...].reshape(cols, batch), (((1,), (1,)), ((), ())),
            preferred_element_type=jnp.float32,
        ) * scale
        r = t * tile + lax.broadcasted_iota(jnp.int32, (tile, cols), 0)
        where_diagonal = jnp.where(r // sub == j, slot_of(q1, q2) * sub + r % sub, -1)
        on_diagonal = where_diagonal == lax.broadcasted_iota(jnp.int32, (tile, cols), 1)
        gap = corr - 1.0
        terms = jnp.where(on_diagonal, gap * gap, off_weight * corr * corr)
        g = jnp.where(on_diagonal, 2.0 * gap, 2.0 * off_weight * corr)
        g_buf[pl.ds(pl.multiple_of(t * tile, tile), tile), :] = g.astype(jnp.bfloat16)
        gt_buf[:, pl.ds(pl.multiple_of(t * tile, tile), tile)] = g.T.astype(jnp.bfloat16)
        return total + jnp.sum(terms, axis=0, keepdims=True)

    total = lax.fori_loop(0, cols // tile, correlate, jnp.zeros((1, cols), jnp.float32))

    wide = batch // 3

    def partial(into, left, right):
        def one(t, carry):
            cut = pl.ds(pl.multiple_of(t * wide, wide), wide)
            got = jnp.dot(
                left[...], right[:, :, cut].reshape(cols, wide), preferred_element_type=jnp.float32
            )
            got = (got * scale).reshape(n_dp, sub // 8, 8, wide)
            for n in range(wide // LANES):
                into[:, :, t * (wide // LANES) + n] = got[..., n * LANES : (n + 1) * LANES]
            return carry

        lax.fori_loop(0, batch // wide, one, 0)

    def partial_line(q):
        cut = pl.ds(pl.multiple_of(q * (cols // SIDE), cols // SIDE), cols // SIDE)
        got = jnp.dot(
            gt_buf[cut, :], t0[...].reshape(cols, batch), preferred_element_type=jnp.float32
        )
        got = (got * scale).reshape(SIDE, sub // 8, 8, batch)
        for n in range(batch // LANES):
            p1[pl.ds(q * SIDE, SIDE), :, n] = got[..., n * LANES : (n + 1) * LANES]

    third = batch // LANES // 3
    level = 32768.0

    def pack(value):
        groups = value.shape[0]
        largest = jnp.max(jnp.max(jnp.abs(value), axis=1, keepdims=True), axis=3, keepdims=True)
        largest = jnp.maximum(largest, 1e-30)
        whole = jnp.floor(value * ((level - 2.0) / largest) + (level + 0.5))
        one, two, three = (whole[:, n * third : (n + 1) * third] for n in range(3))
        upper = jnp.floor(two * (1.0 / 256.0))
        words = jnp.concatenate(
            [one * 256.0 + upper, three * 256.0 + (two - upper * 256.0)], axis=1
        ).reshape(groups * 2 * third, 8, LANES)
        lane = lax.broadcasted_iota(jnp.int32, (8, LANES), 1)
        steps = jnp.zeros((8, LANES), jnp.float32)
        for n in range(groups):
            steps = jnp.where(lane == n, largest[n, 0] * (1.0 / (level - 2.0)), steps)
        return jnp.concatenate([words, steps[None]], axis=0)

    def unpack(words, groups):
        tiles = words[: groups * 2 * third].reshape(groups, 2 * third, 8, LANES)
        first, second = tiles[:, :third], tiles[:, third:]
        one, three = jnp.floor(first * (1.0 / 256.0)), jnp.floor(second * (1.0 / 256.0))
        two = (first - one * 256.0) * 256.0 + (second - three * 256.0)
        steps = words[groups * 2 * third]
        step = jnp.stack([steps[:, n : n + 1] for n in range(groups)])[:, None]
        return (jnp.concatenate([one, two, three], axis=1) - level) * step

    used = {sub // 8: 0, sub // 16: 0}

    def post(value, device):
        groups = value.shape[0]
        outs, ins = (whole_out, whole_in) if groups == sub // 8 else (half_out, half_in)
        n = used[groups]
        used[groups] += 1
        outs[n] = pack(value)
        return mail.push(outs.at[n], ins.at[n], device), ins, n, groups

    def take(message):
        copy, ins, n, groups = message
        copy.wait_recv()
        return unpack(ins[n], groups)

    low_part, high_part = pl.ds(0, sub // 16), pl.ds(sub // 16, sub // 16)

    def scatter():
        f, r, l, o = far2, right2, left2, q2
        partial_line(far1)
        far_f = post(p1[slot_of(far1, f)], ring1(right1))
        far_l = post(p1[slot_of(far1, l)], ring1(left1))
        far_r = post(p1[slot_of(far1, r)], ring1(right1))
        far_o = post(p1[slot_of(far1, o)], ring1(left1))
        yield
        partial_line(right1)
        l_right = post(p1[slot_of(right1, l)], ring1(right1))
        partial_line(left1)
        f_left = post(p1[slot_of(left1, f)], ring1(left1))

        def onward(message, at, device):
            return post(p1[at] + take(message), device)

        def settle(n, one, two):
            at = slot_of(q1, n)
            p1[at] = p1[at] + take(one) + take(two)
            return at

        partial_line(q1)
        yield
        f_right = onward(far_f, slot_of(right1, f), ring1(right1))
        l_left = onward(far_l, slot_of(left1, l), ring1(left1))
        r_left = post(p1[slot_of(left1, r)], ring1(left1))
        yield
        r_right = onward(far_r, slot_of(right1, r), ring1(right1))
        o_right = post(p1[slot_of(right1, o)], ring1(right1))
        o_left = onward(far_o, slot_of(left1, o), ring1(left1))
        yield
        at = settle(f, f_right, f_left)
        opp_low = post(p1[at, low_part], ring2(right2))
        opp_high = post(p1[at, high_part], ring2(left2))
        yield
        at_left = settle(l, l_right, l_left)
        lows = [post(p1[at_left, low_part], ring2(left2))]
        yield
        at_right = settle(r, r_right, r_left)
        highs = [post(p1[at_right, high_part], ring2(right2))]
        yield
        lows.append(post(p1[at_right, low_part] + take(opp_low), ring2(right2)))
        highs.append(post(p1[at_left, high_part] + take(opp_high), ring2(left2)))
        yield
        at = settle(o, o_right, o_left)
        yield
        total_low = p1[at, low_part] + take(lows[0]) + take(lows[1])
        total_high = p1[at, high_part] + take(highs[0]) + take(highs[1])
        finish(1, jnp.concatenate([total_low, total_high], axis=0))

    def scatter_z():
        order = [(z + far) % ring]
        for t in range(far - 1, 0, -1):
            order += [(z + t) % ring, (z + ring - t) % ring]
        order.append(z)
        side = [mail.push(p0.at[q * CORES + 1 - c], sib.at[q], sibling) for q in order]

        def settle(n):
            side[n].wait_recv()
            at = order[n] * CORES + c
            p0[at] = p0[at] + sib[order[n]]

        def above(t):
            return (z + t) % ring

        def below(t):
            return (z + ring - t) % ring

        def part(q, cut):
            return p0[q * CORES + c, cut]

        def pass_on(message, cut, dest, device):
            return post(part(dest, cut) + take(message), device)

        yield
        settle(0)
        ua = post(part(above(far), low_part), zdev(up))
        db = post(part(below(far), high_part), zdev(down))
        settle(1)
        ub = post(part(above(far - 1), high_part), zdev(up))
        settle(2)
        da = post(part(below(far - 1), low_part), zdev(down))
        yield
        for n in range(3, ring):
            settle(n)
        for t in range(far - 1, 0, -1):
            yield
            ua = pass_on(ua, low_part, above(t), zdev(up))
            db = pass_on(db, high_part, below(t), zdev(down))
            if t > 1:
                yield
                ub = pass_on(ub, high_part, above(t - 1), zdev(up))
                da = pass_on(da, low_part, below(t - 1), zdev(down))
        yield
        total_high = part(z, high_part) + take(ub)
        total_low = part(z, low_part) + take(da)
        total_low = total_low + take(ua)
        total_high = total_high + take(db)
        finish(0, jnp.concatenate([total_low, total_high], axis=0))

    def finish(v, tiles):
        got = jnp.concatenate(
            [
                jnp.concatenate([tiles[g, n] for n in range(batch // LANES)], axis=1)
                for g in range(sub // 8)
            ],
            axis=0,
        )
        first = jnp.sum(got, axis=1, keepdims=True) * scale
        cross = jnp.sum(got * cent[v], axis=1, keepdims=True) * scale
        og[v, i] = (inv_std[v] * (got - first - cent[v] * cross)).astype(jnp.bfloat16)

    half = cols // 2

    def weigh_first(t, carry):
        cut = pl.ds(pl.multiple_of(t * half, half), half)
        got = jnp.dot(
            og[0].reshape(cols, batch),
            fk[0, :, :, cut].reshape(batch, half),
            preferred_element_type=jnp.float32,
        )
        part_buf[:, :, cut] = got.reshape(n_dp, sub, half)
        return carry

    def weigh(v, lines):
        places = [index_of(q, n) for q in lines for n in range(SIDE)]

        def one(t, carry):
            cut = pl.ds(pl.multiple_of(t * half, half), half)
            got = jnp.dot(
                jnp.concatenate([og[v, a] for a in places], axis=0),
                fk[v, :, :, cut].reshape(batch, half),
                preferred_element_type=jnp.float32,
            )
            for n, a in enumerate(places):
                part_buf[a, :, cut] += got[n * sub : (n + 1) * sub]
            return carry

        lax.fori_loop(0, 2, one, 0)

    def loss_chain(value):
        stages = (
            (loss_x, x, [(y * SIDE + (x + d) % SIDE, j) for d in range(1, SIDE)]),
            (loss_y, y, [(((y + d) % SIDE) * SIDE + x, j) for d in range(1, SIDE)]),
            (loss_z, z, [zdev((z + d) % ring) for d in range(1, ring)]),
            (loss_c, c, [sibling]),
        )
        for buf, at, others in stages:
            buf[at] = value
            copies = [mail.push(buf.at[at], buf.at[at], device) for device in others]
            yield
            for copy in copies:
                copy.wait_recv()
            value = buf[0]
            for n in range(1, buf.shape[0]):
                value = value + buf[n]
        loss[...] = value[0:1, 0:1] / (n_mp * cols)

    second = scatter()
    run(second, 1)
    partial(p0, g_buf, t1)
    first = scatter_z()
    run(first, 1)
    score = loss_chain(jnp.broadcast_to(jnp.sum(total, axis=1, keepdims=True), (8, 128)))
    run(second, 1)
    run(first, 1)
    run(score, 1)
    run(second, 1)
    run(first, 2)
    run(second, 1)
    run(first, 2)
    run(second, 2)
    run(first, 1)
    run(second, 1)
    run(first, 1)
    run(second, 1)
    run(score, 1)
    run(first)
    out_first = gather(lambda a: og.at[0, a], index_of, 0)
    run(out_first, 1)
    run(second)
    out_second = gather(lambda a: og.at[1, a], index_of, 1)
    run(out_second, 1)
    run(score, 1)
    run(wanted, 1)
    run(out_first, 4)
    run(out_second, 2)
    run(wanted, 1)
    run(out_second, 2)
    run(out_first, 3)
    run(wanted, 1)
    run(out_second, 2)
    run(wanted, 1)
    run(out_second, 1)
    run(wanted)
    run(score)
    run(out_first)
    lax.fori_loop(0, 2, weigh_first, 0)
    run(out_second, 1)
    weigh(1, (q1, left1, right1))

    run(out_second)
    weigh(1, (far1,))

    def hand_over(t, carry):
        cut = pl.ds(pl.multiple_of(t * half, half), half)
        grad[cut, :] = part_buf[:, :, cut].reshape(cols, half).T
        return carry

    lax.fori_loop(0, 2, hand_over, 0)

    mail.close()


def body(n_dp, n_mp, features, weight):
    rows, depth = features.shape[1], features.shape[2]
    cols = weight.shape[1]
    batch = rows * n_dp
    sub = cols // n_dp
    ring = n_mp // CORES
    far = ring // 2
    tiles = sub // 8 * (batch // LANES) * 2 // 3
    f32, bf16 = jnp.float32, jnp.bfloat16
    V = pltpu.VMEM
    scratch = [
        V((depth, cols), bf16),
        V((2, rows, depth), bf16),
        V((2, rows, cols), f32),
        V((2, n_dp, sub, LANES), f32),
        V((2, n_dp, sub * rows // LANES, LANES), f32),
        V((2, sub, batch), f32),
        V((n_mp, sub, batch), bf16),
        V((n_dp, sub, batch), bf16),
        V((cols, cols), bf16),
        V((cols, cols), bf16),
        V((n_mp, sub // 8, batch // LANES, 8, LANES), f32),
        V((n_dp, sub // 8, batch // LANES, 8, LANES), f32),
        V((WHOLE, tiles + 1, 8, LANES), f32),
        V((WHOLE, tiles + 1, 8, LANES), f32),
        V((HALF, tiles // 2 + 1, 8, LANES), f32),
        V((HALF, tiles // 2 + 1, 8, LANES), f32),
        V((ring, sub // 8, batch // LANES, 8, LANES), f32),
        V((2, n_dp, sub, batch), bf16),
        V((2, n_dp, rows, cols), bf16),
        V((n_dp, sub, cols), f32),
        V((SIDE, 8, 128), f32),
        V((SIDE, 8, 128), f32),
        V((ring, 8, 128), f32),
        V((CORES, 8, 128), f32),
        pltpu.SemaphoreType.DMA((MSGS,)),
        pltpu.SemaphoreType.DMA((MSGS,)),
        pltpu.SemaphoreType.DMA((17,)),
    ]
    grad, loss = pl.pallas_call(
        functools.partial(kernel, n_dp, n_mp),
        out_shape=(
            jax.ShapeDtypeStruct((cols, cols), f32),
            jax.ShapeDtypeStruct((1, 1), f32),
        ),
        in_specs=[pl.BlockSpec(memory_space=pl.ANY)] * 2,
        out_specs=(pl.BlockSpec(memory_space=V), pl.BlockSpec(memory_space=V)),
        scratch_shapes=scratch,
        compiler_params=pltpu.CompilerParams(
            collective_id=0, has_side_effects=True, vmem_limit_bytes=60 * 2**20
        ),
    )(features, weight)
    return (grad, loss.reshape(()))


def solution(mesh):
    placed = (P(None, "dp", None), P(None, "mp"))
    return jax.shard_map(
        functools.partial(body, mesh.shape["dp"], mesh.shape["mp"]),
        mesh=mesh,
        in_specs=placed,
        out_specs=(P("dp", "mp"), P()),
        check_vma=False,
    )
```

```python
import functools

import jax
import jax.numpy as jnp
from jax import lax
from jax.experimental import pallas as pl
from jax.experimental.pallas import tpu as pltpu
from jax.sharding import PartitionSpec as P

epsilon = 1e-05
off_weight = 0.0051
SIDE = 4
CORES = 2
LANES = 128
MSGS = 190
WHOLE, HALF = 12, 20
MESH = pl.DeviceIdType.MESH
OFFSETS = sorted(
    ((a, b) for a in range(SIDE) for b in range(SIDE) if a or b),
    key=lambda o: -min(o[0], SIDE - o[0]) - min(o[1], SIDE - o[1]),
)


class Mail:
    def __init__(self, send_sem, recv_sem):
        self.send_sem, self.recv_sem, self.sent = send_sem, recv_sem, []

    def push(self, src, dst, device):
        index = len(self.sent)
        copy = pltpu.make_async_remote_copy(
            src_ref=src,
            dst_ref=dst,
            send_sem=self.send_sem.at[index],
            recv_sem=self.recv_sem.at[index],
            device_id=device,
            device_id_type=MESH,
        )
        copy.start()
        self.sent.append(copy)
        return copy

    def close(self):
        for copy in self.sent:
            copy.wait_send()


def kernel(
    n_dp,
    n_mp,
    features,
    weight,
    grad,
    loss,
    w_buf,
    f_buf,
    acc,
    turned,
    arrived,
    cent,
    t0,
    t1,
    g_buf,
    gt_buf,
    p0,
    p1,
    whole_out,
    whole_in,
    half_out,
    half_in,
    sib,
    og,
    fk,
    loss_x,
    loss_y,
    loss_z,
    loss_c,
    send_sem,
    recv_sem,
    load_sem,
):
    rows = f_buf.shape[1]
    depth, cols = w_buf.shape
    batch = rows * n_dp
    sub = cols // n_dp
    ring = n_mp // CORES
    far = ring // 2
    scale = 1.0 / batch

    i = lax.axis_index("dp")
    j = lax.axis_index("mp")
    y, x = i // SIDE, i % SIDE
    z, c = j // CORES, j % CORES
    q1 = x * (1 - c) + y * c
    q2 = y * (1 - c) + x * c
    s1 = 1 * (1 - c) + SIDE * c
    s2 = SIDE * (1 - c) + 1 * c

    def index_of(a, b):
        return a * s1 + b * s2

    def slot_of(a, b):
        return a * SIDE + b

    def ring1(q):
        return (index_of(q, q2), j)

    def ring2(q):
        return (index_of(q1, q), j)

    def zdev(q):
        return (i, q * CORES + c)

    right1, left1, far1 = (q1 + 1) % SIDE, (q1 + SIDE - 1) % SIDE, (q1 + 2) % SIDE
    right2, left2, far2 = (q2 + 1) % SIDE, (q2 + SIDE - 1) % SIDE, (q2 + 2) % SIDE
    up, down = (z + 1) % ring, (z + ring - 1) % ring
    sibling = (i, z * CORES + 1 - c)
    mail = Mail(send_sem, recv_sem)
    low, high = pl.ds(0, sub // 2), pl.ds(sub // 2, sub // 2)

    parts = 8
    step = depth // parts

    def loads(k):
        cut = pl.ds(pl.multiple_of(k * step, step), step)
        return (
            pltpu.make_async_copy(weight.at[cut, :], w_buf.at[cut, :], load_sem.at[k]),
            pltpu.make_async_copy(
                features.at[:, :, cut], f_buf.at[:, :, cut], load_sem.at[parts + k]
            ),
        )

    for k in range(parts):
        for load in loads(k):
            load.start()

    barrier = pltpu.get_barrier_semaphore()
    for d in range(1, n_dp):
        pl.semaphore_signal(barrier, inc=1, device_id=((i + d) % n_dp, j), device_id_type=MESH)
    for d in range(1, ring):
        pl.semaphore_signal(barrier, inc=1, device_id=zdev((z + d) % ring), device_id_type=MESH)
    pl.semaphore_signal(barrier, inc=1, device_id=sibling, device_id_type=MESH)

    acc[...] = jnp.zeros_like(acc)

    def project(k, carry):
        for load in loads(k):
            load.wait()
        cut = pl.ds(pl.multiple_of(k * step, step), step)
        left = f_buf[:, :, cut].reshape(2 * rows, step)
        got = jnp.dot(left, w_buf[cut, :], preferred_element_type=jnp.float32)
        acc[...] += got.reshape(2, rows, cols)
        return carry

    lax.fori_loop(0, parts, project, 0)
    spare = LANES - rows
    keep = sub * rows // LANES
    tail = sub - keep
    place = lax.broadcasted_iota(jnp.int32, (spare, cols), 1) % sub // tail
    for v in range(2):
        fill = jnp.zeros((spare, cols), jnp.float32)
        for n in range(rows // spare):
            moved = pltpu.roll(acc[v, n * spare : (n + 1) * spare, :], cols - keep + n * tail, 1)
            fill = jnp.where(place == n, moved, fill)
        turned[v] = jnp.concatenate([acc[v], fill], axis=0).T.reshape(n_dp, sub, LANES)

    pl.semaphore_wait(barrier, n_dp - 1 + ring - 1 + 1)

    def run(chain, steps=99):
        for _ in range(steps):
            if next(chain, 0) == 0:
                return

    quarters = cols // LANES

    def quarter(q):
        return pl.ds(pl.multiple_of((q % quarters) * LANES, LANES), LANES)

    def feature_cut(a):
        return pl.ds(pl.multiple_of(a * cols + (z % quarters) * LANES, LANES), LANES)

    def feature_chain():
        own = pltpu.make_async_copy(
            features.at[c, :, feature_cut(i)], fk.at[c, i, :, quarter(z)], load_sem.at[2 * parts]
        )
        own.start()
        copies = []
        for n, (dx, dy) in enumerate(OFFSETS):
            other = (y + dy) % SIDE * SIDE + (x + dx) % SIDE
            copies.append(
                mail.push(
                    features.at[c, :, feature_cut(other)], fk.at[c, i, :, quarter(z)], (other, j)
                )
            )
        yield
        own.wait()
        for copy in copies:
            copy.wait_recv()
        halves = (pl.ds(0, n_dp // 2), pl.ds(n_dp // 2, n_dp // 2))

        def send(n, q, device):
            part = fk.at[c, halves[n], :, quarter(q)]
            return mail.push(part, part, device)

        def to_side(q):
            part = fk.at[c, :, :, quarter(q)]
            return mail.push(part, part, sibling)

        ups = [send(0, z, zdev(up)), send(1, z, zdev(up))]
        downs = [send(1, z, zdev(down)), send(0, z, zdev(down))]
        side = [to_side(z)]
        yield
        ups[0].wait_recv()
        ups.append(send(0, z + ring - 1, zdev(up)))
        downs[0].wait_recv()
        downs.append(send(1, z + 1, zdev(down)))
        yield
        ups[1].wait_recv()
        side.append(to_side(z + ring - 1))
        downs[1].wait_recv()
        side.append(to_side(z + 1))
        yield
        ups[2].wait_recv()
        downs[2].wait_recv()
        side.append(to_side(z + 2))
        yield
        for copy in side:
            copy.wait_recv()

    wanted = feature_chain()

    strip_copies = ([], [])
    for v in (0, 1):
        for dx, dy in OFFSETS:
            other = (y + dy) % SIDE * SIDE + (x + dx) % SIDE
            strip_copies[v].append(
                mail.push(turned.at[v, other, pl.ds(0, keep)], arrived.at[v, i], (other, j))
            )
        arrived[v, i] = turned[v, i, 0:keep, :]
    inv_std = [None, None]

    def normalize(v):
        for copy in strip_copies[v]:
            copy.wait_recv()
        whole = jnp.concatenate([arrived[v, a][:, 0:rows] for a in range(n_dp)], axis=1)
        parts = [
            arrived[v, a][n * tail : (n + 1) * tail, rows:LANES]
            for a in range(n_dp)
            for n in range(rows // spare)
        ]
        strip = jnp.concatenate([whole, jnp.concatenate(parts, axis=1)], axis=0)
        mean = jnp.sum(strip, axis=1, keepdims=True) * scale
        shifted = strip - mean
        variance = jnp.sum(shifted * shifted, axis=1, keepdims=True) * scale
        inv_std[v] = lax.rsqrt(variance + epsilon)
        centered = shifted * inv_std[v]
        cent[v] = centered
        return centered.astype(jnp.bfloat16)

    def gather(block, at, first_flip, direct=()):
        own = block(at(q1, q2))
        ends = {}

        def onward(n, a):
            part = block(at(a, q2))
            if n in direct:
                ends[n] = mail.push(part, part, ring2(far2))
            return (mail.push(part, part, ring2(right2)), mail.push(part, part, ring2(left2)))

        def across(n, a, pair):
            pair[0].wait_recv()
            pair[1].wait_recv()
            if n in direct:
                return
            if (n + first_flip) % 2 == 0:
                part = block(at(a, left2))
                ends[n] = mail.push(part, part, ring2(right2))
            else:
                part = block(at(a, right2))
                ends[n] = mail.push(part, part, ring2(left2))

        to_right = mail.push(own, own, ring1(right1))
        to_left = mail.push(own, own, ring1(left1))
        to_far = mail.push(own, own, ring1(far1))
        pair_own = onward(0, q1)
        yield
        to_right.wait_recv()
        pair_left = onward(1, left1)
        yield
        to_left.wait_recv()
        pair_right = onward(2, right1)
        yield
        across(0, q1, pair_own)
        yield
        to_far.wait_recv()
        pair_far = onward(3, far1)
        yield
        across(1, left1, pair_left)
        yield
        across(2, right1, pair_right)
        yield
        across(3, far1, pair_far)
        yield
        for n in (0, 1, 2):
            ends[n].wait_recv()
        yield
        ends[3].wait_recv()

    def gather_z():
        side = []

        def block(q):
            return t0.at[q * CORES + c]

        def to_side(q):
            side.append(mail.push(block(q), block(q), sibling))

        def hop(q, cut, device):
            part = block(q).at[cut]
            return mail.push(part, part, device)

        up_low, down_high = hop(z, low, zdev(up)), hop(z, high, zdev(down))
        up_high, down_low = hop(z, high, zdev(up)), hop(z, low, zdev(down))
        to_side(z)
        for t in range(1, far):
            below, above = (z + ring - t) % ring, (z + t) % ring
            yield
            up_low.wait_recv()
            up_low = hop(below, low, zdev(up))
            down_high.wait_recv()
            down_high = hop(above, high, zdev(down))
            yield
            up_high.wait_recv()
            if t < far - 1:
                up_high = hop(below, high, zdev(up))
            down_low.wait_recv()
            if t < far - 1:
                down_low = hop(above, low, zdev(down))
            to_side(below)
            to_side(above)
        yield
        up_low.wait_recv()
        down_high.wait_recv()
        to_side((z + far) % ring)
        yield
        for copy in side:
            copy.wait_recv()

    rows_of_second = gather(lambda a: t1.at[a], slot_of, 0, (0, 1, 2, 3))
    rows_of_first = gather_z()
    t0[j] = normalize(0)
    run(rows_of_first, 1)
    t1[slot_of(q1, q2)] = normalize(1)
    run(rows_of_second, 1)
    run(rows_of_first, 2)
    run(rows_of_second, 2)
    run(rows_of_first, 1)
    run(rows_of_second, 2)
    run(rows_of_first, 1)
    run(rows_of_second, 1)
    run(rows_of_first, 1)
    run(rows_of_second, 1)
    run(rows_of_first, 2)
    run(rows_of_second)
    run(rows_of_first)
    run(wanted, 1)

    tile = 256

    def correlate(t, total):
        per = tile // sub
        left = t0[pl.ds(t * per, per)].reshape(tile, batch)
        corr = lax.dot_general(
            left, t1[...].reshape(cols, batch), (((1,), (1,)), ((), ())),
            preferred_element_type=jnp.float32,
        ) * scale
        r = t * tile + lax.broadcasted_iota(jnp.int32, (tile, cols), 0)
        where_diagonal = jnp.where(r // sub == j, slot_of(q1, q2) * sub + r % sub, -1)
        on_diagonal = where_diagonal == lax.broadcasted_iota(jnp.int32, (tile, cols), 1)
        gap = corr - 1.0
        terms = jnp.where(on_diagonal, gap * gap, off_weight * corr * corr)
        g = jnp.where(on_diagonal, 2.0 * gap, 2.0 * off_weight * corr)
        g_buf[pl.ds(pl.multiple_of(t * tile, tile), tile), :] = g.astype(jnp.bfloat16)
        gt_buf[:, pl.ds(pl.multiple_of(t * tile, tile), tile)] = g.T.astype(jnp.bfloat16)
        return total + jnp.sum(terms, axis=0, keepdims=True)

    total = lax.fori_loop(0, cols // tile, correlate, jnp.zeros((1, cols), jnp.float32))

    wide = batch // 3

    def partial(into, left, right):
        def one(t, carry):
            cut = pl.ds(pl.multiple_of(t * wide, wide), wide)
            got = jnp.dot(
                left[...], right[:, :, cut].reshape(cols, wide), preferred_element_type=jnp.float32
            )
            got = (got * scale).reshape(n_dp, sub // 8, 8, wide)
            for n in range(wide // LANES):
                into[:, :, t * (wide // LANES) + n] = got[..., n * LANES : (n + 1) * LANES]
            return carry

        lax.fori_loop(0, batch // wide, one, 0)

    def partial_line(q):
        cut = pl.ds(pl.multiple_of(q * (cols // SIDE), cols // SIDE), cols // SIDE)
        got = jnp.dot(
            gt_buf[cut, :], t0[...].reshape(cols, batch), preferred_element_type=jnp.float32
        )
        got = (got * scale).reshape(SIDE, sub // 8, 8, batch)
        for n in range(batch // LANES):
            p1[pl.ds(q * SIDE, SIDE), :, n] = got[..., n * LANES : (n + 1) * LANES]

    third = batch // LANES // 3
    level = 32768.0

    def pack(value):
        groups = value.shape[0]
        largest = jnp.max(jnp.max(jnp.abs(value), axis=1, keepdims=True), axis=3, keepdims=True)
        largest = jnp.maximum(largest, 1e-30)
        whole = jnp.floor(value * ((level - 2.0) / largest) + (level + 0.5))
        one, two, three = (whole[:, n * third : (n + 1) * third] for n in range(3))
        upper = jnp.floor(two * (1.0 / 256.0))
        words = jnp.concatenate(
            [one * 256.0 + upper, three * 256.0 + (two - upper * 256.0)], axis=1
        ).reshape(groups * 2 * third, 8, LANES)
        lane = lax.broadcasted_iota(jnp.int32, (8, LANES), 1)
        steps = jnp.zeros((8, LANES), jnp.float32)
        for n in range(groups):
            steps = jnp.where(lane == n, largest[n, 0] * (1.0 / (level - 2.0)), steps)
        return jnp.concatenate([words, steps[None]], axis=0)

    def unpack(words, groups):
        tiles = words[: groups * 2 * third].reshape(groups, 2 * third, 8, LANES)
        first, second = tiles[:, :third], tiles[:, third:]
        one, three = jnp.floor(first * (1.0 / 256.0)), jnp.floor(second * (1.0 / 256.0))
        two = (first - one * 256.0) * 256.0 + (second - three * 256.0)
        steps = words[groups * 2 * third]
        step = jnp.stack([steps[:, n : n + 1] for n in range(groups)])[:, None]
        return (jnp.concatenate([one, two, three], axis=1) - level) * step

    used = {sub // 8: 0, sub // 16: 0}

    def post(value, device):
        groups = value.shape[0]
        outs, ins = (whole_out, whole_in) if groups == sub // 8 else (half_out, half_in)
        n = used[groups]
        used[groups] += 1
        outs[n] = pack(value)
        return mail.push(outs.at[n], ins.at[n], device), ins, n, groups

    def take(message):
        copy, ins, n, groups = message
        copy.wait_recv()
        return unpack(ins[n], groups)

    low_part, high_part = pl.ds(0, sub // 16), pl.ds(sub // 16, sub // 16)

    def scatter():
        f, r, l, o = far2, right2, left2, q2
        partial_line(far1)
        far_f = post(p1[slot_of(far1, f)], ring1(right1))
        far_l = post(p1[slot_of(far1, l)], ring1(left1))
        far_r = post(p1[slot_of(far1, r)], ring1(right1))
        far_o = post(p1[slot_of(far1, o)], ring1(left1))
        yield
        partial_line(right1)
        l_right = post(p1[slot_of(right1, l)], ring1(right1))
        partial_line(left1)
        f_left = post(p1[slot_of(left1, f)], ring1(left1))

        def onward(message, at, device):
            return post(p1[at] + take(message), device)

        def settle(n, one, two):
            at = slot_of(q1, n)
            p1[at] = p1[at] + take(one) + take(two)
            return at

        partial_line(q1)
        yield
        f_right = onward(far_f, slot_of(right1, f), ring1(right1))
        l_left = onward(far_l, slot_of(left1, l), ring1(left1))
        r_left = post(p1[slot_of(left1, r)], ring1(left1))
        yield
        r_right = onward(far_r, slot_of(right1, r), ring1(right1))
        o_right = post(p1[slot_of(right1, o)], ring1(right1))
        o_left = onward(far_o, slot_of(left1, o), ring1(left1))
        yield
        at = settle(f, f_right, f_left)
        opp_low = post(p1[at, low_part], ring2(right2))
        opp_high = post(p1[at, high_part], ring2(left2))
        yield
        at_left = settle(l, l_right, l_left)
        lows = [post(p1[at_left, low_part], ring2(left2))]
        yield
        at_right = settle(r, r_right, r_left)
        highs = [post(p1[at_right, high_part], ring2(right2))]
        yield
        lows.append(post(p1[at_right, low_part] + take(opp_low), ring2(right2)))
        highs.append(post(p1[at_left, high_part] + take(opp_high), ring2(left2)))
        yield
        at = settle(o, o_right, o_left)
        yield
        total_low = p1[at, low_part] + take(lows[0]) + take(lows[1])
        total_high = p1[at, high_part] + take(highs[0]) + take(highs[1])
        finish(1, jnp.concatenate([total_low, total_high], axis=0))

    def scatter_z():
        order = [(z + far) % ring]
        for t in range(far - 1, 0, -1):
            order += [(z + t) % ring, (z + ring - t) % ring]
        order.append(z)
        side = [mail.push(p0.at[q * CORES + 1 - c], sib.at[q], sibling) for q in order]

        def settle(n):
            side[n].wait_recv()
            at = order[n] * CORES + c
            p0[at] = p0[at] + sib[order[n]]

        def above(t):
            return (z + t) % ring

        def below(t):
            return (z + ring - t) % ring

        def part(q, cut):
            return p0[q * CORES + c, cut]

        def pass_on(message, cut, dest, device):
            return post(part(dest, cut) + take(message), device)

        yield
        settle(0)
        ua = post(part(above(far), low_part), zdev(up))
        db = post(part(below(far), high_part), zdev(down))
        settle(1)
        ub = post(part(above(far - 1), high_part), zdev(up))
        settle(2)
        da = post(part(below(far - 1), low_part), zdev(down))
        yield
        for n in range(3, ring):
            settle(n)
        for t in range(far - 1, 0, -1):
            yield
            ua = pass_on(ua, low_part, above(t), zdev(up))
            db = pass_on(db, high_part, below(t), zdev(down))
            if t > 1:
                yield
                ub = pass_on(ub, high_part, above(t - 1), zdev(up))
                da = pass_on(da, low_part, below(t - 1), zdev(down))
        yield
        total_high = part(z, high_part) + take(ub)
        total_low = part(z, low_part) + take(da)
        total_low = total_low + take(ua)
        total_high = total_high + take(db)
        finish(0, jnp.concatenate([total_low, total_high], axis=0))

    def finish(v, tiles):
        got = jnp.concatenate(
            [
                jnp.concatenate([tiles[g, n] for n in range(batch // LANES)], axis=1)
                for g in range(sub // 8)
            ],
            axis=0,
        )
        first = jnp.sum(got, axis=1, keepdims=True) * scale
        cross = jnp.sum(got * cent[v], axis=1, keepdims=True) * scale
        og[v, i] = (inv_std[v] * (got - first - cent[v] * cross)).astype(jnp.bfloat16)

    half = cols // 2

    def weigh_first(t, carry):
        cut = pl.ds(pl.multiple_of(t * half, half), half)
        got = jnp.dot(
            og[0].reshape(cols, batch),
            fk[0, :, :, cut].reshape(batch, half),
            preferred_element_type=jnp.float32,
        )
        grad[:, :, cut] = got.reshape(n_dp, sub, half)
        return carry

    def weigh(v, lines):
        places = [index_of(q, n) for q in lines for n in range(SIDE)]

        def one(t, carry):
            cut = pl.ds(pl.multiple_of(t * half, half), half)
            got = jnp.dot(
                jnp.concatenate([og[v, a] for a in places], axis=0),
                fk[v, :, :, cut].reshape(batch, half),
                preferred_element_type=jnp.float32,
            )
            for n, a in enumerate(places):
                grad[a, :, cut] += got[n * sub : (n + 1) * sub]
            return carry

        lax.fori_loop(0, 2, one, 0)

    def loss_chain(value):
        stages = (
            (loss_x, x, [(y * SIDE + (x + d) % SIDE, j) for d in range(1, SIDE)]),
            (loss_y, y, [(((y + d) % SIDE) * SIDE + x, j) for d in range(1, SIDE)]),
            (loss_z, z, [zdev((z + d) % ring) for d in range(1, ring)]),
            (loss_c, c, [sibling]),
        )
        for buf, at, others in stages:
            buf[at] = value
            copies = [mail.push(buf.at[at], buf.at[at], device) for device in others]
            yield
            for copy in copies:
                copy.wait_recv()
            value = buf[0]
            for n in range(1, buf.shape[0]):
                value = value + buf[n]
        loss[...] = value[0:1, 0:1] / (n_mp * cols)

    second = scatter()
    run(second, 1)
    partial(p0, g_buf, t1)
    first = scatter_z()
    run(first, 1)
    score = loss_chain(jnp.broadcast_to(jnp.sum(total, axis=1, keepdims=True), (8, 128)))
    run(second, 1)
    run(first, 1)
    run(score, 1)
    run(second, 1)
    run(first, 2)
    run(second, 1)
    run(first, 2)
    run(second, 2)
    run(first, 1)
    run(second, 1)
    run(first, 1)
    run(second, 1)
    run(score, 1)
    run(first)
    out_first = gather(lambda a: og.at[0, a], index_of, 0)
    run(out_first, 1)
    run(wanted, 1)
    run(second)
    out_second = gather(lambda a: og.at[1, a], index_of, 1)
    run(out_second, 1)
    run(score, 1)
    run(out_first, 4)
    run(out_second, 2)
    run(wanted, 1)
    run(out_second, 2)
    run(out_first, 2)
    run(wanted, 1)
    run(out_first, 1)
    run(out_second, 1)
    run(wanted, 1)
    run(out_second, 1)
    run(out_second, 1)
    run(wanted)
    run(score)
    run(out_first)
    lax.fori_loop(0, 2, weigh_first, 0)
    run(out_second, 1)
    weigh(1, (q1, left1, right1))

    run(out_second)
    weigh(1, (far1,))

    mail.close()


def body(n_dp, n_mp, features, weight):
    rows, depth = features.shape[1], features.shape[2]
    cols = weight.shape[1]
    batch = rows * n_dp
    sub = cols // n_dp
    ring = n_mp // CORES
    far = ring // 2
    tiles = sub // 8 * (batch // LANES) * 2 // 3
    f32, bf16 = jnp.float32, jnp.bfloat16
    V = pltpu.VMEM
    scratch = [
        V((depth, cols), bf16),
        V((2, rows, depth), bf16),
        V((2, rows, cols), f32),
        V((2, n_dp, sub, LANES), f32),
        V((2, n_dp, sub * rows // LANES, LANES), f32),
        V((2, sub, batch), f32),
        V((n_mp, sub, batch), bf16),
        V((n_dp, sub, batch), bf16),
        V((cols, cols), bf16),
        V((cols, cols), bf16),
        V((n_mp, sub // 8, batch // LANES, 8, LANES), f32),
        V((n_dp, sub // 8, batch // LANES, 8, LANES), f32),
        V((WHOLE, tiles + 1, 8, LANES), f32),
        V((WHOLE, tiles + 1, 8, LANES), f32),
        V((HALF, tiles // 2 + 1, 8, LANES), f32),
        V((HALF, tiles // 2 + 1, 8, LANES), f32),
        V((ring, sub // 8, batch // LANES, 8, LANES), f32),
        V((2, n_dp, sub, batch), bf16),
        V((2, n_dp, rows, cols), bf16),
        V((SIDE, 8, 128), f32),
        V((SIDE, 8, 128), f32),
        V((ring, 8, 128), f32),
        V((CORES, 8, 128), f32),
        pltpu.SemaphoreType.DMA((MSGS,)),
        pltpu.SemaphoreType.DMA((MSGS,)),
        pltpu.SemaphoreType.DMA((17,)),
    ]
    grad, loss = pl.pallas_call(
        functools.partial(kernel, n_dp, n_mp),
        out_shape=(
            jax.ShapeDtypeStruct((n_dp, sub, cols), f32),
            jax.ShapeDtypeStruct((1, 1), f32),
        ),
        in_specs=[pl.BlockSpec(memory_space=pl.ANY)] * 2,
        out_specs=(pl.BlockSpec(memory_space=V), pl.BlockSpec(memory_space=V)),
        scratch_shapes=scratch,
        compiler_params=pltpu.CompilerParams(
            collective_id=0, has_side_effects=True, vmem_limit_bytes=60 * 2**20
        ),
    )(features, weight)
    return (grad.reshape(cols, cols).T, loss.reshape(()))


def solution(mesh):
    placed = (P(None, "dp", None), P(None, "mp"))
    return jax.shard_map(
        functools.partial(body, mesh.shape["dp"], mesh.shape["mp"]),
        mesh=mesh,
        in_specs=placed,
        out_specs=(P("dp", "mp"), P()),
        check_vma=False,
    )
```

```python
import functools

import jax
import jax.numpy as jnp
from jax import lax
from jax.experimental import pallas as pl
from jax.experimental.pallas import tpu as pltpu
from jax.sharding import PartitionSpec as P

epsilon = 1e-05
off_weight = 0.0051
SIDE = 4
CORES = 2
LANES = 128
MSGS = 190
WHOLE, HALF = 12, 20
MESH = pl.DeviceIdType.MESH
OFFSETS = sorted(
    ((a, b) for a in range(SIDE) for b in range(SIDE) if a or b),
    key=lambda o: -min(o[0], SIDE - o[0]) - min(o[1], SIDE - o[1]),
)


class Mail:
    def __init__(self, send_sem, recv_sem):
        self.send_sem, self.recv_sem, self.sent = send_sem, recv_sem, []

    def push(self, src, dst, device):
        index = len(self.sent)
        copy = pltpu.make_async_remote_copy(
            src_ref=src,
            dst_ref=dst,
            send_sem=self.send_sem.at[index],
            recv_sem=self.recv_sem.at[index],
            device_id=device,
            device_id_type=MESH,
        )
        copy.start()
        self.sent.append(copy)
        return copy

    def close(self):
        for copy in self.sent:
            copy.wait_send()


def kernel(
    n_dp,
    n_mp,
    features,
    weight,
    grad,
    loss,
    w_buf,
    f_buf,
    acc,
    turned,
    arrived,
    cent,
    t0,
    t1,
    g_buf,
    gt_buf,
    p0,
    p1,
    whole_out,
    whole_in,
    half_out,
    half_in,
    sib,
    og,
    fk,
    loss_x,
    loss_y,
    loss_z,
    loss_c,
    send_sem,
    recv_sem,
    load_sem,
):
    rows = f_buf.shape[1]
    depth, cols = w_buf.shape
    batch = rows * n_dp
    sub = cols // n_dp
    ring = n_mp // CORES
    far = ring // 2
    scale = 1.0 / batch

    i = lax.axis_index("dp")
    j = lax.axis_index("mp")
    y, x = i // SIDE, i % SIDE
    z, c = j // CORES, j % CORES
    q1 = x * (1 - c) + y * c
    q2 = y * (1 - c) + x * c
    s1 = 1 * (1 - c) + SIDE * c
    s2 = SIDE * (1 - c) + 1 * c

    def index_of(a, b):
        return a * s1 + b * s2

    def slot_of(a, b):
        return a * SIDE + b

    def ring1(q):
        return (index_of(q, q2), j)

    def ring2(q):
        return (index_of(q1, q), j)

    def zdev(q):
        return (i, q * CORES + c)

    right1, left1, far1 = (q1 + 1) % SIDE, (q1 + SIDE - 1) % SIDE, (q1 + 2) % SIDE
    right2, left2, far2 = (q2 + 1) % SIDE, (q2 + SIDE - 1) % SIDE, (q2 + 2) % SIDE
    up, down = (z + 1) % ring, (z + ring - 1) % ring
    sibling = (i, z * CORES + 1 - c)
    mail = Mail(send_sem, recv_sem)
    low, high = pl.ds(0, sub // 2), pl.ds(sub // 2, sub // 2)

    parts = 8
    step = depth // parts

    def loads(k):
        cut = pl.ds(pl.multiple_of(k * step, step), step)
        return (
            pltpu.make_async_copy(weight.at[cut, :], w_buf.at[cut, :], load_sem.at[k]),
            pltpu.make_async_copy(
                features.at[:, :, cut], f_buf.at[:, :, cut], load_sem.at[parts + k]
            ),
        )

    for k in range(parts):
        for load in loads(k):
            load.start()

    barrier = pltpu.get_barrier_semaphore()
    for d in range(1, n_dp):
        pl.semaphore_signal(barrier, inc=1, device_id=((i + d) % n_dp, j), device_id_type=MESH)
    for d in range(1, ring):
        pl.semaphore_signal(barrier, inc=1, device_id=zdev((z + d) % ring), device_id_type=MESH)
    pl.semaphore_signal(barrier, inc=1, device_id=sibling, device_id_type=MESH)

    acc[...] = jnp.zeros_like(acc)

    def project(k, carry):
        for load in loads(k):
            load.wait()
        cut = pl.ds(pl.multiple_of(k * step, step), step)
        left = f_buf[:, :, cut].reshape(2 * rows, step)
        got = jnp.dot(left, w_buf[cut, :], preferred_element_type=jnp.float32)
        acc[...] += got.reshape(2, rows, cols)
        return carry

    lax.fori_loop(0, parts, project, 0)
    spare = LANES - rows
    keep = sub * rows // LANES
    tail = sub - keep
    place = lax.broadcasted_iota(jnp.int32, (spare, cols), 1) % sub // tail
    for v in range(2):
        fill = jnp.zeros((spare, cols), jnp.float32)
        for n in range(rows // spare):
            moved = pltpu.roll(acc[v, n * spare : (n + 1) * spare, :], cols - keep + n * tail, 1)
            fill = jnp.where(place == n, moved, fill)
        turned[v] = jnp.concatenate([acc[v], fill], axis=0).T.reshape(n_dp, sub, LANES)

    pl.semaphore_wait(barrier, n_dp - 1 + ring - 1 + 1)

    def run(chain, steps=99):
        for _ in range(steps):
            if next(chain, 0) == 0:
                return

    quarters = cols // LANES

    def quarter(q):
        return pl.ds(pl.multiple_of((q % quarters) * LANES, LANES), LANES)

    def feature_cut(a):
        return pl.ds(pl.multiple_of(a * cols + (z % quarters) * LANES, LANES), LANES)

    def feature_chain():
        own = pltpu.make_async_copy(
            features.at[c, :, feature_cut(i)], fk.at[c, i, :, quarter(z)], load_sem.at[2 * parts]
        )
        own.start()
        copies = []
        for n, (dx, dy) in enumerate(OFFSETS):
            other = (y + dy) % SIDE * SIDE + (x + dx) % SIDE
            copies.append(
                mail.push(
                    features.at[c, :, feature_cut(other)], fk.at[c, i, :, quarter(z)], (other, j)
                )
            )
        yield
        own.wait()
        for copy in copies:
            copy.wait_recv()
        halves = (pl.ds(0, n_dp // 2), pl.ds(n_dp // 2, n_dp // 2))

        def send(n, q, device):
            part = fk.at[c, halves[n], :, quarter(q)]
            return mail.push(part, part, device)

        def to_side(q):
            part = fk.at[c, :, :, quarter(q)]
            return mail.push(part, part, sibling)

        ups = [send(0, z, zdev(up)), send(1, z, zdev(up))]
        downs = [send(1, z, zdev(down)), send(0, z, zdev(down))]
        side = [to_side(z)]
        yield
        ups[0].wait_recv()
        ups.append(send(0, z + ring - 1, zdev(up)))
        downs[0].wait_recv()
        downs.append(send(1, z + 1, zdev(down)))
        yield
        ups[1].wait_recv()
        side.append(to_side(z + ring - 1))
        downs[1].wait_recv()
        side.append(to_side(z + 1))
        yield
        ups[2].wait_recv()
        downs[2].wait_recv()
        side.append(to_side(z + 2))
        yield
        for copy in side:
            copy.wait_recv()

    wanted = feature_chain()

    strip_copies = ([], [])
    for v in (0, 1):
        for dx, dy in OFFSETS:
            other = (y + dy) % SIDE * SIDE + (x + dx) % SIDE
            strip_copies[v].append(
                mail.push(turned.at[v, other, pl.ds(0, keep)], arrived.at[v, i], (other, j))
            )
        arrived[v, i] = turned[v, i, 0:keep, :]
    inv_std = [None, None]

    def normalize(v):
        for copy in strip_copies[v]:
            copy.wait_recv()
        whole = jnp.concatenate([arrived[v, a][:, 0:rows] for a in range(n_dp)], axis=1)
        parts = [
            arrived[v, a][n * tail : (n + 1) * tail, rows:LANES]
            for a in range(n_dp)
            for n in range(rows // spare)
        ]
        strip = jnp.concatenate([whole, jnp.concatenate(parts, axis=1)], axis=0)
        mean = jnp.sum(strip, axis=1, keepdims=True) * scale
        shifted = strip - mean
        variance = jnp.sum(shifted * shifted, axis=1, keepdims=True) * scale
        inv_std[v] = lax.rsqrt(variance + epsilon)
        centered = shifted * inv_std[v]
        cent[v] = centered
        return centered.astype(jnp.bfloat16)

    def gather(block, at, first_flip, direct=()):
        own = block(at(q1, q2))
        ends = {}

        def onward(n, a):
            part = block(at(a, q2))
            if n in direct:
                ends[n] = mail.push(part, part, ring2(far2))
            return (mail.push(part, part, ring2(right2)), mail.push(part, part, ring2(left2)))

        def across(n, a, pair):
            pair[0].wait_recv()
            pair[1].wait_recv()
            if n in direct:
                return
            if (n + first_flip) % 2 == 0:
                part = block(at(a, left2))
                ends[n] = mail.push(part, part, ring2(right2))
            else:
                part = block(at(a, right2))
                ends[n] = mail.push(part, part, ring2(left2))

        to_right = mail.push(own, own, ring1(right1))
        to_left = mail.push(own, own, ring1(left1))
        to_far = mail.push(own, own, ring1(far1))
        pair_own = onward(0, q1)
        yield
        to_right.wait_recv()
        pair_left = onward(1, left1)
        yield
        to_left.wait_recv()
        pair_right = onward(2, right1)
        yield
        across(0, q1, pair_own)
        yield
        to_far.wait_recv()
        pair_far = onward(3, far1)
        yield
        across(1, left1, pair_left)
        yield
        across(2, right1, pair_right)
        yield
        across(3, far1, pair_far)
        yield
        for n in (0, 1, 2):
            ends[n].wait_recv()
        yield
        ends[3].wait_recv()

    def gather_z():
        side = []

        def block(q):
            return t0.at[q * CORES + c]

        def to_side(q):
            side.append(mail.push(block(q), block(q), sibling))

        def hop(q, cut, device):
            part = block(q).at[cut]
            return mail.push(part, part, device)

        up_low, down_high = hop(z, low, zdev(up)), hop(z, high, zdev(down))
        up_high, down_low = hop(z, high, zdev(up)), hop(z, low, zdev(down))
        to_side(z)
        for t in range(1, far):
            below, above = (z + ring - t) % ring, (z + t) % ring
            yield
            up_low.wait_recv()
            up_low = hop(below, low, zdev(up))
            down_high.wait_recv()
            down_high = hop(above, high, zdev(down))
            yield
            up_high.wait_recv()
            if t < far - 1:
                up_high = hop(below, high, zdev(up))
            down_low.wait_recv()
            if t < far - 1:
                down_low = hop(above, low, zdev(down))
            to_side(below)
            to_side(above)
        yield
        up_low.wait_recv()
        down_high.wait_recv()
        to_side((z + far) % ring)
        yield
        for copy in side:
            copy.wait_recv()

    rows_of_second = gather(lambda a: t1.at[a], slot_of, 0, (0, 1, 2, 3))
    rows_of_first = gather_z()
    t0[j] = normalize(0)
    run(rows_of_first, 1)
    t1[slot_of(q1, q2)] = normalize(1)
    run(rows_of_second, 1)
    run(rows_of_first, 2)
    run(rows_of_second, 2)
    run(rows_of_first, 1)
    run(rows_of_second, 2)
    run(rows_of_first, 1)
    run(rows_of_second, 1)
    run(rows_of_first, 1)
    run(rows_of_second, 1)
    run(rows_of_first, 2)
    run(rows_of_second)
    run(rows_of_first)
    run(wanted, 1)

    tile = 256

    def correlate(t, total):
        per = tile // sub
        left = t0[pl.ds(t * per, per)].reshape(tile, batch)
        corr = lax.dot_general(
            left, t1[...].reshape(cols, batch), (((1,), (1,)), ((), ())),
            preferred_element_type=jnp.float32,
        ) * scale
        r = t * tile + lax.broadcasted_iota(jnp.int32, (tile, cols), 0)
        where_diagonal = jnp.where(r // sub == j, slot_of(q1, q2) * sub + r % sub, -1)
        on_diagonal = where_diagonal == lax.broadcasted_iota(jnp.int32, (tile, cols), 1)
        gap = corr - 1.0
        terms = jnp.where(on_diagonal, gap * gap, off_weight * corr * corr)
        g = jnp.where(on_diagonal, 2.0 * gap, 2.0 * off_weight * corr)
        g_buf[pl.ds(pl.multiple_of(t * tile, tile), tile), :] = g.astype(jnp.bfloat16)
        gt_buf[:, pl.ds(pl.multiple_of(t * tile, tile), tile)] = g.T.astype(jnp.bfloat16)
        return total + jnp.sum(terms, axis=0, keepdims=True)

    total = lax.fori_loop(0, cols // tile, correlate, jnp.zeros((1, cols), jnp.float32))

    wide = batch // 3

    def partial(into, left, right):
        def one(t, carry):
            cut = pl.ds(pl.multiple_of(t * wide, wide), wide)
            got = jnp.dot(
                left[...], right[:, :, cut].reshape(cols, wide), preferred_element_type=jnp.float32
            )
            got = (got * scale).reshape(n_dp, sub // 8, 8, wide)
            for n in range(wide // LANES):
                into[:, :, t * (wide // LANES) + n] = got[..., n * LANES : (n + 1) * LANES]
            return carry

        lax.fori_loop(0, batch // wide, one, 0)

    def partial_line(q):
        cut = pl.ds(pl.multiple_of(q * (cols // SIDE), cols // SIDE), cols // SIDE)
        got = jnp.dot(
            gt_buf[cut, :], t0[...].reshape(cols, batch), preferred_element_type=jnp.float32
        )
        got = (got * scale).reshape(SIDE, sub // 8, 8, batch)
        for n in range(batch // LANES):
            p1[pl.ds(q * SIDE, SIDE), :, n] = got[..., n * LANES : (n + 1) * LANES]

    third = batch // LANES // 3
    level = 32768.0

    def pack(value):
        groups = value.shape[0]
        largest = jnp.max(jnp.max(jnp.abs(value), axis=1, keepdims=True), axis=3, keepdims=True)
        largest = jnp.maximum(largest, 1e-30)
        whole = jnp.floor(value * ((level - 2.0) / largest) + (level + 0.5))
        one, two, three = (whole[:, n * third : (n + 1) * third] for n in range(3))
        upper = jnp.floor(two * (1.0 / 256.0))
        words = jnp.concatenate(
            [one * 256.0 + upper, three * 256.0 + (two - upper * 256.0)], axis=1
        ).reshape(groups * 2 * third, 8, LANES)
        lane = lax.broadcasted_iota(jnp.int32, (8, LANES), 1)
        steps = jnp.zeros((8, LANES), jnp.float32)
        for n in range(groups):
            steps = jnp.where(lane == n, largest[n, 0] * (1.0 / (level - 2.0)), steps)
        return jnp.concatenate([words, steps[None]], axis=0)

    def unpack(words, groups):
        tiles = words[: groups * 2 * third].reshape(groups, 2 * third, 8, LANES)
        first, second = tiles[:, :third], tiles[:, third:]
        one, three = jnp.floor(first * (1.0 / 256.0)), jnp.floor(second * (1.0 / 256.0))
        two = (first - one * 256.0) * 256.0 + (second - three * 256.0)
        steps = words[groups * 2 * third]
        step = jnp.stack([steps[:, n : n + 1] for n in range(groups)])[:, None]
        return (jnp.concatenate([one, two, three], axis=1) - level) * step

    used = {sub // 8: 0, sub // 16: 0}

    def post(value, device):
        groups = value.shape[0]
        outs, ins = (whole_out, whole_in) if groups == sub // 8 else (half_out, half_in)
        n = used[groups]
        used[groups] += 1
        outs[n] = pack(value)
        return mail.push(outs.at[n], ins.at[n], device), ins, n, groups

    def take(message):
        copy, ins, n, groups = message
        copy.wait_recv()
        return unpack(ins[n], groups)

    low_part, high_part = pl.ds(0, sub // 16), pl.ds(sub // 16, sub // 16)

    def scatter():
        f, r, l, o = far2, right2, left2, q2
        partial_line(far1)
        far_f = post(p1[slot_of(far1, f)], ring1(right1))
        far_l = post(p1[slot_of(far1, l)], ring1(left1))
        far_r = post(p1[slot_of(far1, r)], ring1(right1))
        far_o = post(p1[slot_of(far1, o)], ring1(left1))
        yield
        partial_line(right1)
        l_right = post(p1[slot_of(right1, l)], ring1(right1))
        partial_line(left1)
        f_left = post(p1[slot_of(left1, f)], ring1(left1))

        def onward(message, at, device):
            return post(p1[at] + take(message), device)

        def settle(n, one, two):
            at = slot_of(q1, n)
            p1[at] = p1[at] + take(one) + take(two)
            return at

        partial_line(q1)
        yield
        f_right = onward(far_f, slot_of(right1, f), ring1(right1))
        l_left = onward(far_l, slot_of(left1, l), ring1(left1))
        r_left = post(p1[slot_of(left1, r)], ring1(left1))
        yield
        r_right = onward(far_r, slot_of(right1, r), ring1(right1))
        o_right = post(p1[slot_of(right1, o)], ring1(right1))
        o_left = onward(far_o, slot_of(left1, o), ring1(left1))
        yield
        at = settle(f, f_right, f_left)
        opp_low = post(p1[at, low_part], ring2(right2))
        opp_high = post(p1[at, high_part], ring2(left2))
        yield
        at_left = settle(l, l_right, l_left)
        lows = [post(p1[at_left, low_part], ring2(left2))]
        yield
        at_right = settle(r, r_right, r_left)
        highs = [post(p1[at_right, high_part], ring2(right2))]
        yield
        lows.append(post(p1[at_right, low_part] + take(opp_low), ring2(right2)))
        highs.append(post(p1[at_left, high_part] + take(opp_high), ring2(left2)))
        yield
        at = settle(o, o_right, o_left)
        yield
        total_low = p1[at, low_part] + take(lows[0]) + take(lows[1])
        total_high = p1[at, high_part] + take(highs[0]) + take(highs[1])
        finish(1, jnp.concatenate([total_low, total_high], axis=0))

    def scatter_z():
        order = [(z + far) % ring]
        for t in range(far - 1, 0, -1):
            order += [(z + t) % ring, (z + ring - t) % ring]
        order.append(z)
        side = [mail.push(p0.at[q * CORES + 1 - c], sib.at[q], sibling) for q in order]

        def settle(n):
            side[n].wait_recv()
            at = order[n] * CORES + c
            p0[at] = p0[at] + sib[order[n]]

        def above(t):
            return (z + t) % ring

        def below(t):
            return (z + ring - t) % ring

        def part(q, cut):
            return p0[q * CORES + c, cut]

        def pass_on(message, cut, dest, device):
            return post(part(dest, cut) + take(message), device)

        yield
        settle(0)
        ua = post(part(above(far), low_part), zdev(up))
        db = post(part(below(far), high_part), zdev(down))
        settle(1)
        ub = post(part(above(far - 1), high_part), zdev(up))
        settle(2)
        da = post(part(below(far - 1), low_part), zdev(down))
        yield
        for n in range(3, ring):
            settle(n)
        for t in range(far - 1, 0, -1):
            yield
            ua = pass_on(ua, low_part, above(t), zdev(up))
            db = pass_on(db, high_part, below(t), zdev(down))
            if t > 1:
                yield
                ub = pass_on(ub, high_part, above(t - 1), zdev(up))
                da = pass_on(da, low_part, below(t - 1), zdev(down))
        yield
        total_high = part(z, high_part) + take(ub)
        total_low = part(z, low_part) + take(da)
        total_low = total_low + take(ua)
        total_high = total_high + take(db)
        finish(0, jnp.concatenate([total_low, total_high], axis=0))

    def finish(v, tiles):
        got = jnp.concatenate(
            [
                jnp.concatenate([tiles[g, n] for n in range(batch // LANES)], axis=1)
                for g in range(sub // 8)
            ],
            axis=0,
        )
        first = jnp.sum(got, axis=1, keepdims=True) * scale
        cross = jnp.sum(got * cent[v], axis=1, keepdims=True) * scale
        og[v, i] = (inv_std[v] * (got - first - cent[v] * cross)).astype(jnp.bfloat16)

    half = cols // 2

    def weigh_first(t, carry):
        cut = pl.ds(pl.multiple_of(t * half, half), half)
        got = jnp.dot(
            og[0].reshape(cols, batch),
            fk[0, :, :, cut].reshape(batch, half),
            preferred_element_type=jnp.float32,
        )
        grad[:, :, cut] = got.reshape(n_dp, sub, half)
        return carry

    def weigh(v, lines):
        places = [index_of(q, n) for q in lines for n in range(SIDE)]

        def one(t, carry):
            cut = pl.ds(pl.multiple_of(t * half, half), half)
            got = jnp.dot(
                jnp.concatenate([og[v, a] for a in places], axis=0),
                fk[v, :, :, cut].reshape(batch, half),
                preferred_element_type=jnp.float32,
            )
            for n, a in enumerate(places):
                grad[a, :, cut] += got[n * sub : (n + 1) * sub]
            return carry

        lax.fori_loop(0, 2, one, 0)

    def loss_chain(value):
        stages = (
            (loss_x, x, [(y * SIDE + (x + d) % SIDE, j) for d in range(1, SIDE)]),
            (loss_y, y, [(((y + d) % SIDE) * SIDE + x, j) for d in range(1, SIDE)]),
            (loss_z, z, [zdev((z + d) % ring) for d in range(1, ring)]),
            (loss_c, c, [sibling]),
        )
        for buf, at, others in stages:
            buf[at] = value
            copies = [mail.push(buf.at[at], buf.at[at], device) for device in others]
            yield
            for copy in copies:
                copy.wait_recv()
            value = buf[0]
            for n in range(1, buf.shape[0]):
                value = value + buf[n]
        loss[...] = value[0:1, 0:1] / (n_mp * cols)

    second = scatter()
    run(second, 1)
    partial(p0, g_buf, t1)
    first = scatter_z()
    run(first, 1)
    score = loss_chain(jnp.broadcast_to(jnp.sum(total, axis=1, keepdims=True), (8, 128)))
    run(second, 1)
    run(first, 1)
    run(score, 1)
    run(second, 1)
    run(first, 2)
    run(second, 1)
    run(first, 2)
    run(second, 1)
    run(first, 1)
    run(second, 1)
    run(first, 1)
    run(second, 1)
    run(second, 1)
    run(score, 1)
    run(first)
    out_first = gather(lambda a: og.at[0, a], index_of, 0)
    run(out_first, 1)
    run(wanted, 1)
    run(second)
    out_second = gather(lambda a: og.at[1, a], index_of, 1)
    run(out_second, 1)
    run(score, 1)
    run(out_first, 4)
    run(out_second, 2)
    run(wanted, 1)
    run(out_second, 2)
    run(out_first, 2)
    run(wanted, 1)
    run(out_first, 1)
    run(out_second, 1)
    run(wanted, 1)
    run(out_second, 1)
    run(out_second, 1)
    run(wanted)
    run(score)
    run(out_first)
    lax.fori_loop(0, 2, weigh_first, 0)
    run(out_second, 1)
    weigh(1, (q1, left1, right1))

    run(out_second)
    weigh(1, (far1,))

    mail.close()


def body(n_dp, n_mp, features, weight):
    rows, depth = features.shape[1], features.shape[2]
    cols = weight.shape[1]
    batch = rows * n_dp
    sub = cols // n_dp
    ring = n_mp // CORES
    far = ring // 2
    tiles = sub // 8 * (batch // LANES) * 2 // 3
    f32, bf16 = jnp.float32, jnp.bfloat16
    V = pltpu.VMEM
    scratch = [
        V((depth, cols), bf16),
        V((2, rows, depth), bf16),
        V((2, rows, cols), f32),
        V((2, n_dp, sub, LANES), f32),
        V((2, n_dp, sub * rows // LANES, LANES), f32),
        V((2, sub, batch), f32),
        V((n_mp, sub, batch), bf16),
        V((n_dp, sub, batch), bf16),
        V((cols, cols), bf16),
        V((cols, cols), bf16),
        V((n_mp, sub // 8, batch // LANES, 8, LANES), f32),
        V((n_dp, sub // 8, batch // LANES, 8, LANES), f32),
        V((WHOLE, tiles + 1, 8, LANES), f32),
        V((WHOLE, tiles + 1, 8, LANES), f32),
        V((HALF, tiles // 2 + 1, 8, LANES), f32),
        V((HALF, tiles // 2 + 1, 8, LANES), f32),
        V((ring, sub // 8, batch // LANES, 8, LANES), f32),
        V((2, n_dp, sub, batch), bf16),
        V((2, n_dp, rows, cols), bf16),
        V((SIDE, 8, 128), f32),
        V((SIDE, 8, 128), f32),
        V((ring, 8, 128), f32),
        V((CORES, 8, 128), f32),
        pltpu.SemaphoreType.DMA((MSGS,)),
        pltpu.SemaphoreType.DMA((MSGS,)),
        pltpu.SemaphoreType.DMA((17,)),
    ]
    grad, loss = pl.pallas_call(
        functools.partial(kernel, n_dp, n_mp),
        out_shape=(
            jax.ShapeDtypeStruct((n_dp, sub, cols), f32),
            jax.ShapeDtypeStruct((1, 1), f32),
        ),
        in_specs=[pl.BlockSpec(memory_space=pl.ANY)] * 2,
        out_specs=(pl.BlockSpec(memory_space=V), pl.BlockSpec(memory_space=V)),
        scratch_shapes=scratch,
        compiler_params=pltpu.CompilerParams(
            collective_id=0, has_side_effects=True, vmem_limit_bytes=60 * 2**20
        ),
    )(features, weight)
    return (grad.reshape(cols, cols).T, loss.reshape(()))


def solution(mesh):
    placed = (P(None, "dp", None), P(None, "mp"))
    return jax.shard_map(
        functools.partial(body, mesh.shape["dp"], mesh.shape["mp"]),
        mesh=mesh,
        in_specs=placed,
        out_specs=(P("dp", "mp"), P()),
        check_vma=False,
    )
```
